32 devices in a mesh: dp: 16 (over z, y, core), opt: 2 (over x).
Axes of the slice: x: 2, y: 2, z: 4, core: 2. Of those that a mesh axis runs over, the one named last changes fastest.
Arguments:
- tokens: bfloat16 [32768, 768], P(('dp', 'opt')), may hold values from -6 to 6
- cotangent: bfloat16 [32768, 768], P(('dp', 'opt')), may hold values from -6 to 6
- lengths: int32 [128], P(('dp', 'opt')), may hold values from 1 to 256, 16384 in all
- key_mask: int32 [32768], P(('dp', 'opt')), may hold values 0 or 1
- type_ids: int32 [32768], P(('dp', 'opt')), may hold values from 0 to 1
- weights: bfloat16 [768, 9216], P(None, 'dp')
- vectors: bfloat16 [10752], P('dp')
- master: float32 [768, 9216], P(None, ('dp', 'opt')), may hold values from -0.21875 to 0.21875
- slow_weights: float32 [768, 9216], P(None, ('dp', 'opt')), may hold values from -0.21875 to 0.21875
- left_stats: float32 [24576, 768], P(('dp', 'opt')), as said below
- right_stats: float32 [9216, 288], P(('dp', 'opt')), as said below
- left_root: float32 [24576, 768], P(('dp', 'opt')), as said below
- right_root: float32 [9216, 288], P(('dp', 'opt')), as said below
- vector_master: float32 [10752], P(('dp', 'opt'))
- vector_moment: float32 [10752], P(('dp', 'opt')), as said below
- slow_vectors: float32 [10752], P(('dp', 'opt'))
Outputs:
- layer_out: bfloat16 [32768, 768], P(('dp', 'opt'))
- input_grad: float32 [32768, 768], P(('dp', 'opt'))
- weight_grad: float32 [768, 9216], P(None, ('dp', 'opt'))
- left_new: float32 [24576, 768], P(('dp', 'opt'))
- right_new: float32 [9216, 288], P(('dp', 'opt'))
- master_new: float32 [768, 9216], P(None, ('dp', 'opt'))
- slow_new: float32 [768, 9216], P(None, ('dp', 'opt'))
- weights_new: bfloat16 [768, 9216], P(None, ('dp', 'opt'))
- vector_grad: float32 [10752], P(('dp', 'opt'))
- moment_new: float32 [10752], P(('dp', 'opt'))
- vector_master_new: float32 [10752], P(('dp', 'opt'))
- slow_vectors_new: float32 [10752], P(('dp', 'opt'))
- vectors_new: bfloat16 [10752], P(('dp', 'opt'))
The draws below stay inside these ranges and needn't reach their ends.
Inputs may be any that keep to these rules, and one draw needn't show every extreme that they name: Each block of left_stats and right_stats is symmetric positive definite. Each block of right_stats is symmetric positive definite. `left_root`: each block is symmetric. `right_root`: each block is symmetric. `vector_moment`: positive.
All inputs are finite; a program needn't handle non-finite values. No bound on the sum of `lengths` or of `key_mask` on one device may be relied on, other than what follows from the above.
Results may differ from the reference program's by a relative error of at most 0.012.
The reference program's roundings to bfloat16 on the way count: a program that leaves them out, or rounds other values in their place, can miss the bound.
Values may be sent and summed in bfloat16 or wider, within the bound.
No kernel may reach another device: no remote copies, remote signals or barrier semaphores. Data moves between devices by JAX's collectives and lax.ppermute only.
A program may use at most 256 MiB of HBM per device.

```python
import math
import jax
import jax.numpy as jnp
import numpy as np
from jax import lax

D = 768
H = 12
HD = 64
FF = 3072
SEQ_LEN = 256
SEQ_DEV = 4
NSEQ = 128
TOKENS = 32768
WCOLS = 9216
NVEC = 10752
BLOCK = 288
DEVICES = 32


def vector_law(key):
    position = jnp.arange(NVEC)
    segment_id = jnp.minimum(position // D, 10)
    is_gain = (segment_id == 2) | (segment_id == 7)
    spreads = jnp.array([0.5, 0.5, 0.15, 0.2, 0.3, 0.2, 0.2, 0.15, 0.2, 0.2, 0.2], jnp.float32)
    spread = spreads[segment_id]
    sample = jnp.clip(jax.random.normal(key, (NVEC,), jnp.float32), -4.0, 4.0)
    return jnp.where(is_gain, 1.0, 0.0) + spread * sample


def draw_vectors(key, part):
    key = jax.random.fold_in(key, 11)
    return vector_law(key).astype(jnp.bfloat16)


def draw_vector_master(key, part):
    key = jax.random.fold_in(key, 12)
    return vector_law(key).astype(jnp.float32)


def draw_slow_vectors(key, part):
    key = jax.random.fold_in(key, 13)
    return vector_law(key).astype(jnp.float32)


def draw_vector_moment(key, part):
    key = jax.random.fold_in(key, 14)
    position = jnp.arange(NVEC)
    segment_id = jnp.minimum(position // D, 10)
    factor = jnp.where((segment_id == 7) | (segment_id == 8), 1.0, 0.25)
    spread = jnp.exp(jax.random.uniform(key, (NVEC,), jnp.float32, 0.0, math.log(4.0)))
    return (spread * factor * float(TOKENS)).astype(jnp.float32)


def draw_weights(key, part):
    key = jax.random.fold_in(key, 21)
    column = jnp.arange(WCOLS)
    scale_cols = jnp.where(column < 3 * D, D ** (-0.5), jnp.where(column < 4 * D, math.sqrt(SEQ_LEN / (8.0 * D)), jnp.where(column < 4 * D + FF, D ** (-0.5), FF ** (-0.5))))
    sample = jnp.clip(jax.random.normal(key, (D, WCOLS), jnp.float32), -5.0, 5.0)
    return (sample * scale_cols[None, :]).astype(jnp.bfloat16)


def diagonal_stats(key, size, scale_level):
    row_pos = jnp.arange(DEVICES * size)[:, None] % size
    col_pos = jnp.arange(size)[None, :]
    factor = jnp.exp(jax.random.uniform(key, (DEVICES * size, size), jnp.float32, 0.0, math.log(4.0)))
    return jnp.where(row_pos == col_pos, factor * scale_level, 0.0).astype(jnp.float32)


def draw_left_stats(key, part):
    key = jax.random.fold_in(key, 31)
    return diagonal_stats(key, D, 0.09 * BLOCK * float(TOKENS))


def draw_right_stats(key, part):
    key = jax.random.fold_in(key, 32)
    return diagonal_stats(key, BLOCK, 0.09 * D * float(TOKENS))


def root_blocks(key, size):
    key_diag, key_noise = jax.random.split(key)
    scale_level = (0.3 * math.sqrt(float(TOKENS))) ** (-0.5)
    diagonal = jnp.exp(jax.random.uniform(key_diag, (DEVICES, size, size), jnp.float32, math.log(0.5), math.log(2.0)))
    sample = jax.random.normal(key_noise, (DEVICES, size, size), jnp.float32)
    symmetric = (sample + jnp.swapaxes(sample, 1, 2)) * (0.22 / math.sqrt(2.0 * size))
    row_pos = jnp.arange(size)[:, None]
    col_pos = jnp.arange(size)[None, :]
    return (jnp.where(row_pos == col_pos, diagonal, symmetric) * scale_level).reshape(DEVICES * size, size).astype(jnp.float32)


def draw_left_root(key, part):
    key = jax.random.fold_in(key, 41)
    return root_blocks(key, D)


def draw_right_root(key, part):
    key = jax.random.fold_in(key, 42)
    return root_blocks(key, BLOCK)


def set_ends(values, rng, least, top_value):
    shape = values.shape
    place = [jax.random.randint(jax.random.fold_in(rng, axis), (), 0, shape[axis]) for axis in range(len(shape))]
    values = values.at[tuple(place)].set(least)
    longest = shape.index(max(shape))
    place[longest] = (place[longest] + 1) % shape[longest]
    return values.at[tuple(place)].set(top_value)


def block_scale(key, shape, pieces, low, largest):
    factor_of = 1.0
    for dim, shards_of in pieces:
        draws = jax.random.uniform(jax.random.fold_in(jax.random.fold_in(key, 6), dim), (shards_of,), jnp.float32, low / len(pieces), largest / len(pieces))
        factor_of = factor_of * jnp.repeat(jnp.exp(draws), shape[dim] // shards_of).reshape((-1,) + (1,) * (len(shape) - 1 - dim))
    return factor_of


def split_up(count, total, reach, slope):
    portions = [(1 << 20) // math.isqrt(grade ** slope) + 1 for grade in range(2, count + 1)]
    surplus, counts = total - reach - (count - 1), [1] * (count - 1)
    while surplus > 0:
        movable = [i for i in range(count - 1) if counts[i] < reach]
        mass, budget = sum([portions[i] for i in movable]), surplus
        for i in movable:
            extra = min(reach - counts[i], max(1, budget * portions[i] // mass), surplus)
            counts[i] = counts[i] + extra
            surplus = surplus - extra
    return np.array([reach] + counts)


def ragged(stream_key, number_of, total, bound, lean):
    if number_of == 2:
        one = jax.random.randint(stream_key, (), max(1, total - bound), min(bound, total - 1) + 1)
        return jnp.stack([one, total - one])
    sizes = jnp.asarray(split_up(number_of, total, bound, lean), jnp.int32)
    twos = (number_of - 1) // 2
    giver, sink = sizes[1:1 + 2 * twos:2], sizes[2:2 + 2 * twos:2]
    margin = jnp.minimum(giver - 1, bound - sink)
    moved = jax.random.randint(jax.random.fold_in(stream_key, 1), (twos,), 0, 1 << 20) % (margin + 1)
    sizes = sizes.at[1:1 + 2 * twos:2].set(giver - moved).at[2:2 + 2 * twos:2].set(sink + moved)
    return sizes[jax.random.permutation(jax.random.fold_in(stream_key, 2), number_of)]


def noise(stream_key, extent, scale, limit, cuts=(), held_as=jnp.bfloat16):
    entries = jax.random.normal(stream_key, extent, jnp.float32) * scale
    if len(cuts) > 0:
        entries = block_scale(stream_key, extent, cuts, -0.22, 0.18) * entries
    return jnp.clip(entries, min=-limit, max=limit).astype(held_as)


def setup_inputs(seed: int = 0) -> dict:
    key_list = jax.random.split(jax.random.key(seed), 17)
    return {
        "tokens": noise(key_list[0], (TOKENS, D), 1.0, 6.0, ((0, 32),)),
        "cotangent": noise(key_list[1], (TOKENS, D), 1.0, 6.0, ((0, 32),)),
        "lengths": ragged(key_list[2], NSEQ, SEQ_DEV * DEVICES * SEQ_LEN // 2, SEQ_LEN, 2).astype(jnp.int32),
        "key_mask": set_ends((jax.random.randint(key_list[3], (TOKENS,), 0, 8) < 7).astype(jnp.int32), jax.random.fold_in(key_list[3], 1), 0, 1),
        "type_ids": set_ends(jax.random.randint(key_list[4], (TOKENS,), 0, 2), jax.random.fold_in(key_list[4], 1), 0, 1).astype(jnp.int32),
        "weights": draw_weights(jax.random.fold_in(key_list[16], 71), 0),
        "vectors": draw_vectors(jax.random.fold_in(key_list[16], 71), 0),
        "master": noise(key_list[7], (D, WCOLS), D ** -0.5, 0.21875, ((1, 32),), jnp.float32),
        "slow_weights": noise(key_list[8], (D, WCOLS), D ** -0.5, 0.21875, ((1, 32),), jnp.float32),
        "left_stats": draw_left_stats(jax.random.fold_in(key_list[16], 71), 0),
        "right_stats": draw_right_stats(jax.random.fold_in(key_list[16], 71), 0),
        "left_root": draw_left_root(jax.random.fold_in(key_list[16], 71), 0),
        "right_root": draw_right_root(jax.random.fold_in(key_list[16], 71), 0),
        "vector_master": draw_vector_master(jax.random.fold_in(key_list[16], 71), 0),
        "vector_moment": draw_vector_moment(jax.random.fold_in(key_list[16], 71), 0),
        "slow_vectors": draw_slow_vectors(jax.random.fold_in(key_list[16], 71), 0),
    }


@jax.custom_vjp
def low(v):
    return lax.optimization_barrier(v.astype(jnp.bfloat16)).astype(jnp.float32)

@jax.custom_vjp
def low_back(v):
    return v

def low_keep(v):
    return (low(v), None)

def low_pass(kept, grad):
    return (grad,)

def back_keep(v):
    return (v, None)

def back_low(kept, grad):
    return (low(grad),)
low.defvjp(low_keep, low_pass)
low_back.defvjp(back_keep, back_low)
highest = lax.Precision.HIGHEST
norm_eps = 1e-12
learning_rate = 0.03
vector_rate = 0.2
stat_decay = 0.5
slow_decay = 0.9

def layer_norm(inputs, norm_gain, norm_shift):
    centre = lax.optimization_barrier(jnp.mean(inputs, axis=-1, keepdims=True))
    offset = inputs - centre
    return offset * lax.rsqrt(lax.optimization_barrier(jnp.mean(offset * offset, axis=-1, keepdims=True)) + norm_eps) * norm_gain + norm_shift

def segment(vector_table, slot_index):
    return vector_table[slot_index * D:(slot_index + 1) * D]

def layer_forward(inputs, region, allowed, matrix, vector_table):
    seq_count = allowed.shape[0]
    seq_span = allowed.shape[1]
    row_count = inputs.shape[0]
    embedded = inputs + jnp.where(region, segment(vector_table, 1), segment(vector_table, 0))
    qkv_bias = jnp.concatenate([segment(vector_table, 4), jnp.zeros_like(segment(vector_table, 4)), segment(vector_table, 5)])
    qkv_values = low(low_back(jnp.dot(low(embedded), matrix[:, :3 * D], precision=highest) + qkv_bias))
    query_heads = qkv_values[:, :D].reshape(seq_count, seq_span, H, HD)
    key_heads = qkv_values[:, D:2 * D].reshape(seq_count, seq_span, H, HD)
    value_heads = qkv_values[:, 2 * D:].reshape(seq_count, seq_span, H, HD)
    raw_scores = jnp.einsum('sqhd,skhd->shqk', query_heads, key_heads, precision=highest) * HD ** (-0.5)
    scores = jnp.where(allowed[:, None, None, :], low_back(raw_scores), -1e+30)
    attn_probs = low(jax.nn.softmax(scores, axis=-1))
    context = jnp.einsum('shqk,skhd->sqhd', attn_probs, value_heads, precision=highest).reshape(row_count, D)
    context = low(low_back(context))
    branch = low_back(jnp.dot(context, matrix[:, 3 * D:4 * D], precision=highest) + segment(vector_table, 6))
    normed_one = layer_norm(embedded + branch, segment(vector_table, 2), segment(vector_table, 3))
    pre_active = low_back(jnp.dot(low(normed_one), matrix[:, 4 * D:4 * D + FF], precision=highest) + vector_table[10 * D:10 * D + FF])
    active = low(jax.nn.gelu(pre_active, approximate=False))
    feed_out = low_back(jnp.dot(active, matrix[:, 4 * D + FF:].T, precision=highest) + segment(vector_table, 9))
    return layer_norm(normed_one + feed_out, segment(vector_table, 7), segment(vector_table, 8))

def reference(tokens, cotangent, lengths, key_mask, type_ids, weights, vectors, master, slow_weights, left_stats, right_stats, left_root, right_root, vector_master, vector_moment, slow_vectors):
    matrix = weights.astype(jnp.float32)
    vector_table = vectors.astype(jnp.float32)
    total_seqs = lengths.shape[0]
    group_size = math.gcd(total_seqs, max(1, 4096 // SEQ_LEN))
    group_count = total_seqs // group_size
    group_rows = group_size * SEQ_LEN
    position = jnp.arange(SEQ_LEN)
    allowed_all = (position[None, :] < lengths[:, None]) & ((key_mask.reshape(total_seqs, SEQ_LEN) == 1) | (position[None, :] == 0))
    group_items = (tokens.reshape(group_count, group_rows, D), cotangent.reshape(group_count, group_rows, D), (type_ids == 1).reshape(group_count, group_rows, 1), allowed_all.reshape(group_count, group_size, SEQ_LEN))

    def one_group(running, group_item):
        inputs, upstream, region, allowed = group_item

        def forward(first_arg, second_arg, third_arg):
            return layer_forward(first_arg, region, allowed, second_arg, third_arg)
        output, pullback = jax.vjp(forward, inputs.astype(jnp.float32), matrix, vector_table)
        grad_inputs, grad_matrix, grad_table = pullback(upstream.astype(jnp.float32))
        return ((running[0] + grad_matrix, running[1] + grad_table), (output.astype(jnp.bfloat16), grad_inputs))
    zero_sums = (jnp.zeros((D, WCOLS), jnp.float32), jnp.zeros((NVEC,), jnp.float32))
    (weight_grad, vector_grad), (outputs, input_grads) = lax.scan(one_group, zero_sums, group_items)
    owned_grad = weight_grad.reshape(D, DEVICES, BLOCK).transpose(1, 0, 2)

    def refresh(block_item):
        grad_block, left_old, right_old, left_factor, right_factor = block_item
        left_next = stat_decay * left_old + (1.0 - stat_decay) * jnp.dot(grad_block, grad_block.T, precision=highest)
        right_next = stat_decay * right_old + (1.0 - stat_decay) * jnp.dot(grad_block.T, grad_block, precision=highest)
        steered = jnp.dot(jnp.dot(left_factor, grad_block, precision=highest), right_factor, precision=highest)
        return (left_next, right_next, steered)
    left_new, right_new, steered = lax.map(refresh, (owned_grad, left_stats.reshape(DEVICES, D, D), right_stats.reshape(DEVICES, BLOCK, BLOCK), left_root.reshape(DEVICES, D, D), right_root.reshape(DEVICES, BLOCK, BLOCK)))
    steered = steered.transpose(1, 0, 2).reshape(D, WCOLS)
    master_new = master - learning_rate * steered
    slow_new = slow_decay * slow_weights + (1.0 - slow_decay) * master_new
    weights_new = master_new.astype(jnp.bfloat16)
    moment_new = stat_decay * vector_moment + (1.0 - stat_decay) * vector_grad * vector_grad
    vector_master_new = vector_master - vector_rate * vector_grad / (jnp.sqrt(moment_new) + 1e-08)
    slow_vectors_new = slow_decay * slow_vectors + (1.0 - slow_decay) * vector_master_new
    vectors_new = vector_master_new.astype(jnp.bfloat16)
    return (outputs.reshape(TOKENS, D), input_grads.reshape(TOKENS, D), weight_grad, left_new.reshape(DEVICES * D, D), right_new.reshape(DEVICES * BLOCK, BLOCK), master_new, slow_new, weights_new, vector_grad, moment_new, vector_master_new, slow_vectors_new, vectors_new)
```

```python
import functools
import math

import jax
import jax.numpy as jnp
import numpy as np
from jax import lax
from jax.experimental import pallas as pl
from jax.experimental.pallas import tpu as pltpu
from jax.sharding import PartitionSpec as P

D = 768
H = 12
HD = 64
FF = 3072
WCOLS = 4 * D + 2 * FF
NVEC = 10 * D + FF

highest = lax.Precision.HIGHEST
norm_eps = 1e-12
learning_rate = 0.03
vector_rate = 0.2
stat_decay = 0.5
slow_decay = 0.9
f32 = jnp.float32
bf16 = jnp.bfloat16
AXES = ("dp", "opt")


def contract(left_side, right_side, left_dim, right_dim):
    return lax.dot_general(
        left_side, right_side, (((left_dim,), (right_dim,)), ((), ())), preferred_element_type=f32
    )


def block_index(z, y, c, x):
    return z * 8 + y * 4 + c * 2 + x


def permutation(move):
    pairs = []
    for b in range(32):
        z, y, c, x = b // 8, (b // 4) % 2, (b // 2) % 2, b % 2
        pairs.append((b, block_index(*move(z, y, c, x))))
    return pairs


Z_CYCLE = permutation(lambda z, y, c, x: ((2, 0, 3, 1)[z], y, c, x))
Z_CYCLE_BACK = permutation(lambda z, y, c, x: ((1, 3, 0, 2)[z], y, c, x))
Z_NEAR = permutation(lambda z, y, c, x: (z ^ 1, y, c, x))
Z_FAR = permutation(lambda z, y, c, x: (z ^ 2, y, c, x))
Z_MIDDLE = permutation(lambda z, y, c, x: ((0, 2, 1, 3)[z], y, c, x))
PLANE_A = permutation(lambda z, y, c, x: (z, 1 - y, c, x) if c == 0 else (z, y, c, 1 - x))
PLANE_B = permutation(lambda z, y, c, x: (z, y, c, 1 - x) if c == 0 else (z, 1 - y, c, x))
CORES = permutation(lambda z, y, c, x: (z, y, 1 - c, x))


def send(values, pairs):
    return lax.ppermute(values, AXES, pairs)


QUARTER_SLOT = np.array([[0, 1, 3, 2], [1, 0, 3, 2], [1, 3, 0, 2], [1, 3, 2, 0]])


def unit_of(flag):
    return flag[0, 0]


class Ring:
    def __init__(self):
        dp = lax.axis_index("dp")
        self.z, self.y, self.c = dp // 4, (dp // 2) % 2, dp % 2
        self.x = lax.axis_index("opt")
        slots = [self.number([int(v) for v in QUARTER_SLOT[:, q]]) for q in range(4)]
        self.place = jnp.stack([self.y, self.c, self.x, self.z] + slots).astype(jnp.int32)

    def number(self, values):
        out = values[3]
        for z in (2, 1, 0):
            out = jnp.where(self.z == z, values[z], out)
        return out

    def pick(self, table, *choices):
        return self.number([choices[k] for k in table])

    def gather_early(self, weights, vectors):
        rows, entries = weights.shape[1] // 2, vectors.shape[0] // 2
        own = lax.dynamic_slice_in_dim(weights, self.x * rows, rows, 1).T
        few = lax.dynamic_slice_in_dim(vectors, self.x * entries, entries, 0)
        few = jnp.pad(few, (0, D - entries))[None, :]
        slab = jnp.where(jnp.arange(16)[:, None] == self.z, few, 0).astype(bf16)

        def merge(old, new):
            return jnp.where(old == 0, new, old)

        got = send(jnp.concatenate([own, slab]), Z_CYCLE)
        side = send(own, PLANE_A)
        pair = jnp.stack([own, side])
        across = send(pair, PLANE_B)
        half = jnp.concatenate([pair, across])
        slot_a = [half, send(half, CORES)]
        one, slab = got[:rows], merge(slab, got[rows:])
        got = send(jnp.concatenate([self.pick((0, 1, 1, 0), own, one), slab]), Z_NEAR)
        far = send(slab, Z_FAR)
        middle = send(own, Z_MIDDLE)
        two, slab = got[:rows], merge(merge(slab, got[rows:]), far)
        block = jnp.concatenate([self.pick((0, 1, 0, 1), one, two), slab])
        pair = jnp.stack([block, send(block, PLANE_A)])
        three = send(middle, Z_NEAR)
        slot_c = self.pick((1, 0, 1, 0), one, two)
        slot_d = self.pick((1, 0, 0, 1), middle, three)
        across = send(pair, PLANE_B)
        slot_b = [pair, across, send(pair, CORES), send(across, CORES)]
        own = jnp.stack([slot_c, slot_d])
        self.late = jnp.stack([own, send(own, PLANE_A)])
        slabs = jnp.stack([v[k, rows : rows + 4, :entries] for v, k in self.eight(slot_b)])
        owned = jnp.swapaxes(self.ordered(slabs.astype(f32)), 0, 1)
        return slot_a, slot_b, owned.reshape(-1)

    @staticmethod
    def eight(slot):
        return [(slot[0], 0), (slot[0], 1), (slot[1], 0), (slot[1], 1), (slot[2], 0), (slot[2], 1), (slot[3], 0), (slot[3], 1)]

    def gather_late(self, flag):
        across = send(self.late, PLANE_B)
        swapped = send(self.late, CORES)
        across = across * unit_of(flag).astype(bf16)
        return [self.late, across, swapped, send(across, CORES)]

    def hits(self):
        return jnp.stack([block_place((self.y, self.c, self.x), who, k) for who in (0, 1) for k in range(4)])

    def ordered(self, pieces):
        hit = (jnp.arange(8)[:, None] == self.hits()[None, :]).reshape((8, 8) + (1,) * (pieces.ndim - 1))
        return jnp.sum(jnp.where(hit, pieces[None], 0.0), axis=1)

    def disordered(self, blocks):
        hit = (jnp.arange(8)[None, :] == self.hits()[:, None]).reshape((8, 8) + (1,) * (blocks.ndim - 1))
        return jnp.sum(jnp.where(hit, blocks[None], 0.0), axis=1)

    def reduction(self, keep, give):
        return Reduction(keep, give)

    def vector_reduction(self, vector_sums):
        pieces = self.disordered(jnp.swapaxes(vector_sums.reshape(4, 8, -1), 0, 1))
        kept, more = pieces[:4], pieces[4:]
        for pairs, count in ((CORES, 4), (PLANE_B, 2), (PLANE_A, 1)):
            if count < 4:
                kept, more = kept[:count], kept[count : 2 * count]
            kept = kept + unpack(send(pack(more), pairs), kept.shape[-1])
        kept = kept[0]
        for pairs in (Z_NEAR, Z_FAR):
            kept = kept + unpack(send(pack(kept), pairs), kept.shape[-1])
        return lax.dynamic_index_in_dim(kept, self.z, 0, False)

    def reduce_far(self, sum_one, sum_two):
        far = send(self.pick((1, 1, 0, 0), sum_one, sum_two).astype(bf16), Z_FAR).astype(f32)
        return sum_one + far, sum_two + far

    def reduce_tail(self, sum_zero, sum_one, sum_two, sum_three):
        rows = sum_zero.shape[0]
        done = []
        for here in (slice(0, rows // 2), slice(rows // 2, rows)):
            near = send(self.pick((1, 0, 1, 0), sum_zero[here], sum_three[here]).astype(bf16), Z_NEAR).astype(f32)
            zero, three = sum_zero[here] + near, sum_three[here] + near
            give = self.pick((0, 1, 2, 3), sum_one[here], three, zero, sum_two[here]).astype(bf16)
            last = send(give, Z_CYCLE_BACK).astype(f32)
            done.append(self.pick((0, 1, 2, 3), zero, sum_one[here], sum_two[here], three) + last)
        return jnp.concatenate(done)


class Reduction:
    def __init__(self, keep, give):
        self.keep = keep
        self.got = [send(give, CORES)]

    def have(self, here):
        total = self.keep[here].astype(f32)
        for got in self.got:
            total = total + got[here].astype(f32)
        return total

    def across(self, flag=None):
        give = self.have(slice(2, 4))
        if flag is not None:
            give = give * unit_of(flag)
        self.got.append(send(give.astype(bf16), PLANE_B))

    def side(self, flag=None):
        give = self.have(slice(1, 2))
        if flag is not None:
            give = give * unit_of(flag)
        self.got.append(send(give.astype(bf16), PLANE_A))

    def total(self):
        return self.have(0)

    def keep_after(self):
        return self.got[0]


class Plain:
    def __init__(self):
        self.place = jnp.asarray(np.array([0, 0, 0, 0, 0, 1, 2, 3]), jnp.int32)

    def gather_early(self, weights, vectors):
        turned = lax.all_gather(weights, "dp", axis=1, tiled=True).T
        blocks = turned.reshape(4, 8, -1, D)
        self.mine, self.theirs = (blocks[:, np.array(k)] for k in ([0, 4, 1, 5], [2, 3, 6, 7]))
        entries = vectors.shape[0]
        tiles = -(-entries // 2048)
        padded = jnp.pad(vectors, (0, tiles * 2048 - entries)).reshape(tiles * 16, 128)
        gathered = lax.all_gather(padded, "dp", axis=0, tiled=True)
        gathered = gathered.reshape(-1, tiles * 2048)[:, :entries].reshape(-1).astype(f32)
        slot_b = [jnp.pad(v, ((0, 0), (0, 16), (0, 0))) for v in self.halves(1)]
        return [self.mine[0], self.theirs[0]], slot_b, gathered

    def halves(self, q):
        return [self.mine[q, :2], self.mine[q, 2:], self.theirs[q, :2], self.theirs[q, 2:]]

    def gather_late(self, flag):
        return [jnp.stack(both, axis=1) for both in zip(self.halves(2), self.halves(3))]

    def reduction(self, keep, give):
        return PlainReduction(keep, give)

    def vector_reduction(self, vector_sums):
        return lax.psum_scatter(vector_sums, AXES, scatter_dimension=0, tiled=True)

    def reduce_far(self, sum_one, sum_two):
        return sum_one, sum_two

    def reduce_tail(self, sum_zero, sum_one, sum_two, sum_three):
        sums = jnp.concatenate([sum_zero, sum_one, sum_two, sum_three])
        return lax.psum_scatter(sums, AXES, scatter_dimension=0, tiled=True).astype(f32)


class PlainReduction:
    def __init__(self, keep, give):
        self.pieces = jnp.concatenate([keep, give])

    def across(self, flag=None):
        pass

    def side(self, flag=None):
        pass

    def total(self):
        order = np.argsort(np.array([0, 4, 1, 5, 2, 3, 6, 7]))
        pieces = jnp.swapaxes(self.pieces[order], 0, 1)
        return pieces.reshape(pieces.shape[0], -1, D)

    def keep_after(self):
        return self.pieces


def pack(values):
    high = lax.reduce_precision(values, 8, 7)
    both = jnp.concatenate([high, values - high], axis=-1).astype(bf16)
    gaps = [(0, 0)] * (both.ndim - 2) + [(0, 12), (0, D - both.shape[-1])]
    return jnp.pad(both, gaps)


def unpack(packed, count):
    wide = packed[..., :4, :].astype(f32)
    return wide[..., :count] + wide[..., count : 2 * count]


VMEM_LIMIT = 60 * 1024 * 1024
whole = pl.BlockSpec(memory_space=pltpu.VMEM)
scalars = pl.BlockSpec(memory_space=pltpu.SMEM)
anywhere = pl.BlockSpec(memory_space=pl.ANY)
shape = jax.ShapeDtypeStruct
CHUNK = 256
CHUNKS = FF // CHUNK
Q = 3 * D
SPAN = 256
PART = 256
flag_shape = jax.ShapeDtypeStruct((8, 128), jnp.float32)


def call(kernel, outs, out_specs, scratch, flops, moved, *args, specs, name):
    return pl.pallas_call(
        kernel,
        out_shape=outs,
        in_specs=specs,
        out_specs=out_specs,
        scratch_shapes=scratch,
        compiler_params=pltpu.CompilerParams(vmem_limit_bytes=VMEM_LIMIT),
        cost_estimate=pl.CostEstimate(flops=flops, bytes_accessed=moved, transcendentals=0),
        name=name,
    )(*args)


def block_place(place, who, k):
    y, c, x = place[0], place[1], place[2]
    core = c if who == 0 else 1 - c
    first, second = k & 1, k >> 1
    to_y = jnp.where(core == 0, y ^ first, y ^ second)
    to_x = jnp.where(core == 0, x ^ second, x ^ first)
    return to_y * 4 + core * 2 + to_x


def block_rows(place, who, k, rows):
    return pl.ds(pl.multiple_of(block_place(place, who, k) * rows, math.gcd(rows, 16)), rows)


def begin(source, target, sem):
    copy = pltpu.make_async_copy(source, target, sem)
    copy.start()
    return copy


def slot_pieces(slots):
    out = []
    for slot, refs in enumerate(slots):
        if len(refs) == 2:
            out.append([(refs[k // 4], (k % 4,)) for k in range(8)])
        else:
            more = () if len(slots) == 2 or slot < 2 else (slot - 2,)
            out.append([(refs[k // 2], (k % 2,) + more) for k in range(8)])
    return out


def ingest(place, quarter, slots, into, sems):
    rows = into.shape[0] // 8
    targets = [into.at[block_rows(place, k // 4, k % 4, rows)] for k in range(8)]
    all_pieces = slot_pieces(slots)
    for slot, pieces in enumerate(all_pieces):

        @pl.when(place[4 + quarter] == slot)
        def _():
            for k, (ref, index) in enumerate(pieces):
                pltpu.make_async_copy(ref.at[(*index, pl.ds(0, rows))], targets[k], sems.at[k]).start()

    return [
        pltpu.make_async_copy(ref.at[(*index, pl.ds(0, rows))], targets[k], sems.at[k])
        for k, (ref, index) in enumerate(all_pieces[0])
    ]


def hand_out(place, source, keep, give, part, sems):
    rows = source.shape[0] // 8
    return [
        begin(source.at[block_rows(place, who, k, rows)], target.at[k, part], sems.at[4 * who + k])
        for who, target in ((1, give), (0, keep))
        for k in range(4)
    ]


def finish(*copies):
    for copy in copies:
        if isinstance(copy, (list, tuple)):
            finish(*copy)
        else:
            copy.wait()


def rows_of(i, step):
    return pl.ds(pl.multiple_of(i * step, step), step)


def loop(count, body):
    def step(i, carry):
        body(i)
        return carry

    lax.fori_loop(0, count, step, 0)


def column(row, width):
    return jnp.broadcast_to(row, (width, row.shape[1])).T


def embed(tokens, region, table):
    is_region = column(region, 128)[:, 0:1] > 0.5
    return tokens.astype(f32) + jnp.where(is_region, table[1:2, :], table[0:1, :])


def attend_kernel(
    place, a0, a1, b0, b1, b2, b3, tokens, region, allowed, table, bias,
    turned_out, context_out, spreads, flag,
    weights, low, turned, context_turned, context, mask, sems,
):
    copies = ingest(place, 0, ((a0, a1), (b0, b1, b2, b3)), weights, sems)
    flag[...] = jnp.ones_like(flag)
    rows = tokens.shape[0]

    def prepare(i):
        here = rows_of(i, PART)
        low[here, :] = embed(tokens[here, :], region[:, here], table[...]).astype(bf16)
        mask[here, :] = column(allowed[:, here], SPAN)

    loop(rows // PART, prepare)
    finish(copies)
    step = 384

    def project(i):
        here = rows_of(i, step)
        made = contract(weights[here, :], low[...], 1, 1) + column(bias[:, here], 128)[:, 0:1]
        made = made * jnp.where(i < D // step, HD ** (-0.5), 1.0)
        turned[here, :] = made.astype(bf16)

    loop(Q // step, project)
    sent = begin(turned, turned_out, sems.at[8])

    together = 8

    def units(i):
        places = []
        for j in range(together):
            u = i * together + j
            places.append((u % H, pl.multiple_of((u % H) * HD, HD), rows_of(u // H, SPAN)))
        scores = [
            contract(turned[pl.ds(D + at, HD), cols], turned[pl.ds(at, HD), cols], 0, 0)
            for _, at, cols in places
        ]
        probs = []
        for (h, at, cols), score in zip(places, scores):
            score = jnp.minimum(score, mask[cols, :])
            peak = jnp.max(score, axis=0, keepdims=True)
            powers = jnp.exp(score - peak)
            total = jnp.sum(powers, axis=0, keepdims=True)
            probs.append((powers * (1.0 / total)).astype(bf16))
            spreads[pl.ds(h, 1), cols] = peak + jnp.log(total)
        for (h, at, cols), prob in zip(places, probs):
            context_turned[pl.ds(at, HD), cols] = contract(turned[pl.ds(2 * D + at, HD), cols], prob, 1, 0).astype(bf16)

    loop(H * (rows // SPAN) // together, units)

    def turn(i):
        here = rows_of(i, 128)
        context[here, :] = context_turned[:, here].T

    loop(rows // 128, turn)
    finish(begin(context, context_out, sems.at[9]), sent)


def attend(place, pieces, tokens, region, allowed, table, bias):
    rows = tokens.shape[0]
    return call(
        attend_kernel,
        [shape((Q, rows), bf16), shape((rows, D), bf16), shape((H, rows), f32), flag_shape],
        [anywhere, anywhere, whole, whole],
        [
            pltpu.VMEM((Q, D), bf16),
            pltpu.VMEM((rows, D), bf16),
            pltpu.VMEM((Q, rows), bf16),
            pltpu.VMEM((D, rows), bf16),
            pltpu.VMEM((rows, D), bf16),
            pltpu.VMEM((rows, SPAN), f32),
            pltpu.SemaphoreType.DMA((10,)),
        ],
        2 * rows * Q * D + 4 * rows * 256 * D,
        20 << 20,
        place, *pieces, tokens, region, allowed, table, bias,
        specs=[scalars] + [anywhere] * 6 + [whole] * 5,
        name="attend",
    )


def normalise(inputs):
    centre = jnp.mean(inputs, axis=-1, keepdims=True)
    offset = inputs - centre
    spread = lax.rsqrt(jnp.mean(offset * offset, axis=-1, keepdims=True) + norm_eps)
    return offset * spread, spread


def normalise_back(scaled, unit, spread):
    return spread * (
        scaled
        - jnp.mean(scaled, axis=-1, keepdims=True)
        - unit * jnp.mean(scaled * unit, axis=-1, keepdims=True)
    )


def gelu_both(v):
    cumulative = 0.5 * (1.0 + lax.erf(v * math.sqrt(0.5)))
    density = jnp.exp(-0.5 * v * v) * (1.0 / math.sqrt(2.0 * math.pi))
    return v * cumulative, cumulative + v * density


def weight_chunk(weights, offset, i):
    return weights[pl.ds(pl.multiple_of(offset + i * CHUNK, CHUNK), CHUNK), :]


def three_sums(count, body, sums):
    zero = jnp.zeros((8, D), f32)

    def step(i, carry):
        made = body(i)
        return tuple(
            have + jnp.sum(more.reshape(-1, 8, D), axis=0) for have, more in zip(carry, made)
        )

    made = lax.fori_loop(0, count, step, (zero, zero, zero))
    for i in range(3):
        sums[i : i + 1, :] = jnp.sum(made[i], axis=0, keepdims=True)


STEP = 512


def feed_kernel(
    place, a0, a1, b0, b1, b2, b3, c0, c1, c2, c3, tokens_in, context_in, cotangent_in, region, table, up_bias,
    layer_out_to, slope_to, unit_one_to, spread_one, normed_low_to, grad_second_to, feed_low_to, sums, keep, give, rest, flag,
    weights, pre_a, pre_b, total, tokens, context, cotangent, active, slope, unit_one, normed_low, made, sems, more,
):
    rows = tokens.shape[0]
    early = [begin(context_in, context, more.at[0]), begin(tokens_in, tokens, more.at[1])]
    slots = ((a0, a1), (b0, b1, b2, b3), (c0, c1, c2, c3), (c0, c1, c2, c3))
    batches = [ingest(place, 1, slots, weights.at[pl.ds(0, Q)], sems.at[0])]
    flag[...] = jnp.ones_like(flag)
    up, down = D, D + FF
    finish(early, batches[0])
    batches.append(ingest(place, 2, slots, weights.at[pl.ds(Q, Q)], sems.at[1]))
    batches.append(ingest(place, 3, slots, weights.at[pl.ds(2 * Q, Q)], sems.at[2]))
    late = begin(cotangent_in, cotangent, more.at[2])

    def branch(i):
        here = rows_of(i, SPAN)
        total[here, :] = contract(context[here, :], weights[0:D, :], 1, 1)

    loop(rows // SPAN, branch)

    def first(i):
        here = rows_of(i, PART)
        unit, spread = normalise(embed(tokens[here, :], region[:, here], table[...]) + (total[here, :] + table[6:7, :]))
        unit_one[here, :] = unit
        spread_one[here, :] = jnp.broadcast_to(spread, (PART, 128))
        normed_low[here, :] = (unit * table[2:3, :] + table[3:4, :]).astype(bf16)

    loop(rows // PART, first)
    sent = [begin(unit_one, unit_one_to, more.at[3]), begin(normed_low, normed_low_to, more.at[4])]
    finish(batches[1])

    def gelu(pre, i, here):
        cols = rows_of(i, CHUNK)
        return gelu_both(pre[here, :] + up_bias[:, cols])

    def keep_gelu(made, i, here):
        cols = rows_of(i, CHUNK)
        active[here, cols] = made[0].astype(bf16)
        slope[here, cols] = made[1]

    everything = slice(None)

    def middle(t):
        before = jnp.maximum(2 * t - 1, 0)
        both = gelu(pre_b, before, everything)
        pre_a[...] = contract(normed_low[...], weight_chunk(weights, up, 2 * t), 1, 1)
        keep_gelu(both, before, everything)
        both = gelu(pre_a, 2 * t, everything)
        pre_b[...] = contract(normed_low[...], weight_chunk(weights, up, 2 * t + 1), 1, 1)
        keep_gelu(both, 2 * t, everything)

    loop(CHUNKS // 2, middle)

    def final(i):
        here = rows_of(i, PART)
        keep_gelu(gelu(pre_b, CHUNKS - 1, here), CHUNKS - 1, here)

    loop(rows // PART, final)
    sent.append(begin(slope, slope_to, more.at[6]))
    finish(batches[2])

    def add_down(i):
        here = rows_of(i, SPAN)
        total[here, :] = contract(active[here, :], weights[down : down + FF, :], 1, 0)

    loop(rows // SPAN, add_down)
    finish(late)

    def last(i):
        here = rows_of(i, PART)
        normed_one = unit_one[here, :] * table[2:3, :] + table[3:4, :]
        unit, spread = normalise(normed_one + (total[here, :] + table[9:10, :]))
        context[here, :] = (unit * table[7:8, :] + table[8:9, :]).astype(bf16)
        upstream = cotangent[here, :].astype(f32)
        grad = normalise_back(upstream * table[7:8, :], unit, spread)
        total[here, :] = grad
        low = grad.astype(bf16)
        tokens[here, :] = low
        return upstream * unit, upstream, low.astype(f32)

    three_sums(rows // PART, last, sums)
    sent += [
        begin(context, layer_out_to, more.at[7]),
        begin(total, grad_second_to, more.at[8]),
        begin(tokens, feed_low_to, more.at[9]),
    ]

    def weigh(i):
        here = rows_of(i, STEP)
        made[here, :] = contract(active[:, here], tokens[...], 0, 0).astype(bf16)

    loop(FF // STEP, weigh)
    finish(
        hand_out(place, made.at[pl.ds(D, Q)], keep, give, 0, sems.at[0]),
        begin(made.at[pl.ds(0, D)], rest, more.at[5]),
        sent,
    )


def feed(place, pieces, tokens, region, context, cotangent, table, up_bias):
    rows = tokens.shape[0]
    return call(
        feed_kernel,
        [
            shape((rows, D), bf16),
            shape((rows, FF), f32),
            shape((rows, D), f32),
            shape((rows, 128), f32),
            shape((rows, D), bf16),
            shape((rows, D), f32),
            shape((rows, D), bf16),
            shape((3, D), f32),
            shape((4, 1, Q // 8, D), bf16),
            shape((4, 1, Q // 8, D), bf16),
            shape((D, D), bf16),
            flag_shape,
        ],
        [anywhere] * 3 + [whole] + [anywhere] * 3 + [whole] + [anywhere] * 3 + [whole],
        [
            pltpu.VMEM((3 * Q, D), bf16),
            pltpu.VMEM((rows, CHUNK), f32),
            pltpu.VMEM((rows, CHUNK), f32),
            pltpu.VMEM((rows, D), f32),
            pltpu.VMEM((rows, D), bf16),
            pltpu.VMEM((rows, D), bf16),
            pltpu.VMEM((rows, D), bf16),
            pltpu.VMEM((rows, FF), bf16),
            pltpu.VMEM((rows, FF), f32),
            pltpu.VMEM((rows, D), f32),
            pltpu.VMEM((rows, D), bf16),
            pltpu.VMEM((FF, D), bf16),
            pltpu.SemaphoreType.DMA((3, 8)),
            pltpu.SemaphoreType.DMA((10,)),
        ],
        2 * rows * (3 * Q + FF) * D,
        50 << 20,
        place, *pieces, tokens, context, cotangent, region, table, up_bias,
        specs=[scalars] + [anywhere] * 13 + [whole] * 3,
        name="feed",
    )


def back_kernel(
    place, a0, a1, b0, b1, b2, b3, c0, c1, c2, c3, slope_in, grad_second_in, unit_one_in, feed_low_in, spread_one, table,
    grad_pre_to, grad_first_to, branch_low_to, grad_context_to, sums, flag,
    weights, pre_a, pre_b, total, slope, grad_pre, unit_one, feed_low, branch_low, grad_context, sems, more, arrived,
):
    rows = feed_low.shape[0]
    slots = ((a0, a1), (b0, b1, b2, b3), (c0, c1, c2, c3), (c0, c1, c2, c3))
    begin_low = begin(feed_low_in, feed_low, more.at[7])
    batches = [None] * 3
    batches[2] = ingest(place, 3, slots, weights.at[pl.ds(2 * Q, Q)], sems.at[2])
    batches[1] = ingest(place, 2, slots, weights.at[pl.ds(Q, Q)], sems.at[1])
    flag[...] = jnp.ones_like(flag)
    finish(begin_low, batches[1], batches[2])
    for i in range(CHUNKS):
        begin(slope_in.at[:, pl.ds(i * CHUNK, CHUNK)], slope.at[:, pl.ds(i * CHUNK, CHUNK)], arrived.at[i])
    loads = [begin(grad_second_in, total, more.at[1])]
    batches[0] = ingest(place, 1, slots, weights.at[pl.ds(0, Q)], sems.at[0])
    loads.append(begin(unit_one_in, unit_one, more.at[2]))
    up, down = D, D + FF

    def through(pre, i, here):
        cols = rows_of(i, CHUNK)
        return (pre[here, :] * slope[here, cols]).astype(bf16)

    def slope_here(i):
        cols = rows_of(i, CHUNK)
        pltpu.make_async_copy(slope_in.at[:, cols], slope.at[:, cols], arrived.at[i]).wait()

    everything = slice(None)

    def middle(t):
        before = jnp.maximum(2 * t - 1, 0)
        slope_here(2 * t)
        slope_here(2 * t + 1)
        low = through(pre_b, before, everything)
        pre_a[...] = contract(feed_low[...], weight_chunk(weights, down, 2 * t), 1, 1)
        grad_pre[:, rows_of(before, CHUNK)] = low
        low = through(pre_a, 2 * t, everything)
        pre_b[...] = contract(feed_low[...], weight_chunk(weights, down, 2 * t + 1), 1, 1)
        grad_pre[:, rows_of(2 * t, CHUNK)] = low

    loop(CHUNKS // 2, middle)

    def final(i):
        here = rows_of(i, PART)
        grad_pre[here, rows_of(CHUNKS - 1, CHUNK)] = through(pre_b, CHUNKS - 1, here)

    loop(rows // PART, final)
    sent = [begin(grad_pre, grad_pre_to, more.at[3])]
    finish(batches[0], loads)

    def add_up(i):
        here = rows_of(i, SPAN)
        total[here, :] += contract(grad_pre[here, :], weights[up : up + FF, :], 1, 0)

    loop(rows // SPAN, add_up)

    def last(i):
        here = rows_of(i, PART)
        upstream = total[here, :]
        unit = unit_one[here, :]
        grad = normalise_back(upstream * table[2:3, :], unit, spread_one[here, 0:1])
        total[here, :] = grad
        low = grad.astype(bf16)
        branch_low[here, :] = low
        return upstream * unit, upstream, low.astype(f32)

    three_sums(rows // PART, last, sums)
    sent += [begin(total, grad_first_to, more.at[4]), begin(branch_low, branch_low_to, more.at[5])]

    def through_out(i):
        here = rows_of(i, SPAN)
        grad_context[:, here] = contract(branch_low[here, :], weights[0:D, :], 1, 0).T.astype(bf16)

    loop(rows // SPAN, through_out)
    finish(begin(grad_context, grad_context_to, more.at[6]), sent)


def back(place, pieces, slope, grad_second, unit_one, feed_low, spread_one, table):
    rows = feed_low.shape[0]
    return call(
        back_kernel,
        [
            shape((rows, FF), bf16),
            shape((rows, D), f32),
            shape((rows, D), bf16),
            shape((D, rows), bf16),
            shape((3, D), f32),
            flag_shape,
        ],
        [anywhere] * 4 + [whole] * 2,
        [
            pltpu.VMEM((3 * Q, D), bf16),
            pltpu.VMEM((rows, CHUNK), f32),
            pltpu.VMEM((rows, CHUNK), f32),
            pltpu.VMEM((rows, D), f32),
            pltpu.VMEM((rows, FF), f32),
            pltpu.VMEM((rows, FF), bf16),
            pltpu.VMEM((rows, D), f32),
            pltpu.VMEM((rows, D), bf16),
            pltpu.VMEM((rows, D), bf16),
            pltpu.VMEM((D, rows), bf16),
            pltpu.SemaphoreType.DMA((3, 8)),
            pltpu.SemaphoreType.DMA((8,)),
            pltpu.SemaphoreType.DMA((CHUNKS,)),
        ],
        2 * rows * 3 * Q * D,
        45 << 20,
        place, *pieces, slope, grad_second, unit_one, feed_low, spread_one, table,
        specs=[scalars] + [anywhere] * 14 + [whole] * 2,
        name="back",
    )


def up_grad_kernel(
    place, rest, grad_pre_in, normed_low, branch_low, context,
    keep, give, up_sums, flag,
    grad_pre, made, sems, more,
):
    count = FF // STEP
    flag[...] = jnp.ones_like(flag)
    other = begin(rest, made.at[pl.ds(D + FF, D)], sems.at[2, 0])
    for i in [*range(count // 2, count), *range(count // 2)]:
        here = pl.ds(i * STEP, STEP)
        begin(grad_pre_in.at[:, here], grad_pre.at[:, here], more.at[i])

    def weigh(i):
        here = rows_of(i, STEP)
        pltpu.make_async_copy(grad_pre_in.at[:, here], grad_pre.at[:, here], more.at[i]).wait()
        made[pl.ds(pl.multiple_of(D + i * STEP, 256), STEP), :] = contract(grad_pre[:, here], normed_low[...], 0, 0).astype(bf16)
        up_sums[:, here] = jnp.sum(grad_pre[:, here].astype(f32), 0, keepdims=True)

    loop(count // 2, lambda i: weigh(count // 2 + i))
    finish(other)
    copies = hand_out(place, made.at[pl.ds(Q, Q)], keep, give, 1, sems.at[1])
    loop(count // 2, weigh)

    def weigh_out(i):
        here = rows_of(i, 384)
        made[here, :] = contract(branch_low[:, here], context[...], 0, 0).astype(bf16)

    loop(2, weigh_out)
    finish(copies, hand_out(place, made.at[pl.ds(0, Q)], keep, give, 0, sems.at[0]))


def up_grad(place, rest, grad_pre, normed_low, branch_low, context):
    rows = grad_pre.shape[0]
    return call(
        up_grad_kernel,
        [shape((4, 2, Q // 8, D), bf16)] * 2 + [shape((1, FF), f32), flag_shape],
        [anywhere] * 2 + [whole] * 2,
        [
            pltpu.VMEM((rows, FF), bf16),
            pltpu.VMEM((2 * Q, D), bf16),
            pltpu.SemaphoreType.DMA((3, 8)),
            pltpu.SemaphoreType.DMA((FF // STEP,)),
        ],
        2 * rows * (FF + D) * D,
        20 << 20,
        place, rest, grad_pre, normed_low, branch_low, context,
        specs=[scalars, anywhere, anywhere] + [whole] * 3,
        name="up_grad",
    )


def attend_back_kernel(
    place, turned, grad_context, spreads, allowed, tokens, region, table, after,
    mixed_to, keep, give, bias_sums, flag,
    low, mixed, made, mask, sems,
):
    rows = turned.shape[1]
    flag[...] = jnp.ones_like(flag)

    def prepare(i):
        here = rows_of(i, PART)
        low[here, :] = embed(tokens[here, :], region[:, here], table[...]).astype(bf16)
        mask[here, :] = column(allowed[:, here], SPAN)

    loop(rows // PART, prepare)

    together = 6

    def units(i):
        places = []
        for j in range(together):
            u = i * together + j
            places.append((u % H, pl.multiple_of((u % H) * HD, HD), rows_of(u // H, SPAN)))
        query = [turned[pl.ds(at, HD), cols] for _, at, cols in places]
        key = [turned[pl.ds(D + at, HD), cols] for _, at, cols in places]
        grad = [grad_context[pl.ds(at, HD), cols] for _, at, cols in places]
        scores = [contract(k, q, 0, 0) for k, q in zip(key, query)]
        grad_probs = [
            contract(turned[pl.ds(2 * D + at, HD), cols], g, 0, 0) for (_, at, cols), g in zip(places, grad)
        ]
        made = []
        for (h, at, cols), score, grad_prob in zip(places, scores, grad_probs):
            probs = jnp.exp(jnp.minimum(score, mask[cols, :]) - spreads[pl.ds(h, 1), cols])
            inner = jnp.sum(probs * grad_prob, axis=0, keepdims=True)
            made.append(((probs * (grad_prob - inner)).astype(bf16), probs.astype(bf16)))
        for (h, at, cols), q, k, g, (grad_score, prob) in zip(places, query, key, grad, made):
            mixed[pl.ds(at, HD), cols] = (contract(k, grad_score, 1, 0) * HD ** (-0.5)).astype(bf16)
            mixed[pl.ds(D + at, HD), cols] = contract(q, grad_score, 1, 1).astype(bf16)
            mixed[pl.ds(2 * D + at, HD), cols] = contract(g, prob, 1, 1).astype(bf16)

    loop(H * (rows // SPAN) // together, units)
    sent = begin(mixed, mixed_to, sems.at[8])
    ones = jnp.ones((rows, 128), bf16)

    def weigh(i):
        here = rows_of(i, 768)
        made[here, :] = contract(mixed[here, :], low[...], 1, 0).astype(bf16)
        bias_sums[:, here] = contract(mixed[here, :], ones, 1, 0).T[0:8, :]

    loop(3, weigh)
    finish(hand_out(place, made, keep, give, 0, sems), sent)


def attend_back(place, turned, grad_context, spreads, allowed, tokens, region, table, after):
    rows = turned.shape[1]
    return call(
        attend_back_kernel,
        [
            shape((Q, rows), bf16),
            shape((4, 1, Q // 8, D), bf16),
            shape((4, 1, Q // 8, D), bf16),
            shape((8, Q), f32),
            flag_shape,
        ],
        [anywhere, anywhere, anywhere, whole, whole],
        [
            pltpu.VMEM((rows, D), bf16),
            pltpu.VMEM((Q, rows), bf16),
            pltpu.VMEM((Q, D), bf16),
            pltpu.VMEM((rows, SPAN), f32),
            pltpu.SemaphoreType.DMA((9,)),
        ],
        2 * rows * Q * D + 10 * rows * 256 * D,
        25 << 20,
        place, turned, grad_context, spreads, allowed, tokens, region, table, after,
        specs=[scalars] + [whole] * 7 + [anywhere],
        name="attend_back",
    )


def input_kernel(place, a0, a1, b0, b1, b2, b3, mixed, grad_first, region, after, input_grad_to, sums, weights, made, sems):
    finish(ingest(place, 0, ((a0, a1), (b0, b1, b2, b3)), weights, sems))
    rows = grad_first.shape[0]

    def through(i):
        here = rows_of(i, SPAN)
        made[here, :] = grad_first[here, :] + contract(mixed[:, here], weights[...], 0, 0)
        begin(made.at[here], input_grad_to.at[here], sems.at[i])

    loop(rows // SPAN, through)
    zero = jnp.zeros((8, D), f32)

    def count(i, have):
        here = rows_of(i, PART)
        is_region = column(region[:, here], 128)[:, 0:1] > 0.5
        grad = made[here, :]
        return (
            have[0] + jnp.sum(jnp.where(is_region, 0.0, grad).reshape(-1, 8, D), 0),
            have[1] + jnp.sum(jnp.where(is_region, grad, 0.0).reshape(-1, 8, D), 0),
        )

    both = lax.fori_loop(0, rows // PART, count, (zero, zero))
    for i in range(2):
        sums[i : i + 1, :] = jnp.sum(both[i], 0, keepdims=True)
    for i in range(rows // SPAN):
        here = pl.ds(i * SPAN, SPAN)
        pltpu.make_async_copy(made.at[here], input_grad_to.at[here], sems.at[i]).wait()


def input_back(place, pieces, mixed, grad_first, region, after):
    rows = grad_first.shape[0]
    return call(
        input_kernel,
        [shape((rows, D), f32), shape((2, D), f32)],
        [anywhere, whole],
        [pltpu.VMEM((Q, D), bf16), pltpu.VMEM((rows, D), f32), pltpu.SemaphoreType.DMA((8,))],
        2 * rows * Q * D,
        15 << 20,
        place, *pieces, mixed, grad_first, region, after,
        specs=[scalars] + [anywhere] * 6 + [whole] * 3 + [anywhere],
        name="input_back",
    )


def per_device(
    ring,
    tokens,
    cotangent,
    lengths,
    key_mask,
    type_ids,
    weights,
    vectors,
    master,
    slow_weights,
    left_stats,
    right_stats,
    left_root,
    right_root,
    vector_master,
    vector_moment,
    slow_vectors,
):
    row_count = tokens.shape[0]
    seq_count = lengths.shape[0]
    seq_span = row_count // seq_count
    ring = ring()
    place = ring.place
    slot_a, slot_b, vector_table = ring.gather_early(weights, vectors)
    table = vector_table[: 10 * D].reshape(10, D)
    up_bias = vector_table[10 * D :].reshape(1, FF)
    qkv_bias = jnp.concatenate([table[4:5], jnp.zeros((1, D), f32), table[5:6]], axis=1)
    region = (type_ids == 1).astype(f32)[None, :]
    position = jnp.arange(seq_span)
    allowed = (position[None, :] < lengths[:, None]) & (
        (key_mask.reshape(seq_count, seq_span) == 1) | (position[None, :] == 0)
    )
    allowed = jnp.where(allowed, 3e38, -1e30).astype(f32).reshape(1, row_count)

    early = [*slot_a, *slot_b]
    turned, context, spreads, flag = attend(place, early, tokens, region, allowed, table, qkv_bias)
    pieces = early + ring.gather_late(flag)
    (
        layer_out, slope, unit_one, spread_one, normed_low, grad_second, feed_low, second_sums, keep, give, rest, flag
    ) = feed(place, pieces, tokens, region, context, cotangent, table, up_bias)
    reduce_three = ring.reduction(keep, give)
    grad_pre, grad_first, branch_low, grad_context, first_sums, flag = back(
        place, pieces, slope, grad_second, unit_one, feed_low, spread_one, table
    )
    reduce_three.across(flag)
    keep, give, up_sums, flag = up_grad(place, rest, grad_pre, normed_low, branch_low, context)
    reduce_three.side(flag)
    reduce_both = ring.reduction(keep, give)
    reduce_both.across()
    mixed, keep, give, bias_sums, flag = attend_back(
        place, turned, grad_context, spreads, allowed, tokens, region, table, reduce_both.keep_after()
    )
    reduce_zero = ring.reduction(keep, give)
    reduce_zero.across()
    reduce_both.side(flag)
    input_grad, type_sums = input_back(place, early, mixed, grad_first, region, reduce_zero.keep_after())
    reduce_zero.side()
    vector_sums = jnp.concatenate(
        [
            type_sums.reshape(-1),
            first_sums[:2].reshape(-1),
            bias_sums[0, :D],
            bias_sums[0, 2 * D :],
            first_sums[2],
            second_sums.reshape(-1),
            up_sums.reshape(-1),
        ]
    )
    owned_vector = ring.vector_reduction(vector_sums)
    both = reduce_both.total()
    sum_one, sum_two = ring.reduce_far(both[0], both[1])
    owned_turned = ring.reduce_tail(reduce_zero.total()[0], sum_one, sum_two, reduce_three.total()[0])
    owned_grad = owned_turned.T
    left_new = stat_decay * left_stats + (1.0 - stat_decay) * jnp.dot(
        owned_grad, owned_grad.T, precision=highest
    )
    right_new = stat_decay * right_stats + (1.0 - stat_decay) * jnp.dot(
        owned_grad.T, owned_grad, precision=highest
    )
    steered = jnp.dot(
        jnp.dot(left_root, owned_grad, precision=highest), right_root, precision=highest
    )
    master_new = master - learning_rate * steered
    slow_new = slow_decay * slow_weights + (1.0 - slow_decay) * master_new
    weights_new = master_new.astype(bf16)
    moment_new = stat_decay * vector_moment + (1.0 - stat_decay) * owned_vector * owned_vector
    vector_master_new = vector_master - vector_rate * owned_vector / (jnp.sqrt(moment_new) + 1e-08)
    slow_vectors_new = slow_decay * slow_vectors + (1.0 - slow_decay) * vector_master_new
    vectors_new = vector_master_new.astype(bf16)
    return (
        layer_out,
        input_grad,
        owned_grad,
        left_new,
        right_new,
        master_new,
        slow_new,
        weights_new,
        owned_vector,
        moment_new,
        vector_master_new,
        slow_vectors_new,
        vectors_new,
    )


def solution(mesh):
    in_specs = (
        P(("dp", "opt"), None),
        P(("dp", "opt"), None),
        P(("dp", "opt")),
        P(("dp", "opt")),
        P(("dp", "opt")),
        P(None, "dp"),
        P("dp"),
        P(None, ("dp", "opt")),
        P(None, ("dp", "opt")),
        P(("dp", "opt"), None),
        P(("dp", "opt"), None),
        P(("dp", "opt"), None),
        P(("dp", "opt"), None),
        P(("dp", "opt")),
        P(("dp", "opt")),
        P(("dp", "opt")),
    )
    out_specs = (
        P(("dp", "opt"), None),
        P(("dp", "opt"), None),
        P(None, ("dp", "opt")),
        P(("dp", "opt"), None),
        P(("dp", "opt"), None),
        P(None, ("dp", "opt")),
        P(None, ("dp", "opt")),
        P(None, ("dp", "opt")),
        P(("dp", "opt")),
        P(("dp", "opt")),
        P(("dp", "opt")),
        P(("dp", "opt")),
        P(("dp", "opt")),
    )
    ring = Ring if dict(mesh.shape) == {"dp": 16, "opt": 2} else Plain
    return jax.shard_map(
        functools.partial(per_device, ring),
        mesh=mesh,
        in_specs=in_specs,
        out_specs=out_specs,
        check_vma=False,
    )
```

```python
import functools
import math

import jax
import jax.numpy as jnp
import numpy as np
from jax import lax
from jax.experimental import pallas as pl
from jax.experimental.pallas import tpu as pltpu
from jax.sharding import PartitionSpec as P

D = 768
H = 12
HD = 64
FF = 3072
WCOLS = 4 * D + 2 * FF
NVEC = 10 * D + FF

highest = lax.Precision.HIGHEST
norm_eps = 1e-12
learning_rate = 0.03
vector_rate = 0.2
stat_decay = 0.5
slow_decay = 0.9
f32 = jnp.float32
bf16 = jnp.bfloat16
AXES = ("dp", "opt")


def contract(left_side, right_side, left_dim, right_dim):
    return lax.dot_general(
        left_side, right_side, (((left_dim,), (right_dim,)), ((), ())), preferred_element_type=f32
    )


def block_index(z, y, c, x):
    return z * 8 + y * 4 + c * 2 + x


def permutation(move):
    pairs = []
    for b in range(32):
        z, y, c, x = b // 8, (b // 4) % 2, (b // 2) % 2, b % 2
        pairs.append((b, block_index(*move(z, y, c, x))))
    return pairs


Z_CYCLE = permutation(lambda z, y, c, x: ((2, 0, 3, 1)[z], y, c, x))
Z_CYCLE_BACK = permutation(lambda z, y, c, x: ((1, 3, 0, 2)[z], y, c, x))
Z_NEAR = permutation(lambda z, y, c, x: (z ^ 1, y, c, x))
Z_FAR = permutation(lambda z, y, c, x: (z ^ 2, y, c, x))
Z_MIDDLE = permutation(lambda z, y, c, x: ((0, 2, 1, 3)[z], y, c, x))
PLANE_A = permutation(lambda z, y, c, x: (z, 1 - y, c, x) if c == 0 else (z, y, c, 1 - x))
PLANE_B = permutation(lambda z, y, c, x: (z, y, c, 1 - x) if c == 0 else (z, 1 - y, c, x))
CORES = permutation(lambda z, y, c, x: (z, y, 1 - c, x))


def send(values, pairs):
    return lax.ppermute(values, AXES, pairs)


QUARTER_SLOT = np.array([[0, 1, 3, 2], [1, 0, 3, 2], [1, 3, 0, 2], [1, 3, 2, 0]])


class Ring:
    def __init__(self):
        dp = lax.axis_index("dp")
        self.z, self.y, self.c = dp // 4, (dp // 2) % 2, dp % 2
        self.x = lax.axis_index("opt")
        slots = [self.number([int(v) for v in QUARTER_SLOT[:, q]]) for q in range(4)]
        self.place = jnp.stack([self.y, self.c, self.x, self.z] + slots).astype(jnp.int32)

    def number(self, values):
        out = values[3]
        for z in (2, 1, 0):
            out = jnp.where(self.z == z, values[z], out)
        return out

    def gather_early(self, weights, vectors):
        place, rows = self.place, weights.shape[1] // 2
        own = prepare_own(place, weights.T, vectors[None, :])
        one = send(own, Z_CYCLE)
        side = send(own, PLANE_A)
        pass_on, slab, pair_a = after_one(place, own, one, side)
        two = send(pass_on, Z_NEAR)
        across_a = send(pair_a, PLANE_B)
        far = send(slab, Z_FAR)
        middle = send(own, Z_MIDDLE)
        swap_a = send(pair_a, CORES)
        block_b, slot_c = after_two(place, pass_on, one, two, far, after=[across_a, swap_a])
        side_b = send(block_b, PLANE_A)
        side_c = send(slot_c, PLANE_A)
        three = send(middle, Z_NEAR)
        swap_aa = send(across_a, CORES)
        pair_b, slot_d = after_three(place, block_b, side_b, middle, three, after=[side_c, swap_aa])
        across_b = send(pair_b, PLANE_B)
        swap_b = send(pair_b, CORES)
        side_d = send(slot_d, PLANE_A)
        self.late = after_four(slot_c, side_c, slot_d, side_d, after=[across_b, swap_b])
        swap_bb = send(across_b, CORES)
        slot_b = [pair_b, across_b, swap_b, swap_bb]
        table = read_vectors(place, slot_b, vectors.shape[0] // 2)
        return [pair_a, across_a, swap_a, swap_aa], slot_b, table.reshape(-1, D)

    def gather_late(self):
        self.across = send(self.late, PLANE_B)
        self.swapped = send(self.late, CORES)
        return [self.late]

    def gather_last(self, context):
        across = hold(self.across, context)
        return [self.late, across, self.swapped, send(across, CORES)]

    def disordered(self, blocks):
        hits = jnp.stack([block_place((self.y, self.c, self.x), who, k) for who in (0, 1) for k in range(4)])
        hit = (jnp.arange(8)[None, :] == hits[:, None]).reshape((8, 8) + (1,) * (blocks.ndim - 1))
        return jnp.sum(jnp.where(hit, blocks[None], 0.0), axis=1)

    def reduction(self, pieces, after=()):
        return Reduction(pieces, after)

    def vectors_begin(self, vector_sums):
        pieces = self.disordered(jnp.swapaxes(vector_sums.reshape(4, 8, -1), 0, 1))
        self.kept = pieces[:4]
        return self.cross_vectors(pieces[4:], CORES)

    def vectors_next(self, pairs):
        if pairs in (PLANE_B, PLANE_A):
            count = self.kept.shape[0] // 2
            more, self.kept = self.kept[count:], self.kept[:count]
            return self.cross_vectors(more, pairs)
        return self.cross_vectors(self.kept, pairs)

    def cross_vectors(self, more, pairs):
        arrived = send(pack(more), pairs)
        self.kept = self.kept + unpack(arrived, self.kept.shape[-1])
        return [arrived]

    def vectors_end(self):
        return lax.dynamic_index_in_dim(self.kept[0], self.z, 0, False)

    def reduce_far(self, rest, after=()):
        self.kept_far, give = far_sums(self.place, rest.parts(), after)
        self.far = send(give, Z_FAR)

    def reduce_near(self, zero, rest, after=()):
        self.kept_near, give = near_sums(self.place, zero.parts(), rest.parts(), after)
        self.near = send(give, Z_NEAR)

    def reduce_last(self, after=()):
        base, give = last_sums(self.place, self.kept_near, self.kept_far, self.near, self.far, after=after)
        return base, send(give, Z_CYCLE_BACK)


class Reduction:
    def __init__(self, pieces, after=()):
        self.keep_lo, self.keep_hi, give_lo, give_hi = pieces
        if after:
            give_hi = hold(give_hi, *after)
        self.got_hi = send(give_hi, CORES)
        self.got_lo = send(give_lo, CORES)
        self.more = []

    def across(self, after=()):
        self.give = [add_pieces([self.keep_hi, self.got_hi], 0, 2, after)]
        self.more.append(send(*self.give, PLANE_B))

    def side(self, after=()):
        self.give = [add_pieces(self.parts(), 1, 1, after)]
        self.more.append(send(*self.give, PLANE_A))

    def parts(self):
        return [self.keep_lo, self.got_lo, *self.more]

    def first(self):
        return [self.got_hi]

    def last(self):
        return self.more[-1:]


class Plain:
    def __init__(self):
        self.place = jnp.asarray(np.array([0, 0, 0, 0, 0, 1, 2, 3]), jnp.int32)

    def gather_early(self, weights, vectors):
        turned = lax.all_gather(weights, "dp", axis=1, tiled=True).T
        blocks = turned.reshape(4, 8, -1, D)
        self.mine, self.theirs = (blocks[:, np.array(k)] for k in ([0, 4, 1, 5], [2, 3, 6, 7]))
        entries = vectors.shape[0]
        tiles = -(-entries // 2048)
        padded = jnp.pad(vectors, (0, tiles * 2048 - entries)).reshape(tiles * 16, 128)
        gathered = lax.all_gather(padded, "dp", axis=0, tiled=True)
        gathered = gathered.reshape(-1, tiles * 2048)[:, :entries].reshape(-1, D).astype(f32)
        slots = [[jnp.pad(v, ((0, 0), (0, 16), (0, 0))) for v in self.halves(q)] for q in (0, 1)]
        return *slots, gathered

    def halves(self, q):
        return [self.mine[q, :2], self.mine[q, 2:], self.theirs[q, :2], self.theirs[q, 2:]]

    def gather_late(self):
        return []

    def gather_last(self, context):
        return [jnp.stack(both, axis=1) for both in zip(self.halves(2), self.halves(3))]

    def reduction(self, pieces, after=()):
        return PlainReduction(pieces)

    def vectors_begin(self, vector_sums):
        self.vector_sums = vector_sums.reshape(-1)
        return []

    def vectors_next(self, pairs):
        return []

    def vectors_end(self):
        return lax.psum_scatter(self.vector_sums, AXES, scatter_dimension=0, tiled=True)

    def reduce_far(self, rest, after=()):
        self.rest = rest

    def reduce_near(self, zero, rest, after=()):
        self.zero = zero

    def reduce_last(self, after=()):
        sums = jnp.concatenate([self.zero.whole(), self.rest.whole()])
        owned = lax.psum_scatter(sums, AXES, scatter_dimension=0, tiled=True)
        return owned.astype(f32), jnp.zeros_like(owned)


class PlainReduction:
    def __init__(self, pieces):
        self.pieces = jnp.concatenate(pieces)
        self.give = []

    def across(self, after=()):
        pass

    def side(self, after=()):
        pass

    def first(self):
        return []

    def last(self):
        return []

    def whole(self):
        order = np.argsort(np.array([0, 4, 1, 5, 2, 3, 6, 7]))
        return jnp.swapaxes(self.pieces[order], 0, 1).reshape(-1, D)


def pack(values):
    high = lax.reduce_precision(values, 8, 7)
    both = jnp.concatenate([high, values - high], axis=-1).astype(bf16)
    gaps = [(0, 0)] * (both.ndim - 2) + [(0, 12), (0, D - both.shape[-1])]
    return jnp.pad(both, gaps)


def unpack(packed, count):
    wide = packed[..., :4, :].astype(f32)
    return wide[..., :count] + wide[..., count : 2 * count]


VMEM_LIMIT = 60 * 1024 * 1024
whole = pl.BlockSpec(memory_space=pltpu.VMEM)
scalars = pl.BlockSpec(memory_space=pltpu.SMEM)
anywhere = pl.BlockSpec(memory_space=pl.ANY)
shape = jax.ShapeDtypeStruct
CHUNK = 256
CHUNKS = FF // CHUNK
Q = 3 * D
SPAN = 256
PART = 256


def call(kernel, outs, out_specs, scratch, flops, moved, *args, specs, name, after=(), limit=VMEM_LIMIT):
    count, skip = len(specs), len(after)

    def body(*refs):
        kernel(*refs[:count], *refs[count + skip :])

    return pl.pallas_call(
        body,
        out_shape=outs,
        in_specs=[*specs, *[anywhere] * skip],
        out_specs=out_specs,
        scratch_shapes=scratch,
        compiler_params=pltpu.CompilerParams(vmem_limit_bytes=limit),
        cost_estimate=pl.CostEstimate(flops=flops, bytes_accessed=moved, transcendentals=0),
        name=name,
    )(*args, *after)


def block_place(place, who, k):
    y, c, x = place[0], place[1], place[2]
    core = c if who == 0 else 1 - c
    first, second = k & 1, k >> 1
    to_y = jnp.where(core == 0, y ^ first, y ^ second)
    to_x = jnp.where(core == 0, x ^ second, x ^ first)
    return to_y * 4 + core * 2 + to_x


def block_rows(place, who, k, rows):
    return pl.ds(pl.multiple_of(block_place(place, who, k) * rows, math.gcd(rows, 16)), rows)


def begin(source, target, sem):
    copy = pltpu.make_async_copy(source, target, sem)
    copy.start()
    return copy


def slot_pieces(slots):
    return [
        [(refs[k // 2], (k % 2,) + ((slot - 2,) if slot > 1 else ())) for k in range(8)]
        for slot, refs in enumerate(slots)
    ]


def ingest(place, quarter, slots, into, sems):
    rows = into.shape[0] // 8
    targets = [into.at[block_rows(place, k // 4, k % 4, rows)] for k in range(8)]
    all_pieces = slot_pieces(slots)
    for slot, pieces in enumerate(all_pieces):

        @pl.when(place[4 + quarter] == slot)
        def _():
            for k, (ref, index) in enumerate(pieces):
                pltpu.make_async_copy(ref.at[(*index, pl.ds(0, rows))], targets[k], sems.at[k]).start()

    return [
        pltpu.make_async_copy(ref.at[(*index, pl.ds(0, rows))], targets[k], sems.at[k])
        for k, (ref, index) in enumerate(all_pieces[0])
    ]


def hand_block(place, source, at, targets, part, sem):
    rows = source.shape[0] // 8
    y, c, x = place[0], place[1], place[2]
    core = (at >> 1) & 1
    flip_y, flip_x = (at >> 2) ^ y, (at & 1) ^ x
    first = jnp.where(core == 0, flip_y, flip_x)
    second = jnp.where(core == 0, flip_x, flip_y)
    which = jnp.where(core == c, 0, 2) + second
    for k, target in enumerate(targets):

        @pl.when(which == k)
        def _():
            pltpu.make_async_copy(source.at[rows_of(at, rows)], target.at[first, part], sem).start()


def hand_wait(source, targets, part, sems):
    rows = source.shape[0] // 8
    for k in range(8):
        pltpu.make_async_copy(source.at[pl.ds(0, rows)], targets[0].at[0, part], sems.at[k]).wait()


def finish(*copies):
    for copy in copies:
        if isinstance(copy, (list, tuple)):
            finish(*copy)
        else:
            copy.wait()


def rows_of(i, step):
    return pl.ds(pl.multiple_of(i * step, math.gcd(step, 256)), step)


def loop(count, body):
    def step(i, carry):
        body(i)
        return carry

    lax.fori_loop(0, count, step, 0)


def column(row, width):
    return jnp.broadcast_to(row, (width, row.shape[1])).T


def is_region(types):
    return column((types == 1).astype(f32), 128)[:, 0:1] > 0.5


def allowed_keys(lengths, keys, s):
    slot = lax.broadcasted_iota(jnp.int32, (1, SPAN), 1)
    allowed = (slot < lengths[s]) & ((keys[:, rows_of(s, SPAN)] == 1) | (slot == 0))
    return jnp.where(allowed, 3e38, -1e30)


def embed(tokens, types, table):
    return tokens.astype(f32) + jnp.where(is_region(types), table[1:2, :], table[0:1, :])


def attend_kernel(
    place, lengths, a0, a1, a2, a3, b0, b1, b2, b3, tokens, types, keys, table,
    turned_out, context_out, spreads,
    weights, low, turned, context_turned, context, mask, sems,
):
    copies = ingest(place, 0, ((a0, a1, a2, a3), (b0, b1, b2, b3)), weights, sems)
    rows = tokens.shape[0]

    def prepare(i):
        here = rows_of(i, PART)
        low[here, :] = embed(tokens[here, :], types[:, here], table[...]).astype(bf16)
        mask[here, :] = column(allowed_keys(lengths, keys, i), SPAN)

    loop(rows // PART, prepare)
    finish(copies)
    step = 384

    def project(i):
        here = rows_of(i, step)
        half = rows_of(i % 2, step)
        bias = jnp.where(i // 2 == 0, table[4:5, half], jnp.where(i // 2 == 2, table[5:6, half], 0.0))
        made = contract(weights[here, :], low[...], 1, 1) + column(bias, 128)[:, 0:1]
        made = made * jnp.where(i < D // step, HD ** (-0.5), 1.0)
        turned[here, :] = made.astype(bf16)

    loop(Q // step, project)
    sent = begin(turned, turned_out, sems.at[8])

    together = 8

    def units(i):
        places = []
        for j in range(together):
            u = i * together + j
            places.append((u % H, pl.multiple_of((u % H) * HD, HD), rows_of(u // H, SPAN)))
        scores = [
            contract(turned[pl.ds(D + at, HD), cols], turned[pl.ds(at, HD), cols], 0, 0)
            for _, at, cols in places
        ]
        probs = []
        for (h, at, cols), score in zip(places, scores):
            score = jnp.minimum(score, mask[cols, :])
            peak = jnp.max(score, axis=0, keepdims=True)
            powers = jnp.exp(score - peak)
            total = jnp.sum(powers, axis=0, keepdims=True)
            probs.append((powers * (1.0 / total)).astype(bf16))
            spreads[pl.ds(h, 1), cols] = peak + jnp.log(total)
        for (h, at, cols), prob in zip(places, probs):
            context_turned[pl.ds(at, HD), cols] = contract(turned[pl.ds(2 * D + at, HD), cols], prob, 1, 0).astype(bf16)

    loop(H * (rows // SPAN) // together, units)

    def turn(i):
        here = rows_of(i, 128)
        context[here, :] = context_turned[:, here].T

    loop(rows // 128, turn)
    finish(begin(context, context_out, sems.at[9]), sent)


def attend(place, lengths, pieces, tokens, types, keys, table, after=()):
    rows = tokens.shape[0]
    return call(
        attend_kernel,
        [shape((Q, rows), bf16), shape((rows, D), bf16), shape((H, rows), f32)],
        [anywhere, anywhere, whole],
        [
            pltpu.VMEM((Q, D), bf16),
            pltpu.VMEM((rows, D), bf16),
            pltpu.VMEM((Q, rows), bf16),
            pltpu.VMEM((D, rows), bf16),
            pltpu.VMEM((rows, D), bf16),
            pltpu.VMEM((rows, SPAN), f32),
            pltpu.SemaphoreType.DMA((10,)),
        ],
        2 * rows * Q * D + 4 * rows * 256 * D,
        20 << 20,
        place, lengths, *pieces, tokens, types, keys, table,
        specs=[scalars] * 2 + [anywhere] * 8 + [whole] * 4,
        name="attend",
        after=after,
    )


def normalise(inputs):
    centre = jnp.mean(inputs, axis=-1, keepdims=True)
    offset = inputs - centre
    spread = lax.rsqrt(jnp.mean(offset * offset, axis=-1, keepdims=True) + norm_eps)
    return offset * spread, spread


def normalise_back(scaled, unit, spread):
    return spread * (
        scaled
        - jnp.mean(scaled, axis=-1, keepdims=True)
        - unit * jnp.mean(scaled * unit, axis=-1, keepdims=True)
    )


def gelu_both(v):
    cumulative = 0.5 * (1.0 + lax.erf(v * math.sqrt(0.5)))
    density = jnp.exp(-0.5 * v * v) * (1.0 / math.sqrt(2.0 * math.pi))
    return v * cumulative, cumulative + v * density


def weight_chunk(weights, offset, i):
    return weights[pl.ds(pl.multiple_of(offset + i * CHUNK, CHUNK), CHUNK), :]


def row_sums(count, body, sums, rows):
    zero = jnp.zeros((8, D), f32)

    def step(i, carry):
        made = body(i)
        return tuple(
            have + jnp.sum(more.reshape(-1, 8, D), axis=0) for have, more in zip(carry, made)
        )

    made = lax.fori_loop(0, count, step, (zero,) * len(rows))
    for have, row in zip(made, rows):
        sums[row : row + 1, 0:D] = jnp.sum(have, axis=0, keepdims=True)


STEP = 512


def middle_kernel(
    place, a0, a1, a2, a3, b0, b1, b2, b3, c0, c1, c2, c3, tokens_in, context_in, cotangent_in, types, table,
    layer_out_to, grad_first_to, grad_context_to, sums, keep_lo, keep_hi, give_lo, give_hi,
    weights, pre_a, pre_b, total, tokens, context, cotangent, layer_out, active, slope, unit_one, spread_one, normed_low,
    grad_context, down_made, sems, more,
):
    rows = tokens.shape[0]
    slots = ((a0, a1, a2, a3), (b0, b1, b2, b3), (c0, c1, c2, c3), (c0, c1, c2, c3))
    early = [begin(context_in, context, more.at[0]), begin(tokens_in, tokens, more.at[1])]
    batches = [ingest(place, 1, slots, weights.at[pl.ds(0, Q)], sems.at[0])]
    up, down = D, D + FF
    finish(early, batches[0])
    batches.append(ingest(place, 2, slots, weights.at[pl.ds(Q, Q)], sems.at[1]))
    batches.append(ingest(place, 3, slots, weights.at[pl.ds(2 * Q, Q)], sems.at[2]))
    late = begin(cotangent_in, cotangent, more.at[2])

    def branch(i):
        here = rows_of(i, SPAN)
        total[here, :] = contract(context[here, :], weights[0:D, :], 1, 1)

    loop(rows // SPAN, branch)

    def first(i):
        here = rows_of(i, PART)
        unit, spread = normalise(embed(tokens[here, :], types[:, here], table[...]) + (total[here, :] + table[6:7, :]))
        unit_one[here, :] = unit
        spread_one[here, :] = jnp.broadcast_to(spread, (PART, 128))
        normed_low[here, :] = (unit * table[2:3, :] + table[3:4, :]).astype(bf16)

    loop(rows // PART, first)
    sent = []
    targets = (keep_lo, keep_hi, give_lo, give_hi)
    finish(batches[1])

    def gelu(pre, i, here):
        bias = table[pl.ds(10 + i // (D // CHUNK), 1), rows_of(i % (D // CHUNK), CHUNK)]
        return gelu_both(pre[here, :] + bias)

    def keep_gelu(made, i, here):
        cols = rows_of(i, CHUNK)
        active[here, cols] = made[0].astype(bf16)
        slope[here, cols] = made[1]

    everything = slice(None)

    def forward(t):
        before = jnp.maximum(2 * t - 1, 0)
        both = gelu(pre_b, before, everything)
        pre_a[...] = contract(normed_low[...], weight_chunk(weights, up, 2 * t), 1, 1)
        keep_gelu(both, before, everything)
        both = gelu(pre_a, 2 * t, everything)
        pre_b[...] = contract(normed_low[...], weight_chunk(weights, up, 2 * t + 1), 1, 1)
        keep_gelu(both, 2 * t, everything)

    loop(CHUNKS // 2, forward)

    def forward_end(i):
        here = rows_of(i, PART)
        keep_gelu(gelu(pre_b, CHUNKS - 1, here), CHUNKS - 1, here)

    loop(rows // PART, forward_end)
    finish(batches[2])

    def add_down(i):
        here = rows_of(i, SPAN)
        total[here, :] = contract(active[here, :], weights[down : down + FF, :], 1, 0)

    loop(rows // SPAN, add_down)
    finish(late)

    def second(i):
        here = rows_of(i, PART)
        normed_one = unit_one[here, :] * table[2:3, :] + table[3:4, :]
        unit, spread = normalise(normed_one + (total[here, :] + table[9:10, :]))
        layer_out[here, :] = (unit * table[7:8, :] + table[8:9, :]).astype(bf16)
        upstream = cotangent[here, :].astype(f32)
        grad = normalise_back(upstream * table[7:8, :], unit, spread)
        total[here, :] = grad
        low = grad.astype(bf16)
        tokens[here, :] = low
        return upstream * unit, upstream, low.astype(f32)

    row_sums(rows // PART, second, sums, (7, 8, 9))
    sent.append(begin(layer_out, layer_out_to, more.at[5]))

    def weigh_down(i):
        here = rows_of(i, STEP)
        down_made[here, :] = contract(active[:, here], tokens[...], 0, 0).astype(bf16)

    loop(FF // STEP, weigh_down)
    third_quarter = down_made.at[pl.ds(D, Q)]
    loop(8, lambda p: hand_block(place, third_quarter, p, targets, 2, sems.at[2, p]))

    def through(pre, i, here):
        return (pre[here, :] * slope[here, rows_of(i, CHUNK)]).astype(bf16)

    def backward(t):
        before = jnp.maximum(2 * t - 1, 0)
        low = through(pre_b, before, everything)
        pre_a[...] = contract(tokens[...], weight_chunk(weights, down, 2 * t), 1, 1)
        active[:, rows_of(before, CHUNK)] = low
        low = through(pre_a, 2 * t, everything)
        pre_b[...] = contract(tokens[...], weight_chunk(weights, down, 2 * t + 1), 1, 1)
        active[:, rows_of(2 * t, CHUNK)] = low

    loop(CHUNKS // 2, backward)

    def backward_end(i):
        here = rows_of(i, PART)
        active[here, rows_of(CHUNKS - 1, CHUNK)] = through(pre_b, CHUNKS - 1, here)

    loop(rows // PART, backward_end)

    def add_up(i):
        here = rows_of(i, SPAN)
        total[here, :] += contract(active[here, :], weights[up : up + FF, :], 1, 0)

    loop(rows // SPAN, add_up)

    def third(i):
        here = rows_of(i, PART)
        upstream = total[here, :]
        unit = unit_one[here, :]
        grad = normalise_back(upstream * table[2:3, :], unit, spread_one[here, 0:1])
        total[here, :] = grad
        low = grad.astype(bf16)
        cotangent[here, :] = low
        of_one = is_region(types[:, here])
        return upstream * unit, upstream, low.astype(f32), jnp.where(of_one, 0.0, grad), jnp.where(of_one, grad, 0.0)

    row_sums(rows // PART, third, sums, (2, 3, 6, 0, 1))
    sent.append(begin(total, grad_first_to, more.at[8]))

    def through_out(i):
        here = rows_of(i, SPAN)
        grad_context[:, here] = contract(cotangent[here, :], weights[0:D, :], 1, 0).T.astype(bf16)

    loop(rows // SPAN, through_out)
    sent.append(begin(grad_context, grad_context_to, more.at[10]))
    moved = begin(down_made.at[pl.ds(0, D)], weights.at[pl.ds(D + FF, D)], more.at[9])

    def weigh_up(i):
        here = rows_of(i, STEP)
        rows_there = pl.ds(pl.multiple_of(D + i * STEP, 256), STEP)
        weights[rows_there, :] = contract(active[:, here], normed_low[...], 0, 0).astype(bf16)
        added = jnp.sum(active[:, here].astype(f32), 0, keepdims=True)
        sums[pl.ds(10, 1), here] = added

    half = FF // STEP // 2
    loop(half, lambda i: weigh_up(half + i))
    finish(moved)
    hand_wait(third_quarter, targets, 2, sems.at[2])
    quarters = weights.at[pl.ds(0, Q)], weights.at[pl.ds(Q, Q)]
    loop(8, lambda p: hand_block(place, quarters[1], p, targets, 1, sems.at[1, p]))

    def weigh_out(i):
        here = rows_of(i, 384)
        weights[here, :] = contract(cotangent[:, here], context[...], 0, 0).astype(bf16)

    loop(2, weigh_out)
    loop(half, weigh_up)
    loop(8, lambda p: hand_block(place, quarters[0], p, targets, 0, sems.at[0, p]))
    hand_wait(quarters[1], targets, 1, sems.at[1])
    hand_wait(quarters[0], targets, 0, sems.at[0])
    finish(sent)


def middle(place, pieces, tokens, types, context, cotangent, table, after=()):
    rows = tokens.shape[0]
    tall = pltpu.VMEM((rows, D), bf16)
    return call(
        middle_kernel,
        [shape((rows, D), bf16), shape((rows, D), f32), shape((D, rows), bf16), shape((11, FF), f32)]
        + [shape((2, 3, Q // 8, D), bf16)] * 4,
        [anywhere] * 3 + [whole] + [anywhere] * 4,
        [
            pltpu.VMEM((3 * Q, D), bf16),
            pltpu.VMEM((rows, CHUNK), f32),
            pltpu.VMEM((rows, CHUNK), f32),
            pltpu.VMEM((rows, D), f32),
            tall,
            tall,
            tall,
            tall,
            pltpu.VMEM((rows, FF), bf16),
            pltpu.VMEM((rows, FF), f32),
            pltpu.VMEM((rows, D), f32),
            pltpu.VMEM((rows, 128), f32),
            tall,
            pltpu.VMEM((D, rows), bf16),
            pltpu.VMEM((FF, D), bf16),
            pltpu.SemaphoreType.DMA((3, 8)),
            pltpu.SemaphoreType.DMA((11,)),
        ],
        6 * rows * 3 * Q * D,
        60 << 20,
        place, *pieces, tokens, context, cotangent, types, table,
        specs=[scalars] + [anywhere] * 15 + [whole] * 2,
        name="middle",
        after=after,
    )


def attend_back_kernel(
    place, lengths, turned, grad_context, spreads, keys,
    mixed_to,
    mixed, mask, sems,
):
    rows = turned.shape[1]

    def prepare(i):
        here = rows_of(i, PART)
        mask[here, :] = column(allowed_keys(lengths, keys, i), SPAN)

    loop(rows // PART, prepare)

    together = 6

    def units(i):
        places = []
        for j in range(together):
            u = i * together + j
            places.append((u % H, pl.multiple_of((u % H) * HD, HD), rows_of(u // H, SPAN)))
        query = [turned[pl.ds(at, HD), cols] for _, at, cols in places]
        key = [turned[pl.ds(D + at, HD), cols] for _, at, cols in places]
        grad = [grad_context[pl.ds(at, HD), cols] for _, at, cols in places]
        scores = [contract(k, q, 0, 0) for k, q in zip(key, query)]
        grad_probs = [
            contract(turned[pl.ds(2 * D + at, HD), cols], g, 0, 0) for (_, at, cols), g in zip(places, grad)
        ]
        made = []
        for (h, at, cols), score, grad_prob in zip(places, scores, grad_probs):
            probs = jnp.exp(jnp.minimum(score, mask[cols, :]) - spreads[pl.ds(h, 1), cols])
            inner = jnp.sum(probs * grad_prob, axis=0, keepdims=True)
            made.append(((probs * (grad_prob - inner)).astype(bf16), probs.astype(bf16)))
        for (h, at, cols), q, k, g, (grad_score, prob) in zip(places, query, key, grad, made):
            mixed[pl.ds(at, HD), cols] = (contract(k, grad_score, 1, 0) * HD ** (-0.5)).astype(bf16)
            mixed[pl.ds(D + at, HD), cols] = contract(q, grad_score, 1, 1).astype(bf16)
            mixed[pl.ds(2 * D + at, HD), cols] = contract(g, prob, 1, 1).astype(bf16)

    loop(H * (rows // SPAN) // together, units)
    finish(begin(mixed, mixed_to, sems.at[0]))


def attend_back(place, lengths, turned, grad_context, spreads, keys, after=()):
    rows = turned.shape[1]
    return call(
        attend_back_kernel,
        [shape((Q, rows), bf16)],
        [anywhere],
        [
            pltpu.VMEM((Q, rows), bf16),
            pltpu.VMEM((rows, SPAN), f32),
            pltpu.SemaphoreType.DMA((1,)),
        ],
        10 * rows * 256 * D,
        25 << 20,
        place, lengths, turned, grad_context, spreads, keys,
        specs=[scalars] * 2 + [whole] * 4,
        limit=36 * 1024 * 1024,
        name="attend_back",
        after=after,
    )[0]


def mixed_grad_kernel(
    place, a0, a1, a2, a3, b0, b1, b2, b3, mixed_in, tokens, types, table, middle_sums,
    keep_lo, keep_hi, give_lo, give_hi, sums,
    low, mixed, made, weights, by_type, sems, more,
):
    step = 384
    for i in range(Q // step):
        here = pl.ds(i * step, step)
        begin(mixed_in.at[here], mixed.at[here], more.at[i])
    copies = ingest(place, 0, ((a0, a1, a2, a3), (b0, b1, b2, b3)), weights, sems)
    rows = tokens.shape[0]
    targets = (keep_lo, keep_hi, give_lo, give_hi)

    def prepare(i):
        here = rows_of(i, PART)
        low[here, :] = embed(tokens[here, :], types[:, here], table[...]).astype(bf16)

    loop(rows // PART, prepare)
    type_row = lax.broadcasted_iota(jnp.int32, (8, rows), 0)
    one_hot = (type_row == types[...]).astype(f32).astype(bf16)

    def weigh(i):
        here = rows_of(i, step)
        pltpu.make_async_copy(mixed_in.at[here], mixed.at[here], more.at[i]).wait()
        made[here, :] = contract(mixed[here, :], low[...], 1, 0).astype(bf16)
        by_type[:, here] = contract(one_hot, mixed[here, :], 1, 1)

    loop(Q // step, weigh)
    finish(copies)
    loop(8, lambda p: hand_block(place, made, p, targets, 0, sems.at[p]))
    high, rest = twice(by_type[...])
    through = contract(high, weights[...], 1, 0) + contract(rest, weights[...], 1, 0)
    sums[0:10, :] = middle_sums[0:10, 0:D]
    sums[0:2, :] = middle_sums[0:2, 0:D] + through[0:2, :]
    for row, start in ((4, 0), (5, 2 * D)):
        sums[row : row + 1, :] = by_type[0:1, start : start + D] + by_type[1:2, start : start + D]
    for i in range(FF // D):
        sums[10 + i : 11 + i, :] = middle_sums[10:11, i * D : (i + 1) * D]
    hand_wait(made, targets, 0, sems)


def mixed_grad(place, pieces, mixed, tokens, types, table, middle_sums, after=()):
    rows = tokens.shape[0]
    return call(
        mixed_grad_kernel,
        [shape((2, 1, Q // 8, D), bf16)] * 4 + [shape((NVEC // D, D), f32)],
        [anywhere] * 4 + [whole],
        [
            pltpu.VMEM((rows, D), bf16),
            pltpu.VMEM((Q, rows), bf16),
            pltpu.VMEM((Q, D), bf16),
            pltpu.VMEM((Q, D), bf16),
            pltpu.VMEM((8, Q), f32),
            pltpu.SemaphoreType.DMA((8,)),
            pltpu.SemaphoreType.DMA((6,)),
        ],
        0,
        0,
        place, *pieces, mixed, tokens, types, table, middle_sums,
        specs=[scalars] + [anywhere] * 9 + [whole] * 4,
        name="mixed_grad",
        after=after,
    )


def input_kernel(place, a0, a1, a2, a3, b0, b1, b2, b3, mixed, grad_first, input_grad_to, weights, made, sems):
    finish(ingest(place, 0, ((a0, a1, a2, a3), (b0, b1, b2, b3)), weights, sems))
    rows = grad_first.shape[0]

    def through(i):
        here = rows_of(i, SPAN)
        made[here, :] = grad_first[here, :] + contract(mixed[:, here], weights[...], 0, 0)
        begin(made.at[here], input_grad_to.at[here], sems.at[i])

    loop(rows // SPAN, through)
    for i in range(rows // SPAN):
        here = pl.ds(i * SPAN, SPAN)
        pltpu.make_async_copy(made.at[here], input_grad_to.at[here], sems.at[i]).wait()


def input_back(place, pieces, mixed, grad_first, after=()):
    rows = grad_first.shape[0]
    return call(
        input_kernel,
        [shape((rows, D), f32)],
        [anywhere],
        [pltpu.VMEM((Q, D), bf16), pltpu.VMEM((rows, D), f32), pltpu.SemaphoreType.DMA((8,))],
        2 * rows * Q * D,
        15 << 20,
        place, *pieces, mixed, grad_first,
        specs=[scalars] + [anywhere] * 8 + [whole] * 2,
        name="input_back",
        after=after,
    )[0]


SMALL_LIMIT = 16 * 1024 * 1024


def small(kernel, outs, *args, name, after=(), scratch=(), specs=None, out_specs=None):
    specs = specs or [scalars if a.dtype == jnp.int32 else whole for a in args]
    many = isinstance(outs, (list, tuple))
    return call(
        kernel, outs, out_specs or ([whole] * len(outs) if many else whole), list(scratch), 0, 0, *args,
        specs=specs, name=name, after=after, limit=SMALL_LIMIT,
    )


def hold(values, *after):
    skip = len(after)
    return pl.pallas_call(
        lambda *refs: None,
        out_shape=shape(values.shape, values.dtype),
        in_specs=[anywhere] * (1 + skip),
        out_specs=anywhere,
        input_output_aliases={0: 0},
        name="hold",
    )(values, *after)


def prepare_kernel(place, turned, few, own, sem):
    rows = own.shape[0] - 16
    copy = begin(turned.at[pl.ds(pl.multiple_of(place[2] * rows, 16), rows)], own.at[pl.ds(0, rows)], sem)
    entries = few.shape[1] // 2
    row = few[...].astype(f32)
    row = jnp.where(place[2] == 0, row[:, :entries], row[:, entries:])
    here = lax.broadcasted_iota(jnp.int32, (16, entries), 0) == place[3]
    own[rows:, :] = jnp.zeros((16, D), bf16)
    own[rows:, 0:entries] = jnp.where(here, row, 0.0).astype(bf16)
    finish(copy)


def prepare_own(place, turned, few):
    return small(
        prepare_kernel, shape((turned.shape[0] // 2 + 16, D), bf16), place, turned, few,
        name="prepare_own", scratch=[pltpu.SemaphoreType.DMA], specs=[scalars, anywhere, whole],
    )


def by_plane(place, table, choices):
    out = choices[table[3]]
    for z in (2, 1, 0):
        out = jnp.where(place[3] == z, choices[table[z]], out)
    return out


def merge(old, new):
    old, new = old.astype(f32), new.astype(f32)
    return jnp.where(old == 0.0, new, old).astype(bf16)


def after_one_kernel(place, own, one, side, pass_on, slab, pair):
    rows = own.shape[0] - 16
    pass_on[:rows, :] = by_plane(place, (0, 1, 1, 0), (own[:rows, :], one[:rows, :]))
    merged = merge(own[rows:, :], one[rows:, :])
    pass_on[rows:, :] = merged
    slab[...] = merged
    pair[0] = own[...]
    pair[1] = side[...]


def after_one(place, own, one, side):
    outs = [shape(own.shape, bf16), shape((16, D), bf16), shape((2, *own.shape), bf16)]
    return small(after_one_kernel, outs, place, own, one, side, name="after_one")


def after_two_kernel(place, pass_on, one, two, far, block, slot):
    rows = one.shape[0] - 16
    block[:rows, :] = by_plane(place, (0, 1, 0, 1), (one[:rows, :], two[:rows, :]))
    block[rows:, :] = merge(merge(pass_on[rows:, :], two[rows:, :]), far[...])
    slot[...] = by_plane(place, (1, 0, 1, 0), (one[:rows, :], two[:rows, :]))


def after_two(place, pass_on, one, two, far, after):
    outs = [shape(one.shape, bf16), shape((one.shape[0] - 16, D), bf16)]
    return small(after_two_kernel, outs, place, pass_on, one, two, far, name="after_two", after=after)


def after_three_kernel(place, block, side, middle, three, pair, slot):
    rows = slot.shape[0]
    pair[0] = block[...]
    pair[1] = side[...]
    slot[...] = by_plane(place, (1, 0, 0, 1), (middle[:rows, :], three[:rows, :]))


def after_three(place, block, side, middle, three, after):
    outs = [shape((2, *block.shape), bf16), shape((block.shape[0] - 16, D), bf16)]
    return small(after_three_kernel, outs, place, block, side, middle, three, name="after_three", after=after)


def after_four_kernel(slot_c, side_c, slot_d, side_d, late):
    late[0, 0], late[0, 1] = slot_c[...], slot_d[...]
    late[1, 0], late[1, 1] = side_c[...], side_d[...]


def after_four(slot_c, side_c, slot_d, side_d, after):
    outs = shape((2, 2, *slot_c.shape), bf16)
    return small(after_four_kernel, outs, slot_c, side_c, slot_d, side_d, name="after_four", after=after)


def read_vectors_kernel(entries, place, a, b, c, d, out, got, sems):
    rows = a.shape[1] - 16
    refs = (a, b, c, d)
    finish([begin(refs[k // 2].at[k % 2, pl.ds(rows, 16)], got.at[k], sems.at[k]) for k in range(8)])
    for k in range(8):
        at = block_place(place, k // 4, k % 4)
        slab = got[k].astype(f32)
        for z in range(4):
            out[pl.ds(z * 8 + at, 1), :] = slab[z : z + 1, 0:entries]


def read_vectors(place, pieces, entries):
    return small(
        functools.partial(read_vectors_kernel, entries), shape((32, entries), f32), place, *pieces,
        name="read_vectors", specs=[scalars] + [anywhere] * 4,
        scratch=[pltpu.VMEM((8, 16, D), bf16), pltpu.SemaphoreType.DMA((8,))],
    )


def picked(kernel, outs, specs, args, name, after=()):
    count, skip = len(specs), len(after)

    def body(*refs):
        kernel(*refs[:count], *refs[count + skip :])

    return pl.pallas_call(
        body,
        grid=(1,),
        out_shape=outs,
        in_specs=[*specs, *[anywhere] * skip],
        out_specs=[pl.BlockSpec(o.shape, lambda i, n=len(o.shape): (0,) * n) for o in outs],
        compiler_params=pltpu.CompilerParams(vmem_limit_bytes=SMALL_LIMIT),
        cost_estimate=pl.CostEstimate(flops=0, bytes_accessed=0, transcendentals=0),
        name=name,
    )(*args, *after)


ADD_ROWS = 96


def add_pieces_kernel(*refs):
    _, n, rows, _ = refs[0].shape
    for a in range(refs[0].shape[0]):
        for b in range(n):

            def step(i):
                here = rows_of(i, ADD_ROWS)
                total = refs[0][a, b, here, :].astype(f32)
                for ref in refs[1:-1]:
                    total = total + ref[a, b, here, :].astype(f32)
                refs[-1][a, b, here, :] = total.astype(bf16)

            loop(rows // ADD_ROWS, step)


def add_pieces(parts, first, count, after=()):
    _, n, rows, width = parts[0].shape
    block = (count, n, rows, width)
    return picked(
        add_pieces_kernel,
        [shape(block, bf16)],
        [pl.BlockSpec(block, lambda i: (first // count, 0, 0, 0))] * len(parts),
        parts,
        "add_pieces",
        after,
    )[0]


def rows_spec(rows):
    return pl.BlockSpec((rows, D), lambda i: (0, 0))


def piece_spec(rows, j):
    return pl.BlockSpec((1, 1, rows, D), lambda i: (0, j, 0, 0))


def sum_of(refs, here):
    total = refs[0][0, 0, here, :].astype(f32)
    for ref in refs[1:]:
        total = total + ref[0, 0, here, :].astype(f32)
    return total


def two_sums_kernel(table, keep_table, place, *refs):
    def step(i):
        here = rows_of(i, ADD_ROWS)
        sums = sum_of(refs[:4], here), sum_of(refs[4:8], here)
        refs[8][here, :] = by_plane(place, keep_table, sums)
        refs[9][here, :] = by_plane(place, table, sums).astype(bf16)

    loop(refs[8].shape[0] // ADD_ROWS, step)


def two_sums(place, table, first, second, name, after):
    rows = first[0][0].shape[2]
    args = first + second
    return picked(
        functools.partial(two_sums_kernel, table, tuple(1 - k for k in table)),
        [shape((rows, D), f32), shape((rows, D), bf16)],
        [scalars] + [piece_spec(rows, j) for _, j in args],
        [place] + [a for a, _ in args],
        name,
        after,
    )


def far_sums(place, rest, after=()):
    return two_sums(place, (1, 1, 0, 0), [(p, 0) for p in rest], [(p, 1) for p in rest], "far_sums", after)


def near_sums(place, zero, rest, after=()):
    return two_sums(place, (1, 0, 1, 0), [(p, 0) for p in zero], [(p, 2) for p in rest], "near_sums", after)


def last_sums_kernel(place, kept_near, kept_far, near, far, base, give):
    def step(i):
        here = rows_of(i, ADD_ROWS)
        sums = (kept_near[here, :] + near[here, :].astype(f32), kept_far[here, :] + far[here, :].astype(f32))
        give[here, :] = by_plane(place, (1, 0, 0, 1), sums).astype(bf16)
        base[here, :] = by_plane(place, (0, 1, 1, 0), sums)

    loop(base.shape[0] // ADD_ROWS, step)


def last_sums(place, *args, after=()):
    rows = args[0].shape[0]
    return picked(
        last_sums_kernel,
        [shape((rows, D), f32), shape((rows, D), bf16)],
        [scalars] + [rows_spec(rows)] * 4,
        [place, *args],
        "last_sums",
        after,
    )


def twice(values):
    high = values.astype(bf16)
    return high, (values - high.astype(f32)).astype(bf16)


def owner_kernel(
    base, last, left, right, left_root, right_root, master, slow,
    grad_to, left_to, right_to, master_to, slow_to, low_to,
    grad_v, last_v, left_v, right_v, left_root_v, right_root_v, master_v, slow_v, low_v, sems,
):
    pairs = (
        (base, grad_v), (last, last_v), (left_root, left_root_v), (right_root, right_root_v),
        (left, left_v), (right, right_v), (master, master_v), (slow, slow_v),
    )
    loads = [begin(a, b, sems.at[i]) for i, (a, b) in enumerate(pairs)]
    finish(loads[:2])
    grad_v[...] = grad_v[...] + last_v[...].astype(f32)
    sent = [begin(grad_v, grad_to, sems.at[8])]
    high, low = twice(grad_v[...])
    wide = jnp.concatenate([high, high, low], axis=1)
    finish(loads[2:4])
    root_high, root_low = twice(left_root_v[...])
    turned = contract(wide, jnp.concatenate([root_high, root_low, root_high], axis=0), 1, 0)
    high_t, low_t = twice(turned)
    root_high, root_low = twice(right_root_v[...])
    steered = (
        contract(root_high, high_t, 1, 0) + contract(root_high, low_t, 1, 0) + contract(root_low, high_t, 1, 0)
    )
    finish(loads[6:])
    made = master_v[...] - learning_rate * steered
    master_v[...] = made
    slow_v[...] = slow_decay * slow_v[...] + (1.0 - slow_decay) * made
    low_v[...] = made.astype(bf16)
    sent += [
        begin(master_v, master_to, sems.at[9]), begin(slow_v, slow_to, sems.at[10]), begin(low_v, low_to, sems.at[11])
    ]
    finish(loads[4:6])
    tall_a = jnp.concatenate([high, high, low], axis=0)
    tall_b = jnp.concatenate([high, low, high], axis=0)
    left_v[...] = stat_decay * left_v[...] + (1.0 - stat_decay) * contract(tall_a, tall_b, 0, 0)
    sent.append(begin(left_v, left_to, sems.at[12]))
    other = jnp.concatenate([high, low, high], axis=1)
    right_v[...] = stat_decay * right_v[...] + (1.0 - stat_decay) * contract(wide, other, 1, 1)
    finish(sent, begin(right_v, right_to, sems.at[13]))


def owner_step(base, last, left, right, left_root, right_root, master, slow):
    rows = base.shape[0]
    flat, stats, small_stats = (rows, D), (D, D), (rows, rows)
    return call(
        owner_kernel,
        [shape(flat, f32), shape(stats, f32), shape(small_stats, f32), shape(flat, f32), shape(flat, f32), shape(flat, bf16)],
        [anywhere] * 6,
        [
            pltpu.VMEM(flat, f32), pltpu.VMEM(flat, bf16), pltpu.VMEM(stats, f32), pltpu.VMEM(small_stats, f32),
            pltpu.VMEM(stats, f32), pltpu.VMEM(small_stats, f32), pltpu.VMEM(flat, f32), pltpu.VMEM(flat, f32),
            pltpu.VMEM(flat, bf16), pltpu.SemaphoreType.DMA((14,)),
        ],
        6 * D * rows * (2 * D + 2 * rows), 15 << 20,
        base, last, left, right, left_root, right_root, master, slow,
        specs=[anywhere] * 8, name="owner_step",
    )


def per_device(
    ring,
    tokens,
    cotangent,
    lengths,
    key_mask,
    type_ids,
    weights,
    vectors,
    master,
    slow_weights,
    left_stats,
    right_stats,
    left_root,
    right_root,
    vector_master,
    vector_moment,
    slow_vectors,
):
    ring = ring()
    place = ring.place
    slot_a, slot_b, table = ring.gather_early(weights, vectors)
    early = [*slot_a, *slot_b]
    types, keys = type_ids[None, :], key_mask[None, :]

    turned, context, spreads = attend(place, lengths, early, tokens, types, keys, table, after=ring.gather_late())
    pieces = early + ring.gather_last(context)
    layer_out, grad_first, grad_context, middle_sums, *parts = middle(
        place, pieces, tokens, types, context, cotangent, table
    )
    rest = ring.reduction(parts)
    rest.across()
    mixed = attend_back(place, lengths, turned, grad_context, spreads, keys, after=rest.give)
    *parts, vector_sums = mixed_grad(place, early, mixed, tokens, types, table, middle_sums)
    zero = ring.reduction(parts)
    swapped = ring.vectors_begin(vector_sums)
    rest.side(after=[vector_sums])
    zero.across(after=rest.give + swapped)
    crossed = ring.vectors_next(PLANE_B)
    input_grad = input_back(place, early, mixed, grad_first, after=zero.give)
    zero.side(after=[input_grad, *rest.last(), *crossed])
    crossed = ring.vectors_next(PLANE_A)
    ring.reduce_far(rest, after=zero.give)
    ring.reduce_near(zero, rest, after=crossed)
    crossed = ring.vectors_next(Z_NEAR)
    base, last = ring.reduce_last(after=crossed)
    ring.vectors_next(Z_FAR)
    owned_vector = ring.vectors_end()
    grad_t, left_new, right_new, master_t, slow_t, low_t = owner_step(
        base, last, left_stats, right_stats, left_root, right_root, master.T, slow_weights.T
    )
    owned_grad, master_new, slow_new, weights_new = grad_t.T, master_t.T, slow_t.T, low_t.T
    moment_new = stat_decay * vector_moment + (1.0 - stat_decay) * owned_vector * owned_vector
    vector_master_new = vector_master - vector_rate * owned_vector / (jnp.sqrt(moment_new) + 1e-08)
    slow_vectors_new = slow_decay * slow_vectors + (1.0 - slow_decay) * vector_master_new
    vectors_new = vector_master_new.astype(bf16)
    return (
        layer_out,
        input_grad,
        owned_grad,
        left_new,
        right_new,
        master_new,
        slow_new,
        weights_new,
        owned_vector,
        moment_new,
        vector_master_new,
        slow_vectors_new,
        vectors_new,
    )


def solution(mesh):
    in_specs = (
        P(("dp", "opt"), None),
        P(("dp", "opt"), None),
        P(("dp", "opt")),
        P(("dp", "opt")),
        P(("dp", "opt")),
        P(None, "dp"),
        P("dp"),
        P(None, ("dp", "opt")),
        P(None, ("dp", "opt")),
        P(("dp", "opt"), None),
        P(("dp", "opt"), None),
        P(("dp", "opt"), None),
        P(("dp", "opt"), None),
        P(("dp", "opt")),
        P(("dp", "opt")),
        P(("dp", "opt")),
    )
    out_specs = (
        P(("dp", "opt"), None),
        P(("dp", "opt"), None),
        P(None, ("dp", "opt")),
        P(("dp", "opt"), None),
        P(("dp", "opt"), None),
        P(None, ("dp", "opt")),
        P(None, ("dp", "opt")),
        P(None, ("dp", "opt")),
        P(("dp", "opt")),
        P(("dp", "opt")),
        P(("dp", "opt")),
        P(("dp", "opt")),
        P(("dp", "opt")),
    )
    ring = Ring if dict(mesh.shape) == {"dp": 16, "opt": 2} else Plain
    return jax.shard_map(
        functools.partial(per_device, ring),
        mesh=mesh,
        in_specs=in_specs,
        out_specs=out_specs,
        check_vma=False,
    )
```

```python
import functools
import math

import jax
import jax.numpy as jnp
import numpy as np
from jax import lax
from jax.experimental import pallas as pl
from jax.experimental.pallas import tpu as pltpu
from jax.sharding import PartitionSpec as P

D = 768
H = 12
HD = 64
FF = 3072
WCOLS = 4 * D + 2 * FF
NVEC = 10 * D + FF

highest = lax.Precision.HIGHEST
norm_eps = 1e-12
learning_rate = 0.03
vector_rate = 0.2
stat_decay = 0.5
slow_decay = 0.9
f32 = jnp.float32
bf16 = jnp.bfloat16
AXES = ("dp", "opt")


def contract(left_side, right_side, left_dim, right_dim):
    return lax.dot_general(
        left_side, right_side, (((left_dim,), (right_dim,)), ((), ())), preferred_element_type=f32
    )


def block_index(z, y, c, x):
    return z * 8 + y * 4 + c * 2 + x


def permutation(move):
    pairs = []
    for b in range(32):
        z, y, c, x = b // 8, (b // 4) % 2, (b // 2) % 2, b % 2
        pairs.append((b, block_index(*move(z, y, c, x))))
    return pairs


Z_CYCLE = permutation(lambda z, y, c, x: ((2, 0, 3, 1)[z], y, c, x))
Z_CYCLE_BACK = permutation(lambda z, y, c, x: ((1, 3, 0, 2)[z], y, c, x))
Z_NEAR = permutation(lambda z, y, c, x: (z ^ 1, y, c, x))
Z_FAR = permutation(lambda z, y, c, x: (z ^ 2, y, c, x))
Z_MIDDLE = permutation(lambda z, y, c, x: ((0, 2, 1, 3)[z], y, c, x))
PLANE_A = permutation(lambda z, y, c, x: (z, 1 - y, c, x) if c == 0 else (z, y, c, 1 - x))
PLANE_B = permutation(lambda z, y, c, x: (z, y, c, 1 - x) if c == 0 else (z, 1 - y, c, x))
CORES = permutation(lambda z, y, c, x: (z, y, 1 - c, x))


def send(values, pairs):
    return lax.ppermute(values, AXES, pairs)


QUARTER_SLOT = np.array([[0, 1, 3, 2], [1, 0, 3, 2], [1, 3, 0, 2], [1, 3, 2, 0]])


FAR_COST = 40 * 10**9


class Ring:
    def __init__(self):
        dp = lax.axis_index("dp")
        self.z, self.y, self.c = dp // 4, (dp // 2) % 2, dp % 2
        self.x = lax.axis_index("opt")
        slots = [self.number([int(v) for v in QUARTER_SLOT[:, q]]) for q in range(4)]
        self.place = jnp.stack([self.y, self.c, self.x, self.z] + slots).astype(jnp.int32)

    def number(self, values):
        out = values[3]
        for z in (2, 1, 0):
            out = jnp.where(self.z == z, values[z], out)
        return out

    def gather_early(self, weights, vectors):
        place, rows = self.place, weights.shape[1] // 2
        own = prepare_own(place, weights.T, vectors[None, :])
        one = send(own, Z_CYCLE)
        side = send(own, PLANE_A)
        pass_on, slab, pair_a = after_one(place, own, one, side)
        two = send(pass_on, Z_NEAR)
        across_a = send(pair_a, PLANE_B)
        far = send(slab, Z_FAR)
        middle = send(own, Z_MIDDLE)
        swap_a = send(pair_a, CORES)
        block_b, slot_c = after_two(place, pass_on, one, two, far, after=[across_a, swap_a])
        side_b = send(block_b, PLANE_A)
        side_c = send(slot_c, PLANE_A)
        three = send(middle, Z_NEAR)
        swap_aa = send(across_a, CORES)
        pair_b, slot_d = after_three(place, block_b, side_b, middle, three, after=[side_c, swap_aa])
        across_b = send(pair_b, PLANE_B)
        swap_b = send(pair_b, CORES)
        side_d = send(slot_d, PLANE_A)
        self.late = after_four(slot_c, side_c, slot_d, side_d, after=[across_b, swap_b])
        swap_bb = send(across_b, CORES)
        slot_b = [pair_b, across_b, swap_b, swap_bb]
        table = read_vectors(place, slot_b, vectors.shape[0] // 2)
        return [pair_a, across_a, swap_a, swap_aa], slot_b, table.reshape(-1, D)

    def gather_late(self):
        self.across = send(self.late, PLANE_B)
        self.swapped = send(self.late, CORES)
        return [self.late]

    def gather_last(self, context):
        across = hold(self.across, context)
        return [self.late, across, self.swapped, send(across, CORES)]

    def reduction(self, pieces, after=()):
        return Reduction(pieces, after)

    def reduce_far(self, both, after=()):
        self.kept_far, give = far_sums(self.place, both.parts(), after)
        self.far = hold(send(give, Z_FAR), cost=FAR_COST)
        return [give]

    def reduce_near(self, zero, three, after=()):
        self.kept_near, give, self.kept_rows = near_sums(self.place, zero.parts(), three.parts(), after)
        self.near = send(give, Z_NEAR)

    def reduce_last(self):
        base, give, rows, packed = last_sums(
            self.place, self.kept_near, self.kept_far, self.kept_rows, self.near, self.far
        )
        last = send(give, Z_CYCLE_BACK)
        arrived = send(packed, Z_FAR).astype(f32)
        half = rows.shape[1]
        rows = rows + (arrived[:, :half] + arrived[:, half:])
        vector = lax.dynamic_index_in_dim(rows, self.z, 0, False)
        return base, last, vector[: NVEC // 32]


class Reduction:
    def __init__(self, pieces, after=()):
        self.keep_lo, self.keep_hi, give_lo, give_hi = pieces
        if after:
            give_hi = hold(give_hi, *after)
        self.got_hi = send(give_hi, CORES)
        self.got_lo = send(give_lo, CORES)
        self.more = []

    def across(self, after=(), cost=0):
        self.give = [add_pieces([self.keep_hi, self.got_hi], 0, 2, after)]
        got = send(*self.give, PLANE_B)
        self.more.append(hold(got, cost=cost) if cost else got)

    def side(self, after=()):
        self.give = [add_pieces(self.parts(), 1, 1, after)]
        self.more.append(send(*self.give, PLANE_A))

    def parts(self):
        return [self.keep_lo, self.got_lo, *self.more]

    def first(self):
        return [self.got_hi]

    def last(self):
        return self.more[-1:]


class Plain:
    def __init__(self):
        self.place = jnp.asarray(np.array([0, 0, 0, 0, 0, 1, 2, 3]), jnp.int32)

    def gather_early(self, weights, vectors):
        turned = lax.all_gather(weights, "dp", axis=1, tiled=True).T
        blocks = turned.reshape(4, 8, -1, D)
        self.mine, self.theirs = (blocks[:, np.array(k)] for k in ([0, 4, 1, 5], [2, 3, 6, 7]))
        entries = vectors.shape[0]
        tiles = -(-entries // 2048)
        padded = jnp.pad(vectors, (0, tiles * 2048 - entries)).reshape(tiles * 16, 128)
        gathered = lax.all_gather(padded, "dp", axis=0, tiled=True)
        gathered = gathered.reshape(-1, tiles * 2048)[:, :entries].reshape(-1, D).astype(f32)
        slots = [[jnp.pad(v, ((0, 0), (0, 16), (0, 0))) for v in self.halves(q)] for q in (0, 1)]
        return *slots, gathered

    def halves(self, q):
        return [self.mine[q, :2], self.mine[q, 2:], self.theirs[q, :2], self.theirs[q, 2:]]

    def gather_late(self):
        return []

    def gather_last(self, context):
        return [jnp.stack(both, axis=1) for both in zip(self.halves(2), self.halves(3))]

    def reduction(self, pieces, after=()):
        return PlainReduction(pieces)

    def reduce_far(self, both, after=()):
        self.both = both
        return []

    def reduce_near(self, zero, three, after=()):
        self.zero, self.three = zero, three

    def reduce_last(self):
        zero = self.zero.whole()
        block = Q // 8
        packed = zero[0, :, block:, :].astype(f32)
        rows = packed[..., : D // 2] + packed[..., D // 2 :]
        vectors = jnp.swapaxes(rows[:, :4, : NVEC // 32], 0, 1).reshape(-1)
        vectors = lax.psum_scatter(vectors, AXES, scatter_dimension=0, tiled=True)
        sums = jnp.concatenate([zero[:, :, :block].reshape(-1, D), *(v.whole().reshape(-1, D) for v in (self.both, self.three))])
        owned = lax.psum_scatter(sums, AXES, scatter_dimension=0, tiled=True)
        return owned.astype(f32), jnp.zeros_like(owned), vectors


class PlainReduction:
    def __init__(self, pieces):
        self.pieces = jnp.concatenate(pieces)
        self.give = []

    def across(self, after=(), cost=0):
        pass

    def side(self, after=()):
        pass

    def first(self):
        return []

    def last(self):
        return []

    def whole(self):
        order = np.argsort(np.array([0, 4, 1, 5, 2, 3, 6, 7]))
        return jnp.swapaxes(self.pieces[order], 0, 1)


VMEM_LIMIT = 60 * 1024 * 1024
whole = pl.BlockSpec(memory_space=pltpu.VMEM)
scalars = pl.BlockSpec(memory_space=pltpu.SMEM)
anywhere = pl.BlockSpec(memory_space=pl.ANY)
shape = jax.ShapeDtypeStruct
CHUNK = 256
CHUNKS = FF // CHUNK
Q = 3 * D
SPAN = 256
PART = 256


def call(kernel, outs, out_specs, scratch, flops, moved, *args, specs, name, after=(), limit=VMEM_LIMIT):
    count, skip = len(specs), len(after)

    def body(*refs):
        kernel(*refs[:count], *refs[count + skip :])

    return pl.pallas_call(
        body,
        out_shape=outs,
        in_specs=[*specs, *[anywhere] * skip],
        out_specs=out_specs,
        scratch_shapes=scratch,
        compiler_params=pltpu.CompilerParams(vmem_limit_bytes=limit),
        cost_estimate=pl.CostEstimate(flops=flops, bytes_accessed=moved, transcendentals=0),
        name=name,
    )(*args, *after)


def block_place(place, who, k):
    y, c, x = place[0], place[1], place[2]
    core = c if who == 0 else 1 - c
    first, second = k & 1, k >> 1
    to_y = jnp.where(core == 0, y ^ first, y ^ second)
    to_x = jnp.where(core == 0, x ^ second, x ^ first)
    return to_y * 4 + core * 2 + to_x


def block_rows(place, who, k, rows):
    return pl.ds(pl.multiple_of(block_place(place, who, k) * rows, math.gcd(rows, 16)), rows)


def begin(source, target, sem):
    copy = pltpu.make_async_copy(source, target, sem)
    copy.start()
    return copy


def slot_pieces(slots):
    return [
        [(refs[k // 2], (k % 2,) + ((slot - 2,) if slot > 1 else ())) for k in range(8)]
        for slot, refs in enumerate(slots)
    ]


def ingest(place, quarter, slots, into, sems):
    rows = into.shape[0] // 8
    targets = [into.at[block_rows(place, k // 4, k % 4, rows)] for k in range(8)]
    all_pieces = slot_pieces(slots)
    for slot, pieces in enumerate(all_pieces):

        @pl.when(place[4 + quarter] == slot)
        def _():
            for k, (ref, index) in enumerate(pieces):
                pltpu.make_async_copy(ref.at[(*index, pl.ds(0, rows))], targets[k], sems.at[k]).start()

    return [
        pltpu.make_async_copy(ref.at[(*index, pl.ds(0, rows))], targets[k], sems.at[k])
        for k, (ref, index) in enumerate(all_pieces[0])
    ]


def piece_of(place, at):
    y, c, x = place[0], place[1], place[2]
    core = (at >> 1) & 1
    flip_y, flip_x = (at >> 2) ^ y, (at & 1) ^ x
    first = jnp.where(core == 0, flip_y, flip_x)
    second = jnp.where(core == 0, flip_x, flip_y)
    return jnp.where(core == c, 0, 2) + second, first


def hand_block(place, source, at, targets, part, sem):
    rows = source.shape[0] // 8
    which, first = piece_of(place, at)
    for k, target in enumerate(targets):

        @pl.when(which == k)
        def _():
            pltpu.make_async_copy(source.at[rows_of(at, rows)], target.at[first, part, pl.ds(0, rows)], sem).start()


def hand_rows(place, source, at, targets, sem):
    count = source.shape[1]
    which, first = piece_of(place, at)
    for k, target in enumerate(targets):

        @pl.when(which == k)
        def _():
            there = target.at[first, 0, pl.ds(target.shape[2] - count, count)]
            pltpu.make_async_copy(source.at[at], there, sem).start()


def pack_rows(values):
    return jnp.concatenate(twice(values), axis=1)


def unpack_rows(packed):
    half = packed.shape[1] // 2
    wide = packed.astype(f32)
    return wide[:, :half] + wide[:, half:]


def hand_wait(source, targets, part, sems):
    rows = source.shape[0] // 8
    for k in range(8):
        pltpu.make_async_copy(source.at[pl.ds(0, rows)], targets[0].at[0, part, pl.ds(0, rows)], sems.at[k]).wait()


def finish(*copies):
    for copy in copies:
        if isinstance(copy, (list, tuple)):
            finish(*copy)
        else:
            copy.wait()


def rows_of(i, step):
    return pl.ds(pl.multiple_of(i * step, math.gcd(step, 256)), step)


def loop(count, body):
    def step(i, carry):
        body(i)
        return carry

    lax.fori_loop(0, count, step, 0)


def column(row, width):
    return jnp.broadcast_to(row, (width, row.shape[1])).T


def is_region(types):
    return column((types == 1).astype(f32), 128)[:, 0:1] > 0.5


def allowed_keys(lengths, keys, s):
    slot = lax.broadcasted_iota(jnp.int32, (1, SPAN), 1)
    allowed = (slot < lengths[s]) & ((keys[:, rows_of(s, SPAN)] == 1) | (slot == 0))
    return jnp.where(allowed, 3e38, -1e30)


def embed(tokens, types, table):
    return tokens.astype(f32) + jnp.where(is_region(types), table[1:2, :], table[0:1, :])


def attend_kernel(
    place, lengths, a0, a1, a2, a3, b0, b1, b2, b3, tokens, types, keys, table,
    turned_out, context_out, spreads,
    weights, low, turned, context_turned, context, mask, sems,
):
    copies = ingest(place, 0, ((a0, a1, a2, a3), (b0, b1, b2, b3)), weights, sems)
    rows = tokens.shape[0]

    def prepare(i):
        here = rows_of(i, PART)
        low[here, :] = embed(tokens[here, :], types[:, here], table[...]).astype(bf16)
        mask[here, :] = column(allowed_keys(lengths, keys, i), SPAN)

    loop(rows // PART, prepare)
    finish(copies)
    step = 384

    def project(i):
        here = rows_of(i, step)
        half = rows_of(i % 2, step)
        bias = jnp.where(i // 2 == 0, table[4:5, half], jnp.where(i // 2 == 2, table[5:6, half], 0.0))
        made = contract(weights[here, :], low[...], 1, 1) + column(bias, 128)[:, 0:1]
        made = made * jnp.where(i < D // step, HD ** (-0.5), 1.0)
        turned[here, :] = made.astype(bf16)

    loop(Q // step, project)
    sent = begin(turned, turned_out, sems.at[8])

    together = 8

    def units(i):
        places = []
        for j in range(together):
            u = i * together + j
            places.append((u % H, pl.multiple_of((u % H) * HD, HD), rows_of(u // H, SPAN)))
        scores = [
            contract(turned[pl.ds(D + at, HD), cols], turned[pl.ds(at, HD), cols], 0, 0)
            for _, at, cols in places
        ]
        probs = []
        for (h, at, cols), score in zip(places, scores):
            score = jnp.minimum(score, mask[cols, :])
            peak = jnp.max(score, axis=0, keepdims=True)
            powers = jnp.exp(score - peak)
            total = jnp.sum(powers, axis=0, keepdims=True)
            probs.append((powers * (1.0 / total)).astype(bf16))
            spreads[pl.ds(h, 1), cols] = peak + jnp.log(total)
        for (h, at, cols), prob in zip(places, probs):
            context_turned[pl.ds(at, HD), cols] = contract(turned[pl.ds(2 * D + at, HD), cols], prob, 1, 0).astype(bf16)

    loop(H * (rows // SPAN) // together, units)

    def turn(i):
        here = rows_of(i, 128)
        context[here, :] = context_turned[:, here].T

    loop(rows // 128, turn)
    finish(begin(context, context_out, sems.at[9]), sent)


def attend(place, lengths, pieces, tokens, types, keys, table, after=()):
    rows = tokens.shape[0]
    return call(
        attend_kernel,
        [shape((Q, rows), bf16), shape((rows, D), bf16), shape((H, rows), f32)],
        [anywhere, anywhere, whole],
        [
            pltpu.VMEM((Q, D), bf16),
            pltpu.VMEM((rows, D), bf16),
            pltpu.VMEM((Q, rows), bf16),
            pltpu.VMEM((D, rows), bf16),
            pltpu.VMEM((rows, D), bf16),
            pltpu.VMEM((rows, SPAN), f32),
            pltpu.SemaphoreType.DMA((10,)),
        ],
        2 * rows * Q * D + 4 * rows * 256 * D,
        20 << 20,
        place, lengths, *pieces, tokens, types, keys, table,
        specs=[scalars] * 2 + [anywhere] * 8 + [whole] * 4,
        name="attend",
        after=after,
    )


def normalise(inputs):
    centre = jnp.mean(inputs, axis=-1, keepdims=True)
    offset = inputs - centre
    spread = lax.rsqrt(jnp.mean(offset * offset, axis=-1, keepdims=True) + norm_eps)
    return offset * spread, spread


def normalise_back(scaled, unit, spread):
    return spread * (
        scaled
        - jnp.mean(scaled, axis=-1, keepdims=True)
        - unit * jnp.mean(scaled * unit, axis=-1, keepdims=True)
    )


def gelu_both(v):
    cumulative = 0.5 * (1.0 + lax.erf(v * math.sqrt(0.5)))
    density = jnp.exp(-0.5 * v * v) * (1.0 / math.sqrt(2.0 * math.pi))
    return v * cumulative, cumulative + v * density


def weight_chunk(weights, offset, i):
    return weights[pl.ds(pl.multiple_of(offset + i * CHUNK, CHUNK), CHUNK), :]


def row_sums(count, body, sums, rows):
    zero = jnp.zeros((8, D), f32)

    def step(i, carry):
        made = body(i)
        return tuple(
            have + jnp.sum(more.reshape(-1, 8, D), axis=0) for have, more in zip(carry, made)
        )

    made = lax.fori_loop(0, count, step, (zero,) * len(rows))
    for have, row in zip(made, rows):
        sums[row : row + 1, 0:D] = jnp.sum(have, axis=0, keepdims=True)


STEP = 512


def middle_kernel(
    place, a0, a1, a2, a3, b0, b1, b2, b3, c0, c1, c2, c3, tokens_in, context_in, cotangent_in, types, table,
    layer_out_to, grad_first_to, grad_context_to, sums,
    keep_lo, keep_hi, give_lo, give_hi, keep_lo3, keep_hi3, give_lo3, give_hi3,
    weights, pre_a, pre_b, total, tokens, context, cotangent, layer_out, active, slope, unit_one, spread_one, normed_low,
    grad_context, down_made, sems, more,
):
    rows = tokens.shape[0]
    slots = ((a0, a1, a2, a3), (b0, b1, b2, b3), (c0, c1, c2, c3), (c0, c1, c2, c3))
    early = [begin(context_in, context, more.at[0]), begin(tokens_in, tokens, more.at[1])]
    batches = [ingest(place, 1, slots, weights.at[pl.ds(0, Q)], sems.at[0])]
    up, down = D, D + FF
    finish(early, batches[0])
    batches.append(ingest(place, 2, slots, weights.at[pl.ds(Q, Q)], sems.at[1]))
    batches.append(ingest(place, 3, slots, weights.at[pl.ds(2 * Q, Q)], sems.at[2]))
    late = begin(cotangent_in, cotangent, more.at[2])

    def branch(i):
        here = rows_of(i, SPAN)
        total[here, :] = contract(context[here, :], weights[0:D, :], 1, 1)

    loop(rows // SPAN, branch)

    def first(i):
        here = rows_of(i, PART)
        unit, spread = normalise(embed(tokens[here, :], types[:, here], table[...]) + (total[here, :] + table[6:7, :]))
        unit_one[here, :] = unit
        spread_one[here, :] = jnp.broadcast_to(spread, (PART, 128))
        normed_low[here, :] = (unit * table[2:3, :] + table[3:4, :]).astype(bf16)

    loop(rows // PART, first)
    sent = []
    targets = (keep_lo, keep_hi, give_lo, give_hi)
    targets3 = (keep_lo3, keep_hi3, give_lo3, give_hi3)
    finish(batches[1])

    def gelu(pre, i, here):
        bias = table[pl.ds(10 + i // (D // CHUNK), 1), rows_of(i % (D // CHUNK), CHUNK)]
        return gelu_both(pre[here, :] + bias)

    def keep_gelu(made, i, here):
        cols = rows_of(i, CHUNK)
        active[here, cols] = made[0].astype(bf16)
        slope[here, cols] = made[1]

    everything = slice(None)

    def forward(t):
        before = jnp.maximum(2 * t - 1, 0)
        both = gelu(pre_b, before, everything)
        pre_a[...] = contract(normed_low[...], weight_chunk(weights, up, 2 * t), 1, 1)
        keep_gelu(both, before, everything)
        both = gelu(pre_a, 2 * t, everything)
        pre_b[...] = contract(normed_low[...], weight_chunk(weights, up, 2 * t + 1), 1, 1)
        keep_gelu(both, 2 * t, everything)

    loop(CHUNKS // 2, forward)

    def forward_end(i):
        here = rows_of(i, PART)
        keep_gelu(gelu(pre_b, CHUNKS - 1, here), CHUNKS - 1, here)

    loop(rows // PART, forward_end)
    finish(batches[2])

    def add_down(i):
        here = rows_of(i, SPAN)
        total[here, :] = contract(active[here, :], weights[down : down + FF, :], 1, 0)

    loop(rows // SPAN, add_down)
    finish(late)

    def second(i):
        here = rows_of(i, PART)
        normed_one = unit_one[here, :] * table[2:3, :] + table[3:4, :]
        unit, spread = normalise(normed_one + (total[here, :] + table[9:10, :]))
        layer_out[here, :] = (unit * table[7:8, :] + table[8:9, :]).astype(bf16)
        upstream = cotangent[here, :].astype(f32)
        grad = normalise_back(upstream * table[7:8, :], unit, spread)
        total[here, :] = grad
        low = grad.astype(bf16)
        tokens[here, :] = low
        return upstream * unit, upstream, low.astype(f32)

    row_sums(rows // PART, second, sums, (7, 8, 9))
    sent.append(begin(layer_out, layer_out_to, more.at[5]))

    def weigh_down(i):
        here = rows_of(i, STEP)
        down_made[here, :] = contract(active[:, here], tokens[...], 0, 0).astype(bf16)

    loop(FF // STEP, weigh_down)
    third_quarter = down_made.at[pl.ds(D, Q)]
    loop(8, lambda p: hand_block(place, third_quarter, p, targets3, 0, sems.at[2, p]))

    def through(pre, i, here):
        return (pre[here, :] * slope[here, rows_of(i, CHUNK)]).astype(bf16)

    def backward(t):
        before = jnp.maximum(2 * t - 1, 0)
        low = through(pre_b, before, everything)
        pre_a[...] = contract(tokens[...], weight_chunk(weights, down, 2 * t), 1, 1)
        active[:, rows_of(before, CHUNK)] = low
        low = through(pre_a, 2 * t, everything)
        pre_b[...] = contract(tokens[...], weight_chunk(weights, down, 2 * t + 1), 1, 1)
        active[:, rows_of(2 * t, CHUNK)] = low

    loop(CHUNKS // 2, backward)

    def backward_end(i):
        here = rows_of(i, PART)
        active[here, rows_of(CHUNKS - 1, CHUNK)] = through(pre_b, CHUNKS - 1, here)

    loop(rows // PART, backward_end)

    def add_up(i):
        here = rows_of(i, SPAN)
        total[here, :] += contract(active[here, :], weights[up : up + FF, :], 1, 0)

    loop(rows // SPAN, add_up)

    def third(i):
        here = rows_of(i, PART)
        upstream = total[here, :]
        unit = unit_one[here, :]
        grad = normalise_back(upstream * table[2:3, :], unit, spread_one[here, 0:1])
        total[here, :] = grad
        low = grad.astype(bf16)
        cotangent[here, :] = low
        of_one = is_region(types[:, here])
        return upstream * unit, upstream, low.astype(f32), jnp.where(of_one, 0.0, grad), jnp.where(of_one, grad, 0.0)

    row_sums(rows // PART, third, sums, (2, 3, 6, 0, 1))
    sent.append(begin(total, grad_first_to, more.at[8]))

    def through_out(i):
        here = rows_of(i, SPAN)
        grad_context[:, here] = contract(cotangent[here, :], weights[0:D, :], 1, 0).T.astype(bf16)

    loop(rows // SPAN, through_out)
    sent.append(begin(grad_context, grad_context_to, more.at[10]))
    moved = begin(down_made.at[pl.ds(0, D)], weights.at[pl.ds(D + FF, D)], more.at[9])

    def weigh_up(i):
        here = rows_of(i, STEP)
        rows_there = pl.ds(pl.multiple_of(D + i * STEP, 256), STEP)
        weights[rows_there, :] = contract(active[:, here], normed_low[...], 0, 0).astype(bf16)
        added = jnp.sum(active[:, here].astype(f32), 0, keepdims=True)
        sums[pl.ds(10, 1), here] = added

    half = FF // STEP // 2
    loop(half, lambda i: weigh_up(half + i))
    finish(moved)
    hand_wait(third_quarter, targets3, 0, sems.at[2])
    quarters = weights.at[pl.ds(0, Q)], weights.at[pl.ds(Q, Q)]
    loop(8, lambda p: hand_block(place, quarters[1], p, targets, 1, sems.at[1, p]))

    def weigh_out(i):
        here = rows_of(i, 384)
        weights[here, :] = contract(cotangent[:, here], context[...], 0, 0).astype(bf16)

    loop(2, weigh_out)
    loop(half, weigh_up)
    loop(8, lambda p: hand_block(place, quarters[0], p, targets, 0, sems.at[0, p]))
    hand_wait(quarters[1], targets, 1, sems.at[1])
    hand_wait(quarters[0], targets, 0, sems.at[0])
    finish(sent)


def middle(place, pieces, tokens, types, context, cotangent, table, after=()):
    rows = tokens.shape[0]
    tall = pltpu.VMEM((rows, D), bf16)
    return call(
        middle_kernel,
        [shape((rows, D), bf16), shape((rows, D), f32), shape((D, rows), bf16), shape((11, FF), f32)]
        + [shape((2, 2, Q // 8, D), bf16)] * 4
        + [shape((2, 1, Q // 8, D), bf16)] * 4,
        [anywhere] * 3 + [whole] + [anywhere] * 8,
        [
            pltpu.VMEM((3 * Q, D), bf16),
            pltpu.VMEM((rows, CHUNK), f32),
            pltpu.VMEM((rows, CHUNK), f32),
            pltpu.VMEM((rows, D), f32),
            tall,
            tall,
            tall,
            tall,
            pltpu.VMEM((rows, FF), bf16),
            pltpu.VMEM((rows, FF), f32),
            pltpu.VMEM((rows, D), f32),
            pltpu.VMEM((rows, 128), f32),
            tall,
            pltpu.VMEM((D, rows), bf16),
            pltpu.VMEM((FF, D), bf16),
            pltpu.SemaphoreType.DMA((3, 8)),
            pltpu.SemaphoreType.DMA((11,)),
        ],
        6 * rows * 3 * Q * D,
        60 << 20,
        place, *pieces, tokens, context, cotangent, types, table,
        specs=[scalars] + [anywhere] * 15 + [whole] * 2,
        name="middle",
        after=after,
    )


def attend_back_kernel(
    place, lengths, turned, grad_context, spreads, keys,
    mixed_to,
    mixed, mask, sems,
):
    rows = turned.shape[1]

    def prepare(i):
        here = rows_of(i, PART)
        mask[here, :] = column(allowed_keys(lengths, keys, i), SPAN)

    loop(rows // PART, prepare)

    together = 6

    def units(i):
        places = []
        for j in range(together):
            u = i * together + j
            places.append((u % H, pl.multiple_of((u % H) * HD, HD), rows_of(u // H, SPAN)))
        query = [turned[pl.ds(at, HD), cols] for _, at, cols in places]
        key = [turned[pl.ds(D + at, HD), cols] for _, at, cols in places]
        grad = [grad_context[pl.ds(at, HD), cols] for _, at, cols in places]
        scores = [contract(k, q, 0, 0) for k, q in zip(key, query)]
        grad_probs = [
            contract(turned[pl.ds(2 * D + at, HD), cols], g, 0, 0) for (_, at, cols), g in zip(places, grad)
        ]
        made = []
        for (h, at, cols), score, grad_prob in zip(places, scores, grad_probs):
            probs = jnp.exp(jnp.minimum(score, mask[cols, :]) - spreads[pl.ds(h, 1), cols])
            inner = jnp.sum(probs * grad_prob, axis=0, keepdims=True)
            made.append(((probs * (grad_prob - inner)).astype(bf16), probs.astype(bf16)))
        for (h, at, cols), q, k, g, (grad_score, prob) in zip(places, query, key, grad, made):
            mixed[pl.ds(at, HD), cols] = (contract(k, grad_score, 1, 0) * HD ** (-0.5)).astype(bf16)
            mixed[pl.ds(D + at, HD), cols] = contract(q, grad_score, 1, 1).astype(bf16)
            mixed[pl.ds(2 * D + at, HD), cols] = contract(g, prob, 1, 1).astype(bf16)

    loop(H * (rows // SPAN) // together, units)
    finish(begin(mixed, mixed_to, sems.at[0]))


def attend_back(place, lengths, turned, grad_context, spreads, keys, after=()):
    rows = turned.shape[1]
    return call(
        attend_back_kernel,
        [shape((Q, rows), bf16)],
        [anywhere],
        [
            pltpu.VMEM((Q, rows), bf16),
            pltpu.VMEM((rows, SPAN), f32),
            pltpu.SemaphoreType.DMA((1,)),
        ],
        10 * rows * 256 * D,
        25 << 20,
        place, lengths, turned, grad_context, spreads, keys,
        specs=[scalars] * 2 + [whole] * 4,
        limit=36 * 1024 * 1024,
        name="attend_back",
        after=after,
    )[0]


def mixed_grad_kernel(
    place, a0, a1, a2, a3, b0, b1, b2, b3, mixed_in, tokens, types, table, middle_sums,
    keep_lo, keep_hi, give_lo, give_hi,
    low, mixed, made, weights, by_type, sums, wide, packed, sems, more, others,
):
    step = 384
    for i in range(Q // step):
        here = pl.ds(i * step, step)
        begin(mixed_in.at[here], mixed.at[here], more.at[i])
    copies = ingest(place, 0, ((a0, a1, a2, a3), (b0, b1, b2, b3)), weights, sems)
    rows = tokens.shape[0]
    targets = (keep_lo, keep_hi, give_lo, give_hi)

    def prepare(i):
        here = rows_of(i, PART)
        low[here, :] = embed(tokens[here, :], types[:, here], table[...]).astype(bf16)

    loop(rows // PART, prepare)
    type_row = lax.broadcasted_iota(jnp.int32, (8, rows), 0)
    one_hot = (type_row == types[...]).astype(f32).astype(bf16)

    def weigh(i):
        here = rows_of(i, step)
        pltpu.make_async_copy(mixed_in.at[here], mixed.at[here], more.at[i]).wait()
        made[here, :] = contract(mixed[here, :], low[...], 1, 0).astype(bf16)
        by_type[:, here] = contract(one_hot, mixed[here, :], 1, 1)

    loop(Q // step, weigh)
    finish(copies)
    loop(8, lambda p: hand_block(place, made, p, targets, 0, sems.at[p]))
    high, rest = twice(by_type[...])
    through = contract(high, weights[...], 1, 0) + contract(rest, weights[...], 1, 0)
    sums[0:10, :] = middle_sums[0:10, 0:D]
    sums[0:2, :] = middle_sums[0:2, 0:D] + through[0:2, :]
    for row, start in ((4, 0), (5, 2 * D)):
        sums[row : row + 1, :] = by_type[0:1, start : start + D] + by_type[1:2, start : start + D]
    for i in range(FF // D):
        sums[10 + i : 11 + i, :] = middle_sums[10:11, i * D : (i + 1) * D]
    wide[...] = jnp.zeros_like(wide)
    entries = NVEC // 32
    for block in range(8):
        for z in range(4):
            row, lane = divmod((z * 8 + block) * entries, D)
            taken = min(entries, D - lane)
            wide[block, z : z + 1, 0:taken] = sums[row : row + 1, lane : lane + taken]
            if taken < entries:
                wide[block, z : z + 1, taken:entries] = sums[row + 1 : row + 2, 0 : entries - taken]
        packed[block] = pack_rows(wide[block])

    loop(8, lambda p: hand_rows(place, packed, p, targets, others.at[p]))
    hand_wait(made, targets, 0, sems)
    for p in range(8):
        pltpu.make_async_copy(packed.at[p], keep_lo.at[0, 0, pl.ds(Q // 8, 16)], others.at[p]).wait()


def mixed_grad(place, pieces, mixed, tokens, types, table, middle_sums, after=()):
    rows = tokens.shape[0]
    return call(
        mixed_grad_kernel,
        [shape((2, 1, Q // 8 + 16, D), bf16)] * 4,
        [anywhere] * 4,
        [
            pltpu.VMEM((rows, D), bf16),
            pltpu.VMEM((Q, rows), bf16),
            pltpu.VMEM((Q, D), bf16),
            pltpu.VMEM((Q, D), bf16),
            pltpu.VMEM((8, Q), f32),
            pltpu.VMEM((16, D), f32),
            pltpu.VMEM((8, 16, D // 2), f32),
            pltpu.VMEM((8, 16, D), bf16),
            pltpu.SemaphoreType.DMA((8,)),
            pltpu.SemaphoreType.DMA((6,)),
            pltpu.SemaphoreType.DMA((8,)),
        ],
        2 * rows * Q * D,
        12 << 20,
        place, *pieces, mixed, tokens, types, table, middle_sums,
        specs=[scalars] + [anywhere] * 9 + [whole] * 4,
        name="mixed_grad",
        after=after,
    )


def input_kernel(place, a0, a1, a2, a3, b0, b1, b2, b3, mixed, grad_first, input_grad_to, weights, made, sems):
    finish(ingest(place, 0, ((a0, a1, a2, a3), (b0, b1, b2, b3)), weights, sems))
    rows = grad_first.shape[0]

    def through(i):
        here = rows_of(i, SPAN)
        made[here, :] = grad_first[here, :] + contract(mixed[:, here], weights[...], 0, 0)
        begin(made.at[here], input_grad_to.at[here], sems.at[i])

    loop(rows // SPAN, through)
    for i in range(rows // SPAN):
        here = pl.ds(i * SPAN, SPAN)
        pltpu.make_async_copy(made.at[here], input_grad_to.at[here], sems.at[i]).wait()


def input_back(place, pieces, mixed, grad_first, after=()):
    rows = grad_first.shape[0]
    return call(
        input_kernel,
        [shape((rows, D), f32)],
        [anywhere],
        [pltpu.VMEM((Q, D), bf16), pltpu.VMEM((rows, D), f32), pltpu.SemaphoreType.DMA((8,))],
        0,
        0,
        place, *pieces, mixed, grad_first,
        specs=[scalars] + [anywhere] * 8 + [whole] * 2,
        name="input_back",
        after=after,
    )[0]


SMALL_LIMIT = 16 * 1024 * 1024


def small(kernel, outs, *args, name, after=(), scratch=(), specs=None, out_specs=None):
    specs = specs or [scalars if a.dtype == jnp.int32 else whole for a in args]
    many = isinstance(outs, (list, tuple))
    return call(
        kernel, outs, out_specs or ([whole] * len(outs) if many else whole), list(scratch), 0, 0, *args,
        specs=specs, name=name, after=after, limit=SMALL_LIMIT,
    )


def hold(values, *after, cost=0):
    skip = len(after)
    return pl.pallas_call(
        lambda *refs: None,
        out_shape=shape(values.shape, values.dtype),
        in_specs=[anywhere] * (1 + skip),
        out_specs=anywhere,
        input_output_aliases={0: 0},
        cost_estimate=pl.CostEstimate(flops=cost, bytes_accessed=0, transcendentals=0),
        name="hold",
    )(values, *after)


def prepare_kernel(place, turned, few, own, sem):
    rows = own.shape[0] - 16
    copy = begin(turned.at[pl.ds(pl.multiple_of(place[2] * rows, 16), rows)], own.at[pl.ds(0, rows)], sem)
    entries = few.shape[1] // 2
    row = few[...].astype(f32)
    row = jnp.where(place[2] == 0, row[:, :entries], row[:, entries:])
    here = lax.broadcasted_iota(jnp.int32, (16, entries), 0) == place[3]
    own[rows:, :] = jnp.zeros((16, D), bf16)
    own[rows:, 0:entries] = jnp.where(here, row, 0.0).astype(bf16)
    finish(copy)


def prepare_own(place, turned, few):
    return small(
        prepare_kernel, shape((turned.shape[0] // 2 + 16, D), bf16), place, turned, few,
        name="prepare_own", scratch=[pltpu.SemaphoreType.DMA], specs=[scalars, anywhere, whole],
    )


def by_plane(place, table, choices):
    out = choices[table[3]]
    for z in (2, 1, 0):
        out = jnp.where(place[3] == z, choices[table[z]], out)
    return out


def merge(old, new):
    old, new = old.astype(f32), new.astype(f32)
    return jnp.where(old == 0.0, new, old).astype(bf16)


def after_one_kernel(place, own, one, side, pass_on, slab, pair):
    rows = own.shape[0] - 16
    pass_on[:rows, :] = by_plane(place, (0, 1, 1, 0), (own[:rows, :], one[:rows, :]))
    merged = merge(own[rows:, :], one[rows:, :])
    pass_on[rows:, :] = merged
    slab[...] = merged
    pair[0] = own[...]
    pair[1] = side[...]


def after_one(place, own, one, side):
    outs = [shape(own.shape, bf16), shape((16, D), bf16), shape((2, *own.shape), bf16)]
    return small(after_one_kernel, outs, place, own, one, side, name="after_one")


def after_two_kernel(place, pass_on, one, two, far, block, slot):
    rows = one.shape[0] - 16
    block[:rows, :] = by_plane(place, (0, 1, 0, 1), (one[:rows, :], two[:rows, :]))
    block[rows:, :] = merge(merge(pass_on[rows:, :], two[rows:, :]), far[...])
    slot[...] = by_plane(place, (1, 0, 1, 0), (one[:rows, :], two[:rows, :]))


def after_two(place, pass_on, one, two, far, after):
    outs = [shape(one.shape, bf16), shape((one.shape[0] - 16, D), bf16)]
    return small(after_two_kernel, outs, place, pass_on, one, two, far, name="after_two", after=after)


def after_three_kernel(place, block, side, middle, three, pair, slot):
    rows = slot.shape[0]
    pair[0] = block[...]
    pair[1] = side[...]
    slot[...] = by_plane(place, (1, 0, 0, 1), (middle[:rows, :], three[:rows, :]))


def after_three(place, block, side, middle, three, after):
    outs = [shape((2, *block.shape), bf16), shape((block.shape[0] - 16, D), bf16)]
    return small(after_three_kernel, outs, place, block, side, middle, three, name="after_three", after=after)


def after_four_kernel(slot_c, side_c, slot_d, side_d, late):
    late[0, 0], late[0, 1] = slot_c[...], slot_d[...]
    late[1, 0], late[1, 1] = side_c[...], side_d[...]


def after_four(slot_c, side_c, slot_d, side_d, after):
    outs = shape((2, 2, *slot_c.shape), bf16)
    return small(after_four_kernel, outs, slot_c, side_c, slot_d, side_d, name="after_four", after=after)


def read_vectors_kernel(entries, place, a, b, c, d, out, got, sems):
    rows = a.shape[1] - 16
    refs = (a, b, c, d)
    finish([begin(refs[k // 2].at[k % 2, pl.ds(rows, 16)], got.at[k], sems.at[k]) for k in range(8)])
    for k in range(8):
        at = block_place(place, k // 4, k % 4)
        slab = got[k].astype(f32)
        for z in range(4):
            out[pl.ds(z * 8 + at, 1), :] = slab[z : z + 1, 0:entries]


def read_vectors(place, pieces, entries):
    return small(
        functools.partial(read_vectors_kernel, entries), shape((32, entries), f32), place, *pieces,
        name="read_vectors", specs=[scalars] + [anywhere] * 4,
        scratch=[pltpu.VMEM((8, 16, D), bf16), pltpu.SemaphoreType.DMA((8,))],
    )


def picked(kernel, outs, specs, args, name, after=()):
    count, skip = len(specs), len(after)

    def body(*refs):
        kernel(*refs[:count], *refs[count + skip :])

    return pl.pallas_call(
        body,
        grid=(1,),
        out_shape=outs,
        in_specs=[*specs, *[anywhere] * skip],
        out_specs=[pl.BlockSpec(o.shape, lambda i, n=len(o.shape): (0,) * n) for o in outs],
        compiler_params=pltpu.CompilerParams(vmem_limit_bytes=SMALL_LIMIT),
        cost_estimate=pl.CostEstimate(flops=0, bytes_accessed=0, transcendentals=0),
        name=name,
    )(*args, *after)


ADD_ROWS = 96


def add_pieces_kernel(*refs):
    count, n, rows, _ = refs[0].shape
    block = rows // ADD_ROWS * ADD_ROWS
    for a in range(count):
        for b in range(n):

            def step(i):
                here = rows_of(i, ADD_ROWS)
                total = refs[0][a, b, here, :].astype(f32)
                for ref in refs[1:-1]:
                    total = total + ref[a, b, here, :].astype(f32)
                refs[-1][a, b, here, :] = total.astype(bf16)

            loop(block // ADD_ROWS, step)
            if rows > block:
                refs[-1][a, b, block:, :] = pack_rows(sum(unpack_rows(ref[a, b, block:, :]) for ref in refs[:-1]))


def add_pieces(parts, first, count, after=()):
    _, n, rows, width = parts[0].shape
    block = (count, n, rows, width)
    return picked(
        add_pieces_kernel,
        [shape(block, bf16)],
        [pl.BlockSpec(block, lambda i: (first // count, 0, 0, 0))] * len(parts),
        parts,
        "add_pieces",
        after,
    )[0]


def piece_spec(part, j):
    return pl.BlockSpec((1, 1, *part.shape[2:]), lambda i: (0, j, 0, 0))


def sum_of(refs, here):
    total = refs[0][0, 0, here, :].astype(f32)
    for ref in refs[1:]:
        total = total + ref[0, 0, here, :].astype(f32)
    return total


def two_sums_kernel(table, keep_table, place, *refs):
    keep, give = refs[8], refs[9]
    block = keep.shape[0]

    def step(i):
        here = rows_of(i, ADD_ROWS)
        sums = sum_of(refs[:4], here), sum_of(refs[4:8], here)
        keep[here, :] = by_plane(place, keep_table, sums)
        give[here, :] = by_plane(place, table, sums).astype(bf16)

    loop(block // ADD_ROWS, step)
    if len(refs) > 10:
        total = sum(unpack_rows(ref[0, 0, block:, :]) for ref in refs[:4])
        refs[10][...] = total
        give[block:, :] = pack_rows(total)


def two_sums(place, table, first, second, name, after):
    rows, more = second[0][0].shape[2], first[0][0].shape[2] - second[0][0].shape[2]
    args = first + second
    return picked(
        functools.partial(two_sums_kernel, table, tuple(1 - k for k in table)),
        [shape((rows, D), f32), shape((rows + more, D), bf16)] + ([shape((more, D // 2), f32)] if more else []),
        [scalars] + [piece_spec(p, j) for p, j in args],
        [place] + [a for a, _ in args],
        name,
        after,
    )


def far_sums(place, rest, after=()):
    return two_sums(place, (1, 1, 0, 0), [(p, 0) for p in rest], [(p, 1) for p in rest], "far_sums", after)


def near_sums(place, zero, rest, after=()):
    return two_sums(place, (1, 0, 1, 0), [(p, 0) for p in zero], [(p, 0) for p in rest], "near_sums", after)


def last_sums_kernel(place, kept_near, kept_far, kept_rows, near, far, base, give, sums, packed):
    block = base.shape[0]

    def step(i):
        here = rows_of(i, ADD_ROWS)
        both = (kept_near[here, :] + near[here, :].astype(f32), kept_far[here, :] + far[here, :].astype(f32))
        give[here, :] = by_plane(place, (1, 0, 0, 1), both).astype(bf16)
        base[here, :] = by_plane(place, (0, 1, 1, 0), both)

    loop(block // ADD_ROWS, step)
    total = kept_rows[...] + unpack_rows(near[block:, :])
    sums[...] = total
    packed[...] = pack_rows(total)


def last_sums(place, *args):
    rows, more = args[0].shape[0], args[2].shape
    return picked(
        last_sums_kernel,
        [shape((rows, D), f32), shape((rows, D), bf16), shape(more, f32), shape((more[0], D), bf16)],
        [scalars] + [pl.BlockSpec(a.shape, lambda i: (0, 0)) for a in args],
        [place, *args],
        "last_sums",
    )


def twice(values):
    high = values.astype(bf16)
    return high, (values - high.astype(f32)).astype(bf16)


def owner_kernel(
    base, last, left, right, left_root, right_root, master, slow,
    grad_to, left_to, right_to, master_to, slow_to, low_to,
    grad_v, last_v, left_v, right_v, left_root_v, right_root_v, master_v, slow_v, low_v, sems,
):
    pairs = (
        (base, grad_v), (last, last_v), (left_root, left_root_v), (right_root, right_root_v),
        (left, left_v), (right, right_v), (master, master_v), (slow, slow_v),
    )
    loads = [begin(a, b, sems.at[i]) for i, (a, b) in enumerate(pairs)]
    finish(loads[:2])
    grad_v[...] = grad_v[...] + last_v[...].astype(f32)
    sent = [begin(grad_v, grad_to, sems.at[8])]
    high, low = twice(grad_v[...])
    wide = jnp.concatenate([high, high, low], axis=1)
    finish(loads[2:4])
    root_high, root_low = twice(left_root_v[...])
    turned = contract(wide, jnp.concatenate([root_high, root_low, root_high], axis=0), 1, 0)
    high_t, low_t = twice(turned)
    root_high, root_low = twice(right_root_v[...])
    steered = (
        contract(root_high, high_t, 1, 0) + contract(root_high, low_t, 1, 0) + contract(root_low, high_t, 1, 0)
    )
    finish(loads[6:])
    made = master_v[...] - learning_rate * steered
    master_v[...] = made
    slow_v[...] = slow_decay * slow_v[...] + (1.0 - slow_decay) * made
    low_v[...] = made.astype(bf16)
    sent += [
        begin(master_v, master_to, sems.at[9]), begin(slow_v, slow_to, sems.at[10]), begin(low_v, low_to, sems.at[11])
    ]
    finish(loads[4:6])
    tall_a = jnp.concatenate([high, high, low], axis=0)
    tall_b = jnp.concatenate([high, low, high], axis=0)
    left_v[...] = stat_decay * left_v[...] + (1.0 - stat_decay) * contract(tall_a, tall_b, 0, 0)
    sent.append(begin(left_v, left_to, sems.at[12]))
    other = jnp.concatenate([high, low, high], axis=1)
    right_v[...] = stat_decay * right_v[...] + (1.0 - stat_decay) * contract(wide, other, 1, 1)
    finish(sent, begin(right_v, right_to, sems.at[13]))


def owner_step(base, last, left, right, left_root, right_root, master, slow):
    rows = base.shape[0]
    flat, stats, small_stats = (rows, D), (D, D), (rows, rows)
    return call(
        owner_kernel,
        [shape(flat, f32), shape(stats, f32), shape(small_stats, f32), shape(flat, f32), shape(flat, f32), shape(flat, bf16)],
        [anywhere] * 6,
        [
            pltpu.VMEM(flat, f32), pltpu.VMEM(flat, bf16), pltpu.VMEM(stats, f32), pltpu.VMEM(small_stats, f32),
            pltpu.VMEM(stats, f32), pltpu.VMEM(small_stats, f32), pltpu.VMEM(flat, f32), pltpu.VMEM(flat, f32),
            pltpu.VMEM(flat, bf16), pltpu.SemaphoreType.DMA((14,)),
        ],
        6 * D * rows * (2 * D + 2 * rows), 15 << 20,
        base, last, left, right, left_root, right_root, master, slow,
        specs=[anywhere] * 8, name="owner_step",
    )


def per_device(
    ring,
    tokens,
    cotangent,
    lengths,
    key_mask,
    type_ids,
    weights,
    vectors,
    master,
    slow_weights,
    left_stats,
    right_stats,
    left_root,
    right_root,
    vector_master,
    vector_moment,
    slow_vectors,
):
    ring = ring()
    place = ring.place
    slot_a, slot_b, table = ring.gather_early(weights, vectors)
    early = [*slot_a, *slot_b]
    types, keys = type_ids[None, :], key_mask[None, :]

    turned, context, spreads = attend(place, lengths, early, tokens, types, keys, table, after=ring.gather_late())
    pieces = early + ring.gather_last(context)
    layer_out, grad_first, grad_context, middle_sums, *parts = middle(
        place, pieces, tokens, types, context, cotangent, table
    )
    both, three = ring.reduction(parts[:4]), ring.reduction(parts[4:])
    three.across()
    both.across(after=three.give, cost=FAR_COST)
    mixed = attend_back(place, lengths, turned, grad_context, spreads, keys, after=both.give)
    three.side(after=[mixed])
    parts = mixed_grad(place, early, mixed, tokens, types, table, middle_sums, after=three.give)
    zero = ring.reduction(parts, after=three.last())
    zero.across()
    both.side(after=zero.give)
    input_grad = input_back(place, early, mixed, grad_first, after=both.give)
    give = ring.reduce_far(both, after=[input_grad])
    zero.side(after=[input_grad])
    ring.reduce_near(zero, three)
    base, last, owned_vector = ring.reduce_last()
    grad_t, left_new, right_new, master_t, slow_t, low_t = owner_step(
        base, last, left_stats, right_stats, left_root, right_root, master.T, slow_weights.T
    )
    owned_grad, master_new, slow_new, weights_new = grad_t.T, master_t.T, slow_t.T, low_t.T
    moment_new = stat_decay * vector_moment + (1.0 - stat_decay) * owned_vector * owned_vector
    vector_master_new = vector_master - vector_rate * owned_vector / (jnp.sqrt(moment_new) + 1e-08)
    slow_vectors_new = slow_decay * slow_vectors + (1.0 - slow_decay) * vector_master_new
    vectors_new = vector_master_new.astype(bf16)
    return (
        layer_out,
        input_grad,
        owned_grad,
        left_new,
        right_new,
        master_new,
        slow_new,
        weights_new,
        owned_vector,
        moment_new,
        vector_master_new,
        slow_vectors_new,
        vectors_new,
    )


def solution(mesh):
    in_specs = (
        P(("dp", "opt"), None),
        P(("dp", "opt"), None),
        P(("dp", "opt")),
        P(("dp", "opt")),
        P(("dp", "opt")),
        P(None, "dp"),
        P("dp"),
        P(None, ("dp", "opt")),
        P(None, ("dp", "opt")),
        P(("dp", "opt"), None),
        P(("dp", "opt"), None),
        P(("dp", "opt"), None),
        P(("dp", "opt"), None),
        P(("dp", "opt")),
        P(("dp", "opt")),
        P(("dp", "opt")),
    )
    out_specs = (
        P(("dp", "opt"), None),
        P(("dp", "opt"), None),
        P(None, ("dp", "opt")),
        P(("dp", "opt"), None),
        P(("dp", "opt"), None),
        P(None, ("dp", "opt")),
        P(None, ("dp", "opt")),
        P(None, ("dp", "opt")),
        P(("dp", "opt")),
        P(("dp", "opt")),
        P(("dp", "opt")),
        P(("dp", "opt")),
        P(("dp", "opt")),
    )
    ring = Ring if dict(mesh.shape) == {"dp": 16, "opt": 2} else Plain
    return jax.shard_map(
        functools.partial(per_device, ring),
        mesh=mesh,
        in_specs=in_specs,
        out_specs=out_specs,
        check_vma=False,
    )
```

```python
import functools
import math

import jax
import jax.numpy as jnp
import numpy as np
from jax import lax
from jax.experimental import pallas as pl
from jax.experimental.pallas import tpu as pltpu
from jax.sharding import PartitionSpec as P

D = 768
H = 12
HD = 64
FF = 3072
WCOLS = 4 * D + 2 * FF
NVEC = 10 * D + FF

highest = lax.Precision.HIGHEST
norm_eps = 1e-12
learning_rate = 0.03
vector_rate = 0.2
stat_decay = 0.5
slow_decay = 0.9
f32 = jnp.float32
bf16 = jnp.bfloat16
AXES = ("dp", "opt")


def contract(left_side, right_side, left_dim, right_dim):
    return lax.dot_general(
        left_side, right_side, (((left_dim,), (right_dim,)), ((), ())), preferred_element_type=f32
    )


def block_index(z, y, c, x):
    return z * 8 + y * 4 + c * 2 + x


def permutation(move):
    pairs = []
    for b in range(32):
        z, y, c, x = b // 8, (b // 4) % 2, (b // 2) % 2, b % 2
        pairs.append((b, block_index(*move(z, y, c, x))))
    return pairs


Z_CYCLE = permutation(lambda z, y, c, x: ((2, 0, 3, 1)[z], y, c, x))
Z_CYCLE_BACK = permutation(lambda z, y, c, x: ((1, 3, 0, 2)[z], y, c, x))
Z_NEAR = permutation(lambda z, y, c, x: (z ^ 1, y, c, x))
Z_FAR = permutation(lambda z, y, c, x: (z ^ 2, y, c, x))
Z_MIDDLE = permutation(lambda z, y, c, x: ((0, 2, 1, 3)[z], y, c, x))
PLANE_A = permutation(lambda z, y, c, x: (z, 1 - y, c, x) if c == 0 else (z, y, c, 1 - x))
PLANE_B = permutation(lambda z, y, c, x: (z, y, c, 1 - x) if c == 0 else (z, 1 - y, c, x))
CORES = permutation(lambda z, y, c, x: (z, y, 1 - c, x))


def send(values, pairs):
    return lax.ppermute(values, AXES, pairs)


QUARTER_SLOT = np.array([[0, 1, 3, 2], [1, 0, 3, 2], [1, 3, 0, 2], [1, 3, 2, 0]])


FAR_COST = 40 * 10**9


class Ring:
    def __init__(self):
        dp = lax.axis_index("dp")
        self.z, self.y, self.c = dp // 4, (dp // 2) % 2, dp % 2
        self.x = lax.axis_index("opt")
        slots = [self.number([int(v) for v in QUARTER_SLOT[:, q]]) for q in range(4)]
        self.place = jnp.stack([self.y, self.c, self.x, self.z] + slots).astype(jnp.int32)

    def number(self, values):
        out = values[3]
        for z in (2, 1, 0):
            out = jnp.where(self.z == z, values[z], out)
        return out

    def gather_early(self, weights, vectors):
        place, rows = self.place, weights.shape[1] // 2
        own = prepare_own(place, weights.T, vectors[None, :])
        one = send(own, Z_CYCLE)
        side = send(own, PLANE_A)
        pass_on, slab, pair_a = after_one(place, own, one, side)
        two = send(pass_on, Z_NEAR)
        across_a = send(pair_a, PLANE_B)
        far = send(slab, Z_FAR)
        middle = send(own, Z_MIDDLE)
        swap_a = send(pair_a, CORES)
        block_b, slot_c = after_two(place, pass_on, one, two, far, after=[across_a, swap_a])
        side_b = send(block_b, PLANE_A)
        side_c = send(slot_c, PLANE_A)
        three = send(middle, Z_NEAR)
        swap_aa = send(across_a, CORES)
        pair_b, slot_d = after_three(place, block_b, side_b, middle, three, after=[side_c, swap_aa])
        across_b = send(pair_b, PLANE_B)
        swap_b = send(pair_b, CORES)
        side_d = send(slot_d, PLANE_A)
        self.late = after_four(slot_c, side_c, slot_d, side_d, after=[swap_b])
        swap_bb = send(across_b, CORES)
        slot_b = [pair_b, across_b, swap_b, swap_bb]
        table = read_vectors(place, slot_b, vectors.shape[0] // 2)
        return [pair_a, across_a, swap_a, swap_aa], slot_b, table.reshape(-1, D)

    def gather_late(self):
        self.across = send(self.late, PLANE_B)
        self.swapped = send(self.late, CORES)
        return [self.late]

    def gather_last(self, context):
        across = hold(self.across, context)
        return [self.late, across, self.swapped, send(across, CORES)]

    def reduction(self, pieces, after=()):
        return Reduction(pieces, after)

    def reduce_far(self, both, after=()):
        self.kept_far, give = far_sums(self.place, both.parts(), after)
        self.far = hold(send(give, Z_FAR), cost=FAR_COST)
        return [give]

    def reduce_near(self, zero, three, after=()):
        self.kept_near, give, self.kept_rows = near_sums(self.place, zero.parts(), three.parts(), after)
        self.near = send(give, Z_NEAR)

    def reduce_last(self):
        base, give, rows, packed = last_sums(
            self.place, self.kept_near, self.kept_far, self.kept_rows, self.near, self.far
        )
        last = send(give, Z_CYCLE_BACK)
        arrived = send(packed, Z_FAR).astype(f32)
        half = rows.shape[1]
        rows = rows + (arrived[:, :half] + arrived[:, half:])
        vector = lax.dynamic_index_in_dim(rows, self.z, 0, False)
        return base, last, vector[: NVEC // 32]


class Reduction:
    def __init__(self, pieces, after=()):
        self.keep_lo, self.keep_hi, give_lo, give_hi = pieces
        if after:
            give_hi = hold(give_hi, *after)
        self.got_hi = send(give_hi, CORES)
        self.got_lo = send(give_lo, CORES)
        self.more = []

    def across(self, after=(), cost=0):
        self.give = [add_pieces([self.keep_hi, self.got_hi], 0, 2, after)]
        got = send(*self.give, PLANE_B)
        self.more.append(hold(got, cost=cost) if cost else got)

    def side(self, after=()):
        self.give = [add_pieces(self.parts(), 1, 1, after)]
        self.more.append(send(*self.give, PLANE_A))

    def parts(self):
        return [self.keep_lo, self.got_lo, *self.more]

    def first(self):
        return [self.got_hi]

    def last(self):
        return self.more[-1:]


class Plain:
    def __init__(self):
        self.place = jnp.asarray(np.array([0, 0, 0, 0, 0, 1, 2, 3]), jnp.int32)

    def gather_early(self, weights, vectors):
        turned = lax.all_gather(weights, "dp", axis=1, tiled=True).T
        blocks = turned.reshape(4, 8, -1, D)
        self.mine, self.theirs = (blocks[:, np.array(k)] for k in ([0, 4, 1, 5], [2, 3, 6, 7]))
        entries = vectors.shape[0]
        tiles = -(-entries // 2048)
        padded = jnp.pad(vectors, (0, tiles * 2048 - entries)).reshape(tiles * 16, 128)
        gathered = lax.all_gather(padded, "dp", axis=0, tiled=True)
        gathered = gathered.reshape(-1, tiles * 2048)[:, :entries].reshape(-1, D).astype(f32)
        slots = [[jnp.pad(v, ((0, 0), (0, 16), (0, 0))) for v in self.halves(q)] for q in (0, 1)]
        return *slots, gathered

    def halves(self, q):
        return [self.mine[q, :2], self.mine[q, 2:], self.theirs[q, :2], self.theirs[q, 2:]]

    def gather_late(self):
        return []

    def gather_last(self, context):
        return [jnp.stack(both, axis=1) for both in zip(self.halves(2), self.halves(3))]

    def reduction(self, pieces, after=()):
        return PlainReduction(pieces)

    def reduce_far(self, both, after=()):
        self.both = both
        return []

    def reduce_near(self, zero, three, after=()):
        self.zero, self.three = zero, three

    def reduce_last(self):
        zero = self.zero.whole()
        block = Q // 8
        packed = zero[0, :, block:, :].astype(f32)
        rows = packed[..., : D // 2] + packed[..., D // 2 :]
        vectors = jnp.swapaxes(rows[:, :4, : NVEC // 32], 0, 1).reshape(-1)
        vectors = lax.psum_scatter(vectors, AXES, scatter_dimension=0, tiled=True)
        sums = jnp.concatenate([zero[:, :, :block].reshape(-1, D), *(v.whole().reshape(-1, D) for v in (self.both, self.three))])
        owned = lax.psum_scatter(sums, AXES, scatter_dimension=0, tiled=True)
        return owned.astype(f32), jnp.zeros_like(owned), vectors


class PlainReduction:
    def __init__(self, pieces):
        self.pieces = jnp.concatenate(pieces)
        self.give = []

    def across(self, after=(), cost=0):
        pass

    def side(self, after=()):
        pass

    def first(self):
        return []

    def last(self):
        return []

    def whole(self):
        order = np.argsort(np.array([0, 4, 1, 5, 2, 3, 6, 7]))
        return jnp.swapaxes(self.pieces[order], 0, 1)


VMEM_LIMIT = 60 * 1024 * 1024
whole = pl.BlockSpec(memory_space=pltpu.VMEM)
scalars = pl.BlockSpec(memory_space=pltpu.SMEM)
anywhere = pl.BlockSpec(memory_space=pl.ANY)
shape = jax.ShapeDtypeStruct
CHUNK = 256
CHUNKS = FF // CHUNK
Q = 3 * D
SPAN = 256
TALL = 512
flag_shape = jax.ShapeDtypeStruct((8, 128), jnp.float32)
PART = 256


def call(kernel, outs, out_specs, scratch, flops, moved, *args, specs, name, after=(), limit=VMEM_LIMIT):
    count, skip = len(specs), len(after)

    def body(*refs):
        kernel(*refs[:count], *refs[count + skip :])

    return pl.pallas_call(
        body,
        out_shape=outs,
        in_specs=[*specs, *[anywhere] * skip],
        out_specs=out_specs,
        scratch_shapes=scratch,
        compiler_params=pltpu.CompilerParams(vmem_limit_bytes=limit),
        cost_estimate=pl.CostEstimate(flops=flops, bytes_accessed=moved, transcendentals=0),
        name=name,
    )(*args, *after)


def block_place(place, who, k):
    y, c, x = place[0], place[1], place[2]
    core = c if who == 0 else 1 - c
    first, second = k & 1, k >> 1
    to_y = jnp.where(core == 0, y ^ first, y ^ second)
    to_x = jnp.where(core == 0, x ^ second, x ^ first)
    return to_y * 4 + core * 2 + to_x


def block_rows(place, who, k, rows):
    return pl.ds(pl.multiple_of(block_place(place, who, k) * rows, math.gcd(rows, 16)), rows)


def begin(source, target, sem):
    copy = pltpu.make_async_copy(source, target, sem)
    copy.start()
    return copy


def slot_pieces(slots):
    return [
        [(refs[k // 2], (k % 2,) + ((slot - 2,) if slot > 1 else ())) for k in range(8)]
        for slot, refs in enumerate(slots)
    ]


def ingest(place, quarter, slots, into, sems):
    rows = into.shape[0] // 8
    targets = [into.at[block_rows(place, k // 4, k % 4, rows)] for k in range(8)]
    all_pieces = slot_pieces(slots)
    for slot, pieces in enumerate(all_pieces):

        @pl.when(place[4 + quarter] == slot)
        def _():
            for k, (ref, index) in enumerate(pieces):
                pltpu.make_async_copy(ref.at[(*index, pl.ds(0, rows))], targets[k], sems.at[k]).start()

    return [
        pltpu.make_async_copy(ref.at[(*index, pl.ds(0, rows))], targets[k], sems.at[k])
        for k, (ref, index) in enumerate(all_pieces[0])
    ]


def piece_of(place, at):
    y, c, x = place[0], place[1], place[2]
    core = (at >> 1) & 1
    flip_y, flip_x = (at >> 2) ^ y, (at & 1) ^ x
    first = jnp.where(core == 0, flip_y, flip_x)
    second = jnp.where(core == 0, flip_x, flip_y)
    return jnp.where(core == c, 0, 2) + second, first


def hand_block(place, source, at, targets, part, sem):
    rows = source.shape[0] // 8
    which, first = piece_of(place, at)
    for k, target in enumerate(targets):

        @pl.when(which == k)
        def _():
            pltpu.make_async_copy(source.at[rows_of(at, rows)], target.at[first, part, pl.ds(0, rows)], sem).start()


def hand_rows(place, source, at, targets, sem):
    count = source.shape[1]
    which, first = piece_of(place, at)
    for k, target in enumerate(targets):

        @pl.when(which == k)
        def _():
            there = target.at[first, 0, pl.ds(target.shape[2] - count, count)]
            pltpu.make_async_copy(source.at[at], there, sem).start()


def pack_rows(values):
    return jnp.concatenate(twice(values), axis=1)


def unpack_rows(packed):
    half = packed.shape[1] // 2
    wide = packed.astype(f32)
    return wide[:, :half] + wide[:, half:]


def hand_wait(source, targets, part, sems):
    rows = source.shape[0] // 8
    for k in range(8):
        pltpu.make_async_copy(source.at[pl.ds(0, rows)], targets[0].at[0, part, pl.ds(0, rows)], sems.at[k]).wait()


def finish(*copies):
    for copy in copies:
        if isinstance(copy, (list, tuple)):
            finish(*copy)
        else:
            copy.wait()


def rows_of(i, step):
    return pl.ds(pl.multiple_of(i * step, math.gcd(step, 256)), step)


def loop(count, body):
    def step(i, carry):
        body(i)
        return carry

    lax.fori_loop(0, count, step, 0)


def column(row, width):
    return jnp.broadcast_to(row, (width, row.shape[1])).T


def is_region(types):
    return column((types == 1).astype(f32), 128)[:, 0:1] > 0.5


def allowed_keys(lengths, keys, s):
    slot = lax.broadcasted_iota(jnp.int32, (1, SPAN), 1)
    allowed = (slot < lengths[s]) & ((keys[:, rows_of(s, SPAN)] == 1) | (slot == 0))
    return jnp.where(allowed, 3e38, -1e30)


def embed(tokens, types, table):
    return tokens.astype(f32) + jnp.where(is_region(types), table[1:2, :], table[0:1, :])


def attend_kernel(
    place, lengths, a0, a1, a2, a3, b0, b1, b2, b3, tokens_in, types, keys, table,
    turned_out, context_out, spreads,
    weights, low, turned, context_turned, context, mask, tokens, sems, more,
):
    arrived = begin(tokens_in, tokens, sems.at[9])
    copies = ingest(place, 0, ((a0, a1, a2, a3), (b0, b1, b2, b3)), weights, sems)
    rows = tokens.shape[0]

    def prepare(i):
        here = rows_of(i, PART)
        low[here, :] = embed(tokens[here, :], types[:, here], table[...]).astype(bf16)
        mask[here, :] = column(allowed_keys(lengths, keys, i), SPAN)

    finish(arrived)
    loop(rows // PART, prepare)
    finish(copies)
    step = 384

    def project(i):
        here = rows_of(i, step)
        half = rows_of(i % 2, step)
        bias = jnp.where(i // 2 == 0, table[4:5, half], jnp.where(i // 2 == 2, table[5:6, half], 0.0))
        made = contract(weights[here, :], low[...], 1, 1) + column(bias, 128)[:, 0:1]
        made = made * jnp.where(i < D // step, HD ** (-0.5), 1.0)
        turned[here, :] = made.astype(bf16)

    loop(Q // step, project)
    sent = begin(turned, turned_out, sems.at[8])


    def sequence(s):
        cols = rows_of(s, SPAN)
        scores = [
            contract(turned[D + h * HD : D + (h + 1) * HD, cols], turned[h * HD : (h + 1) * HD, cols], 0, 0)
            for h in range(H)
        ]
        probs = []
        for h, score in enumerate(scores):
            score = jnp.minimum(score, mask[cols, :])
            peak = jnp.max(score, axis=0, keepdims=True)
            powers = jnp.exp(score - peak)
            total = jnp.sum(powers, axis=0, keepdims=True)
            probs.append((powers * (1.0 / total)).astype(bf16))
            spreads[h : h + 1, cols] = peak + jnp.log(total)
        for h, prob in enumerate(probs):
            value = turned[2 * D + h * HD : 2 * D + (h + 1) * HD, cols]
            context_turned[h * HD : (h + 1) * HD, :] = contract(value, prob, 1, 0).astype(bf16)
        context[cols, :] = context_turned[...].T
        pltpu.make_async_copy(context.at[cols], context_out.at[cols], more.at[s]).start()

    loop(rows // SPAN, sequence)
    for s in range(rows // SPAN):
        cols = pl.ds(s * SPAN, SPAN)
        pltpu.make_async_copy(context.at[cols], context_out.at[cols], more.at[s]).wait()
    finish(sent)


def attend(place, lengths, pieces, tokens, types, keys, table, after=()):
    rows = tokens.shape[0]
    return call(
        attend_kernel,
        [shape((Q, rows), bf16), shape((rows, D), bf16), shape((H, rows), f32)],
        [anywhere, anywhere, whole],
        [
            pltpu.VMEM((Q, D), bf16),
            pltpu.VMEM((rows, D), bf16),
            pltpu.VMEM((Q, rows), bf16),
            pltpu.VMEM((D, SPAN), bf16),
            pltpu.VMEM((rows, D), bf16),
            pltpu.VMEM((rows, SPAN), f32),
            pltpu.VMEM((rows, D), bf16),
            pltpu.SemaphoreType.DMA((10,)),
            pltpu.SemaphoreType.DMA((rows // SPAN,)),
        ],
        2 * rows * Q * D + 4 * rows * 256 * D,
        20 << 20,
        place, lengths, *pieces, tokens, types, keys, table,
        specs=[scalars] * 2 + [anywhere] * 9 + [whole] * 3,
        name="attend",
        after=after,
    )


def normalise(inputs):
    centre = jnp.mean(inputs, axis=-1, keepdims=True)
    offset = inputs - centre
    spread = lax.rsqrt(jnp.mean(offset * offset, axis=-1, keepdims=True) + norm_eps)
    return offset * spread, spread


def normalise_back(scaled, unit, spread):
    return spread * (
        scaled
        - jnp.mean(scaled, axis=-1, keepdims=True)
        - unit * jnp.mean(scaled * unit, axis=-1, keepdims=True)
    )


def gelu_both(v):
    cumulative = 0.5 * (1.0 + lax.erf(v * math.sqrt(0.5)))
    density = jnp.exp(-0.5 * v * v) * (1.0 / math.sqrt(2.0 * math.pi))
    return v * cumulative, cumulative + v * density


def weight_chunk(weights, offset, i):
    return weights[pl.ds(pl.multiple_of(offset + i * CHUNK, CHUNK), CHUNK), :]


def row_sums(count, body, sums, rows):
    zero = jnp.zeros((8, D), f32)

    def step(i, carry):
        made = body(i)
        return tuple(
            have + jnp.sum(more.reshape(-1, 8, D), axis=0) for have, more in zip(carry, made)
        )

    made = lax.fori_loop(0, count, step, (zero,) * len(rows))
    for have, row in zip(made, rows):
        sums[row : row + 1, 0:D] = jnp.sum(have, axis=0, keepdims=True)


STEP = 768


def middle_kernel(
    place, a0, a1, a2, a3, b0, b1, b2, b3, c0, c1, c2, c3, tokens_in, context_in, cotangent_in, types, table,
    layer_out_to, grad_first_to, grad_context_to, sums,
    keep_lo, keep_hi, give_lo, give_hi, keep_lo3, keep_hi3, give_lo3, give_hi3,
    weights, pre_a, pre_b, total, tokens, context, cotangent, layer_out, active, slope, unit_one, spread_one, normed_low,
    grad_context, down_made, sems, more,
):
    rows = tokens.shape[0]
    slots = ((a0, a1, a2, a3), (b0, b1, b2, b3), (c0, c1, c2, c3), (c0, c1, c2, c3))
    early = [begin(context_in, context, more.at[0]), begin(tokens_in, tokens, more.at[1])]
    batches = [ingest(place, 1, slots, weights.at[pl.ds(0, Q)], sems.at[0])]
    up, down = D, D + FF
    finish(early, batches[0])
    batches.append(ingest(place, 2, slots, weights.at[pl.ds(Q, Q)], sems.at[1]))
    batches.append(ingest(place, 3, slots, weights.at[pl.ds(2 * Q, Q)], sems.at[2]))
    late = begin(cotangent_in, cotangent, more.at[2])

    def branch(i):
        here = rows_of(i, SPAN)
        total[here, :] = contract(context[here, :], weights[0:D, :], 1, 1)

    loop(rows // SPAN, branch)

    def first(i):
        here = rows_of(i, PART)
        unit, spread = normalise(embed(tokens[here, :], types[:, here], table[...]) + (total[here, :] + table[6:7, :]))
        unit_one[here, :] = unit
        spread_one[here, :] = jnp.broadcast_to(spread, (PART, 128))
        normed_low[here, :] = (unit * table[2:3, :] + table[3:4, :]).astype(bf16)

    loop(rows // PART, first)
    sent = []
    targets = (keep_lo, keep_hi, give_lo, give_hi)
    targets3 = (keep_lo3, keep_hi3, give_lo3, give_hi3)
    finish(batches[1])

    def gelu(pre, i, here):
        bias = table[pl.ds(10 + i // (D // CHUNK), 1), rows_of(i % (D // CHUNK), CHUNK)]
        return gelu_both(pre[here, :] + bias)

    def keep_gelu(made, i, here):
        cols = rows_of(i, CHUNK)
        active[here, cols] = made[0].astype(bf16)
        slope[here, cols] = made[1]

    everything = slice(None)

    def forward(t):
        before = jnp.maximum(2 * t - 1, 0)
        both = gelu(pre_b, before, everything)
        pre_a[...] = contract(normed_low[...], weight_chunk(weights, up, 2 * t), 1, 1)
        keep_gelu(both, before, everything)
        both = gelu(pre_a, 2 * t, everything)
        pre_b[...] = contract(normed_low[...], weight_chunk(weights, up, 2 * t + 1), 1, 1)
        keep_gelu(both, 2 * t, everything)

    loop(CHUNKS // 2, forward)

    def forward_end(i):
        here = rows_of(i, PART)
        keep_gelu(gelu(pre_b, CHUNKS - 1, here), CHUNKS - 1, here)

    loop(rows // PART, forward_end)
    finish(batches[2])

    def add_down(i):
        here = rows_of(i, TALL)
        total[here, :] = contract(active[here, :], weights[down : down + FF, :], 1, 0)

    loop(rows // TALL, add_down)
    finish(late)

    def second(i):
        here = rows_of(i, PART)
        normed_one = unit_one[here, :] * table[2:3, :] + table[3:4, :]
        unit, spread = normalise(normed_one + (total[here, :] + table[9:10, :]))
        layer_out[here, :] = (unit * table[7:8, :] + table[8:9, :]).astype(bf16)
        upstream = cotangent[here, :].astype(f32)
        grad = normalise_back(upstream * table[7:8, :], unit, spread)
        total[here, :] = grad
        low = grad.astype(bf16)
        tokens[here, :] = low
        return upstream * unit, upstream, low.astype(f32)

    row_sums(rows // PART, second, sums, (7, 8, 9))
    sent.append(begin(layer_out, layer_out_to, more.at[5]))

    def weigh_down(i):
        here = rows_of(i, STEP)
        down_made[here, :] = contract(active[:, here], tokens[...], 0, 0).astype(bf16)

    loop(FF // STEP, weigh_down)
    third_quarter = down_made.at[pl.ds(D, Q)]
    loop(8, lambda p: hand_block(place, third_quarter, p, targets3, 0, sems.at[2, p]))

    def through(pre, i, here):
        return (pre[here, :] * slope[here, rows_of(i, CHUNK)]).astype(bf16)

    def backward(t):
        before = jnp.maximum(2 * t - 1, 0)
        low = through(pre_b, before, everything)
        pre_a[...] = contract(tokens[...], weight_chunk(weights, down, 2 * t), 1, 1)
        active[:, rows_of(before, CHUNK)] = low
        low = through(pre_a, 2 * t, everything)
        pre_b[...] = contract(tokens[...], weight_chunk(weights, down, 2 * t + 1), 1, 1)
        active[:, rows_of(2 * t, CHUNK)] = low

    loop(CHUNKS // 2, backward)

    def backward_end(i):
        here = rows_of(i, PART)
        active[here, rows_of(CHUNKS - 1, CHUNK)] = through(pre_b, CHUNKS - 1, here)

    loop(rows // PART, backward_end)

    def add_up(i):
        here = rows_of(i, TALL)
        total[here, :] += contract(active[here, :], weights[up : up + FF, :], 1, 0)

    loop(rows // TALL, add_up)

    def third(i):
        here = rows_of(i, PART)
        upstream = total[here, :]
        unit = unit_one[here, :]
        grad = normalise_back(upstream * table[2:3, :], unit, spread_one[here, 0:1])
        total[here, :] = grad
        low = grad.astype(bf16)
        cotangent[here, :] = low
        of_one = is_region(types[:, here])
        return upstream * unit, upstream, low.astype(f32), jnp.where(of_one, 0.0, grad), jnp.where(of_one, grad, 0.0)

    row_sums(rows // PART, third, sums, (2, 3, 6, 0, 1))
    sent.append(begin(total, grad_first_to, more.at[8]))

    def through_out(i):
        here = rows_of(i, SPAN)
        grad_context[:, here] = contract(cotangent[here, :], weights[0:D, :], 1, 0).T.astype(bf16)

    loop(rows // SPAN, through_out)
    sent.append(begin(grad_context, grad_context_to, more.at[10]))
    moved = begin(down_made.at[pl.ds(0, D)], weights.at[pl.ds(D + FF, D)], more.at[9])

    def weigh_up(i):
        here = rows_of(i, STEP)
        rows_there = pl.ds(pl.multiple_of(D + i * STEP, 256), STEP)
        weights[rows_there, :] = contract(active[:, here], normed_low[...], 0, 0).astype(bf16)
        added = jnp.sum(active[:, here].astype(f32), 0, keepdims=True)
        sums[pl.ds(10, 1), here] = added

    half = FF // STEP // 2
    loop(half, lambda i: weigh_up(half + i))
    finish(moved)
    hand_wait(third_quarter, targets3, 0, sems.at[2])
    quarters = weights.at[pl.ds(0, Q)], weights.at[pl.ds(Q, Q)]
    loop(8, lambda p: hand_block(place, quarters[1], p, targets, 1, sems.at[1, p]))

    def weigh_out(i):
        here = rows_of(i, 384)
        weights[here, :] = contract(cotangent[:, here], context[...], 0, 0).astype(bf16)

    def hand_one(p):
        hand_block(place, quarters[0], p, targets, 0, sems.at[0, p])

    def weigh_and_hand(i):
        weigh_up(i)
        loop(3, lambda p: hand_one(2 + 3 * i + p))

    loop(2, weigh_out)
    loop(2, hand_one)
    loop(half, weigh_and_hand)
    hand_wait(quarters[1], targets, 1, sems.at[1])
    hand_wait(quarters[0], targets, 0, sems.at[0])
    finish(sent)


def middle(place, pieces, tokens, types, context, cotangent, table, after=()):
    rows = tokens.shape[0]
    tall = pltpu.VMEM((rows, D), bf16)
    return call(
        middle_kernel,
        [shape((rows, D), bf16), shape((rows, D), f32), shape((D, rows), bf16), shape((11, FF), f32)]
        + [shape((2, 2, Q // 8, D), bf16)] * 4
        + [shape((2, 1, Q // 8, D), bf16)] * 4,
        [anywhere] * 3 + [whole] + [anywhere] * 8,
        [
            pltpu.VMEM((3 * Q, D), bf16),
            pltpu.VMEM((rows, CHUNK), f32),
            pltpu.VMEM((rows, CHUNK), f32),
            pltpu.VMEM((rows, D), f32),
            tall,
            tall,
            tall,
            tall,
            pltpu.VMEM((rows, FF), bf16),
            pltpu.VMEM((rows, FF), f32),
            pltpu.VMEM((rows, D), f32),
            pltpu.VMEM((rows, 128), f32),
            tall,
            pltpu.VMEM((D, rows), bf16),
            pltpu.VMEM((FF, D), bf16),
            pltpu.SemaphoreType.DMA((3, 8)),
            pltpu.SemaphoreType.DMA((11,)),
        ],
        6 * rows * 3 * Q * D,
        60 << 20,
        place, *pieces, tokens, context, cotangent, types, table,
        specs=[scalars] + [anywhere] * 15 + [whole] * 2,
        name="middle",
        after=after,
    )


def attend_back_kernel(
    place, lengths, turned, grad_context, spreads, keys,
    mixed_to,
    mixed, mask, sems,
):
    rows = turned.shape[1]

    def prepare(i):
        here = rows_of(i, PART)
        mask[here, :] = column(allowed_keys(lengths, keys, i), SPAN)

    loop(rows // PART, prepare)

    together = 6

    def units(i):
        places = []
        for j in range(together):
            u = i * together + j
            places.append((u % H, pl.multiple_of((u % H) * HD, HD), rows_of(u // H, SPAN)))
        query = [turned[pl.ds(at, HD), cols] for _, at, cols in places]
        key = [turned[pl.ds(D + at, HD), cols] for _, at, cols in places]
        grad = [grad_context[pl.ds(at, HD), cols] for _, at, cols in places]
        scores = [contract(k, q, 0, 0) for k, q in zip(key, query)]
        grad_probs = [
            contract(turned[pl.ds(2 * D + at, HD), cols], g, 0, 0) for (_, at, cols), g in zip(places, grad)
        ]
        made = []
        for (h, at, cols), score, grad_prob in zip(places, scores, grad_probs):
            probs = jnp.exp(jnp.minimum(score, mask[cols, :]) - spreads[pl.ds(h, 1), cols])
            inner = jnp.sum(probs * grad_prob, axis=0, keepdims=True)
            made.append(((probs * (grad_prob - inner)).astype(bf16), probs.astype(bf16)))
        for (h, at, cols), q, k, g, (grad_score, prob) in zip(places, query, key, grad, made):
            mixed[pl.ds(at, HD), cols] = (contract(k, grad_score, 1, 0) * HD ** (-0.5)).astype(bf16)
            mixed[pl.ds(D + at, HD), cols] = contract(q, grad_score, 1, 1).astype(bf16)
            mixed[pl.ds(2 * D + at, HD), cols] = contract(g, prob, 1, 1).astype(bf16)

    loop(H * (rows // SPAN) // together, units)
    finish(begin(mixed, mixed_to, sems.at[0]))


def attend_back(place, lengths, turned, grad_context, spreads, keys, after=()):
    rows = turned.shape[1]
    return call(
        attend_back_kernel,
        [shape((Q, rows), bf16)],
        [anywhere],
        [
            pltpu.VMEM((Q, rows), bf16),
            pltpu.VMEM((rows, SPAN), f32),
            pltpu.SemaphoreType.DMA((1,)),
        ],
        10 * rows * 256 * D,
        25 << 20,
        place, lengths, turned, grad_context, spreads, keys,
        specs=[scalars] * 2 + [whole] * 4,
        limit=36 * 1024 * 1024,
        name="attend_back",
        after=after,
    )[0]


def mixed_grad_kernel(
    place, a0, a1, a2, a3, b0, b1, b2, b3, mixed_in, tokens, types, table, middle_sums,
    keep_lo, keep_hi, give_lo, give_hi,
    low, mixed, made, weights, by_type, sums, wide, packed, sems, more, others,
):
    step = 384
    for i in range(Q // step):
        here = pl.ds(i * step, step)
        begin(mixed_in.at[here], mixed.at[here], more.at[i])
    copies = ingest(place, 0, ((a0, a1, a2, a3), (b0, b1, b2, b3)), weights, sems)
    rows = tokens.shape[0]
    targets = (keep_lo, keep_hi, give_lo, give_hi)

    def prepare(i):
        here = rows_of(i, PART)
        low[here, :] = embed(tokens[here, :], types[:, here], table[...]).astype(bf16)

    loop(rows // PART, prepare)
    type_row = lax.broadcasted_iota(jnp.int32, (8, rows), 0)
    one_hot = (type_row == types[...]).astype(f32).astype(bf16)

    def weigh(i):
        here = rows_of(i, step)
        pltpu.make_async_copy(mixed_in.at[here], mixed.at[here], more.at[i]).wait()
        made[here, :] = contract(mixed[here, :], low[...], 1, 0).astype(bf16)
        by_type[:, here] = contract(one_hot, mixed[here, :], 1, 1)

    loop(Q // step, weigh)
    finish(copies)
    loop(8, lambda p: hand_block(place, made, p, targets, 0, sems.at[p]))
    high, rest = twice(by_type[...])
    through = contract(high, weights[...], 1, 0) + contract(rest, weights[...], 1, 0)
    sums[0:10, :] = middle_sums[0:10, 0:D]
    sums[0:2, :] = middle_sums[0:2, 0:D] + through[0:2, :]
    for row, start in ((4, 0), (5, 2 * D)):
        sums[row : row + 1, :] = by_type[0:1, start : start + D] + by_type[1:2, start : start + D]
    for i in range(FF // D):
        sums[10 + i : 11 + i, :] = middle_sums[10:11, i * D : (i + 1) * D]
    wide[...] = jnp.zeros_like(wide)
    entries = NVEC // 32
    for block in range(8):
        for z in range(4):
            row, lane = divmod((z * 8 + block) * entries, D)
            taken = min(entries, D - lane)
            wide[block, z : z + 1, 0:taken] = sums[row : row + 1, lane : lane + taken]
            if taken < entries:
                wide[block, z : z + 1, taken:entries] = sums[row + 1 : row + 2, 0 : entries - taken]
        packed[block] = pack_rows(wide[block])

    loop(8, lambda p: hand_rows(place, packed, p, targets, others.at[p]))
    hand_wait(made, targets, 0, sems)
    for p in range(8):
        pltpu.make_async_copy(packed.at[p], keep_lo.at[0, 0, pl.ds(Q // 8, 16)], others.at[p]).wait()


def mixed_grad(place, pieces, mixed, tokens, types, table, middle_sums, after=()):
    rows = tokens.shape[0]
    return call(
        mixed_grad_kernel,
        [shape((2, 1, Q // 8 + 16, D), bf16)] * 4,
        [anywhere] * 4,
        [
            pltpu.VMEM((rows, D), bf16),
            pltpu.VMEM((Q, rows), bf16),
            pltpu.VMEM((Q, D), bf16),
            pltpu.VMEM((Q, D), bf16),
            pltpu.VMEM((8, Q), f32),
            pltpu.VMEM((16, D), f32),
            pltpu.VMEM((8, 16, D // 2), f32),
            pltpu.VMEM((8, 16, D), bf16),
            pltpu.SemaphoreType.DMA((8,)),
            pltpu.SemaphoreType.DMA((6,)),
            pltpu.SemaphoreType.DMA((8,)),
        ],
        2 * rows * Q * D,
        12 << 20,
        place, *pieces, mixed, tokens, types, table, middle_sums,
        specs=[scalars] + [anywhere] * 9 + [whole] * 4,
        name="mixed_grad",
        after=after,
    )


def input_kernel(place, a0, a1, a2, a3, b0, b1, b2, b3, mixed, grad_first, input_grad_to, flag, weights, made, sems):
    flag[...] = jnp.zeros_like(flag)
    finish(ingest(place, 0, ((a0, a1, a2, a3), (b0, b1, b2, b3)), weights, sems))
    rows = grad_first.shape[0]

    def through(i):
        here = rows_of(i, SPAN)
        made[here, :] = grad_first[here, :] + contract(mixed[:, here], weights[...], 0, 0)
        begin(made.at[here], input_grad_to.at[here], sems.at[i])

    loop(rows // SPAN, through)
    for i in range(rows // SPAN):
        here = pl.ds(i * SPAN, SPAN)
        pltpu.make_async_copy(made.at[here], input_grad_to.at[here], sems.at[i]).wait()


def input_back(place, pieces, mixed, grad_first, after=()):
    rows = grad_first.shape[0]
    return call(
        input_kernel,
        [shape((rows, D), f32), flag_shape],
        [anywhere, whole],
        [pltpu.VMEM((Q, D), bf16), pltpu.VMEM((rows, D), f32), pltpu.SemaphoreType.DMA((8,))],
        0,
        0,
        place, *pieces, mixed, grad_first,
        specs=[scalars] + [anywhere] * 8 + [whole] * 2,
        name="input_back",
        after=after,
    )


SMALL_LIMIT = 16 * 1024 * 1024


def small(kernel, outs, *args, name, after=(), scratch=(), specs=None, out_specs=None):
    specs = specs or [scalars if a.dtype == jnp.int32 else whole for a in args]
    many = isinstance(outs, (list, tuple))
    return call(
        kernel, outs, out_specs or ([whole] * len(outs) if many else whole), list(scratch), 0, 0, *args,
        specs=specs, name=name, after=after, limit=SMALL_LIMIT,
    )


def hold(values, *after, cost=0):
    skip = len(after)
    return pl.pallas_call(
        lambda *refs: None,
        out_shape=shape(values.shape, values.dtype),
        in_specs=[anywhere] * (1 + skip),
        out_specs=anywhere,
        input_output_aliases={0: 0},
        cost_estimate=pl.CostEstimate(flops=cost, bytes_accessed=0, transcendentals=0),
        name="hold",
    )(values, *after)


def prepare_kernel(place, turned, few, own, sem):
    rows = own.shape[0] - 16
    copy = begin(turned.at[pl.ds(pl.multiple_of(place[2] * rows, 16), rows)], own.at[pl.ds(0, rows)], sem)
    entries = few.shape[1] // 2
    row = few[...].astype(f32)
    row = jnp.where(place[2] == 0, row[:, :entries], row[:, entries:])
    here = lax.broadcasted_iota(jnp.int32, (16, entries), 0) == place[3]
    own[rows:, :] = jnp.zeros((16, D), bf16)
    own[rows:, 0:entries] = jnp.where(here, row, 0.0).astype(bf16)
    finish(copy)


def prepare_own(place, turned, few):
    return small(
        prepare_kernel, shape((turned.shape[0] // 2 + 16, D), bf16), place, turned, few,
        name="prepare_own", scratch=[pltpu.SemaphoreType.DMA], specs=[scalars, anywhere, whole],
    )


def by_plane(place, table, choices):
    out = choices[table[3]]
    for z in (2, 1, 0):
        out = jnp.where(place[3] == z, choices[table[z]], out)
    return out


def merge(old, new):
    old, new = old.astype(f32), new.astype(f32)
    return jnp.where(old == 0.0, new, old).astype(bf16)


def after_one_kernel(place, own, one, side, pass_on, slab, pair):
    rows = own.shape[0] - 16
    pass_on[:rows, :] = by_plane(place, (0, 1, 1, 0), (own[:rows, :], one[:rows, :]))
    merged = merge(own[rows:, :], one[rows:, :])
    pass_on[rows:, :] = merged
    slab[...] = merged
    pair[0] = own[...]
    pair[1] = side[...]


def after_one(place, own, one, side):
    outs = [shape(own.shape, bf16), shape((16, D), bf16), shape((2, *own.shape), bf16)]
    return small(after_one_kernel, outs, place, own, one, side, name="after_one")


def after_two_kernel(place, pass_on, one, two, far, block, slot):
    rows = one.shape[0] - 16
    block[:rows, :] = by_plane(place, (0, 1, 0, 1), (one[:rows, :], two[:rows, :]))
    block[rows:, :] = merge(merge(pass_on[rows:, :], two[rows:, :]), far[...])
    slot[...] = by_plane(place, (1, 0, 1, 0), (one[:rows, :], two[:rows, :]))


def after_two(place, pass_on, one, two, far, after):
    outs = [shape(one.shape, bf16), shape((one.shape[0] - 16, D), bf16)]
    return small(after_two_kernel, outs, place, pass_on, one, two, far, name="after_two", after=after)


def after_three_kernel(place, block, side, middle, three, pair, slot):
    rows = slot.shape[0]
    pair[0] = block[...]
    pair[1] = side[...]
    slot[...] = by_plane(place, (1, 0, 0, 1), (middle[:rows, :], three[:rows, :]))


def after_three(place, block, side, middle, three, after):
    outs = [shape((2, *block.shape), bf16), shape((block.shape[0] - 16, D), bf16)]
    return small(after_three_kernel, outs, place, block, side, middle, three, name="after_three", after=after)


def after_four_kernel(slot_c, side_c, slot_d, side_d, late):
    late[0, 0], late[0, 1] = slot_c[...], slot_d[...]
    late[1, 0], late[1, 1] = side_c[...], side_d[...]


def after_four(slot_c, side_c, slot_d, side_d, after):
    outs = shape((2, 2, *slot_c.shape), bf16)
    return small(after_four_kernel, outs, slot_c, side_c, slot_d, side_d, name="after_four", after=after)


def read_vectors_kernel(entries, place, a, b, c, d, out, got, sems):
    rows = a.shape[1] - 16
    refs = (a, b, c, d)
    finish([begin(refs[k // 2].at[k % 2, pl.ds(rows, 16)], got.at[k], sems.at[k]) for k in range(8)])
    for k in range(8):
        at = block_place(place, k // 4, k % 4)
        slab = got[k].astype(f32)
        for z in range(4):
            out[pl.ds(z * 8 + at, 1), :] = slab[z : z + 1, 0:entries]


def read_vectors(place, pieces, entries):
    return small(
        functools.partial(read_vectors_kernel, entries), shape((32, entries), f32), place, *pieces,
        name="read_vectors", specs=[scalars] + [anywhere] * 4,
        scratch=[pltpu.VMEM((8, 16, D), bf16), pltpu.SemaphoreType.DMA((8,))],
    )


def picked(kernel, outs, specs, args, name, after=()):
    count, skip = len(specs), len(after)

    def body(*refs):
        kernel(*refs[:count], *refs[count + skip :])

    return pl.pallas_call(
        body,
        grid=(1,),
        out_shape=outs,
        in_specs=[*specs, *[anywhere] * skip],
        out_specs=[pl.BlockSpec(o.shape, lambda i, n=len(o.shape): (0,) * n) for o in outs],
        compiler_params=pltpu.CompilerParams(vmem_limit_bytes=SMALL_LIMIT),
        cost_estimate=pl.CostEstimate(flops=0, bytes_accessed=0, transcendentals=0),
        name=name,
    )(*args, *after)


ADD_ROWS = 96


def add_pieces_kernel(*refs):
    count, n, rows, _ = refs[0].shape
    block = rows // ADD_ROWS * ADD_ROWS
    for a in range(count):
        for b in range(n):

            def step(i):
                here = rows_of(i, ADD_ROWS)
                total = refs[0][a, b, here, :].astype(f32)
                for ref in refs[1:-1]:
                    total = total + ref[a, b, here, :].astype(f32)
                refs[-1][a, b, here, :] = total.astype(bf16)

            loop(block // ADD_ROWS, step)
            if rows > block:
                refs[-1][a, b, block:, :] = pack_rows(sum(unpack_rows(ref[a, b, block:, :]) for ref in refs[:-1]))


def add_pieces(parts, first, count, after=()):
    _, n, rows, width = parts[0].shape
    block = (count, n, rows, width)
    return picked(
        add_pieces_kernel,
        [shape(block, bf16)],
        [pl.BlockSpec(block, lambda i: (first // count, 0, 0, 0))] * len(parts),
        parts,
        "add_pieces",
        after,
    )[0]


def piece_spec(part, j):
    return pl.BlockSpec((1, 1, *part.shape[2:]), lambda i: (0, j, 0, 0))


def sum_of(refs, here):
    total = refs[0][0, 0, here, :].astype(f32)
    for ref in refs[1:]:
        total = total + ref[0, 0, here, :].astype(f32)
    return total


def two_sums_kernel(table, keep_table, place, *refs):
    keep, give = refs[8], refs[9]
    block = keep.shape[0]

    def step(i):
        here = rows_of(i, ADD_ROWS)
        sums = sum_of(refs[:4], here), sum_of(refs[4:8], here)
        keep[here, :] = by_plane(place, keep_table, sums)
        give[here, :] = by_plane(place, table, sums).astype(bf16)

    loop(block // ADD_ROWS, step)
    if len(refs) > 10:
        total = sum(unpack_rows(ref[0, 0, block:, :]) for ref in refs[:4])
        refs[10][...] = total
        give[block:, :] = pack_rows(total)


def two_sums(place, table, first, second, name, after):
    rows, more = second[0][0].shape[2], first[0][0].shape[2] - second[0][0].shape[2]
    args = first + second
    return picked(
        functools.partial(two_sums_kernel, table, tuple(1 - k for k in table)),
        [shape((rows, D), f32), shape((rows + more, D), bf16)] + ([shape((more, D // 2), f32)] if more else []),
        [scalars] + [piece_spec(p, j) for p, j in args],
        [place] + [a for a, _ in args],
        name,
        after,
    )


def far_sums(place, rest, after=()):
    return two_sums(place, (1, 1, 0, 0), [(p, 0) for p in rest], [(p, 1) for p in rest], "far_sums", after)


def near_sums(place, zero, rest, after=()):
    return two_sums(place, (1, 0, 1, 0), [(p, 0) for p in zero], [(p, 0) for p in rest], "near_sums", after)


def last_sums_kernel(place, kept_near, kept_far, kept_rows, near, far, base, give, sums, packed):
    block = base.shape[0]

    def step(i):
        here = rows_of(i, ADD_ROWS)
        both = (kept_near[here, :] + near[here, :].astype(f32), kept_far[here, :] + far[here, :].astype(f32))
        give[here, :] = by_plane(place, (1, 0, 0, 1), both).astype(bf16)
        base[here, :] = by_plane(place, (0, 1, 1, 0), both)

    loop(block // ADD_ROWS, step)
    total = kept_rows[...] + unpack_rows(near[block:, :])
    sums[...] = total
    packed[...] = pack_rows(total)


def last_sums(place, *args):
    rows, more = args[0].shape[0], args[2].shape
    return picked(
        last_sums_kernel,
        [shape((rows, D), f32), shape((rows, D), bf16), shape(more, f32), shape((more[0], D), bf16)],
        [scalars] + [pl.BlockSpec(a.shape, lambda i: (0, 0)) for a in args],
        [place, *args],
        "last_sums",
    )


def twice(values):
    high = values.astype(bf16)
    return high, (values - high.astype(f32)).astype(bf16)


def owner_kernel(
    base, last, left, right, left_root, right_root, master, slow,
    grad_to, left_to, right_to, master_to, slow_to, low_to,
    grad_v, last_v, left_v, right_v, left_root_v, right_root_v, master_v, slow_v, low_v, sems,
):
    pairs = (
        (base, grad_v), (last, last_v), (left_root, left_root_v), (right_root, right_root_v),
        (left, left_v), (right, right_v), (master, master_v), (slow, slow_v),
    )
    loads = [begin(a, b, sems.at[i]) for i, (a, b) in enumerate(pairs)]
    finish(loads[:2])
    grad_v[...] = grad_v[...] + last_v[...].astype(f32)
    sent = [begin(grad_v, grad_to, sems.at[8])]
    high, low = twice(grad_v[...])
    wide = jnp.concatenate([high, high, low], axis=1)
    finish(loads[2:4])
    root_high, root_low = twice(left_root_v[...])
    turned = contract(wide, jnp.concatenate([root_high, root_low, root_high], axis=0), 1, 0)
    high_t, low_t = twice(turned)
    root_high, root_low = twice(right_root_v[...])
    steered = (
        contract(root_high, high_t, 1, 0) + contract(root_high, low_t, 1, 0) + contract(root_low, high_t, 1, 0)
    )
    finish(loads[6:])
    made = master_v[...] - learning_rate * steered
    master_v[...] = made
    slow_v[...] = slow_decay * slow_v[...] + (1.0 - slow_decay) * made
    low_v[...] = made.astype(bf16)
    sent += [
        begin(master_v, master_to, sems.at[9]), begin(slow_v, slow_to, sems.at[10]), begin(low_v, low_to, sems.at[11])
    ]
    finish(loads[4:6])
    tall_a = jnp.concatenate([high, high, low], axis=0)
    tall_b = jnp.concatenate([high, low, high], axis=0)
    left_v[...] = stat_decay * left_v[...] + (1.0 - stat_decay) * contract(tall_a, tall_b, 0, 0)
    sent.append(begin(left_v, left_to, sems.at[12]))
    other = jnp.concatenate([high, low, high], axis=1)
    right_v[...] = stat_decay * right_v[...] + (1.0 - stat_decay) * contract(wide, other, 1, 1)
    finish(sent, begin(right_v, right_to, sems.at[13]))


def owner_step(base, last, left, right, left_root, right_root, master, slow):
    rows = base.shape[0]
    flat, stats, small_stats = (rows, D), (D, D), (rows, rows)
    return call(
        owner_kernel,
        [shape(flat, f32), shape(stats, f32), shape(small_stats, f32), shape(flat, f32), shape(flat, f32), shape(flat, bf16)],
        [anywhere] * 6,
        [
            pltpu.VMEM(flat, f32), pltpu.VMEM(flat, bf16), pltpu.VMEM(stats, f32), pltpu.VMEM(small_stats, f32),
            pltpu.VMEM(stats, f32), pltpu.VMEM(small_stats, f32), pltpu.VMEM(flat, f32), pltpu.VMEM(flat, f32),
            pltpu.VMEM(flat, bf16), pltpu.SemaphoreType.DMA((14,)),
        ],
        6 * D * rows * (2 * D + 2 * rows), 15 << 20,
        base, last, left, right, left_root, right_root, master, slow,
        specs=[anywhere] * 8, name="owner_step",
    )


def per_device(
    ring,
    tokens,
    cotangent,
    lengths,
    key_mask,
    type_ids,
    weights,
    vectors,
    master,
    slow_weights,
    left_stats,
    right_stats,
    left_root,
    right_root,
    vector_master,
    vector_moment,
    slow_vectors,
):
    ring = ring()
    place = ring.place
    slot_a, slot_b, table = ring.gather_early(weights, vectors)
    early = [*slot_a, *slot_b]
    types, keys = type_ids[None, :], key_mask[None, :]

    turned, context, spreads = attend(place, lengths, early, tokens, types, keys, table, after=ring.gather_late())
    pieces = early + ring.gather_last(context)
    layer_out, grad_first, grad_context, middle_sums, *parts = middle(
        place, pieces, tokens, types, context, cotangent, table
    )
    both, three = ring.reduction(parts[:4]), ring.reduction(parts[4:])
    three.across()
    both.across(after=three.give, cost=FAR_COST)
    mixed = attend_back(place, lengths, turned, grad_context, spreads, keys, after=both.give)
    three.side(after=[mixed])
    parts = mixed_grad(place, early, mixed, tokens, types, table, middle_sums, after=three.give)
    zero = ring.reduction(parts, after=three.last())
    zero.across()
    both.side(after=zero.give)
    input_grad, flag = input_back(place, early, mixed, grad_first, after=both.give)
    ring.reduce_far(both, after=[flag])
    zero.side(after=[flag])
    ring.reduce_near(zero, three)
    base, last, owned_vector = ring.reduce_last()
    grad_t, left_new, right_new, master_t, slow_t, low_t = owner_step(
        base, last, left_stats, right_stats, left_root, right_root, master.T, slow_weights.T
    )
    owned_grad, master_new, slow_new, weights_new = grad_t.T, master_t.T, slow_t.T, low_t.T
    moment_new = stat_decay * vector_moment + (1.0 - stat_decay) * owned_vector * owned_vector
    vector_master_new = vector_master - vector_rate * owned_vector / (jnp.sqrt(moment_new) + 1e-08)
    slow_vectors_new = slow_decay * slow_vectors + (1.0 - slow_decay) * vector_master_new
    vectors_new = vector_master_new.astype(bf16)
    return (
        layer_out,
        input_grad,
        owned_grad,
        left_new,
        right_new,
        master_new,
        slow_new,
        weights_new,
        owned_vector,
        moment_new,
        vector_master_new,
        slow_vectors_new,
        vectors_new,
    )


def solution(mesh):
    in_specs = (
        P(("dp", "opt"), None),
        P(("dp", "opt"), None),
        P(("dp", "opt")),
        P(("dp", "opt")),
        P(("dp", "opt")),
        P(None, "dp"),
        P("dp"),
        P(None, ("dp", "opt")),
        P(None, ("dp", "opt")),
        P(("dp", "opt"), None),
        P(("dp", "opt"), None),
        P(("dp", "opt"), None),
        P(("dp", "opt"), None),
        P(("dp", "opt")),
        P(("dp", "opt")),
        P(("dp", "opt")),
    )
    out_specs = (
        P(("dp", "opt"), None),
        P(("dp", "opt"), None),
        P(None, ("dp", "opt")),
        P(("dp", "opt"), None),
        P(("dp", "opt"), None),
        P(None, ("dp", "opt")),
        P(None, ("dp", "opt")),
        P(None, ("dp", "opt")),
        P(("dp", "opt")),
        P(("dp", "opt")),
        P(("dp", "opt")),
        P(("dp", "opt")),
        P(("dp", "opt")),
    )
    ring = Ring if dict(mesh.shape) == {"dp": 16, "opt": 2} else Plain
    return jax.shard_map(
        functools.partial(per_device, ring),
        mesh=mesh,
        in_specs=in_specs,
        out_specs=out_specs,
        check_vma=False,
    )
```

```python
import functools
import math

import jax
import jax.numpy as jnp
import numpy as np
from jax import lax
from jax.experimental import pallas as pl
from jax.experimental.pallas import tpu as pltpu
from jax.sharding import PartitionSpec as P

D = 768
H = 12
HD = 64
FF = 3072
WCOLS = 4 * D + 2 * FF
NVEC = 10 * D + FF

highest = lax.Precision.HIGHEST
norm_eps = 1e-12
learning_rate = 0.03
vector_rate = 0.2
stat_decay = 0.5
slow_decay = 0.9
f32 = jnp.float32
bf16 = jnp.bfloat16
AXES = ("dp", "opt")


def contract(left_side, right_side, left_dim, right_dim):
    return lax.dot_general(
        left_side, right_side, (((left_dim,), (right_dim,)), ((), ())), preferred_element_type=f32
    )


def block_index(z, y, c, x):
    return z * 8 + y * 4 + c * 2 + x


def permutation(move):
    pairs = []
    for b in range(32):
        z, y, c, x = b // 8, (b // 4) % 2, (b // 2) % 2, b % 2
        pairs.append((b, block_index(*move(z, y, c, x))))
    return pairs


Z_CYCLE = permutation(lambda z, y, c, x: ((2, 0, 3, 1)[z], y, c, x))
Z_CYCLE_BACK = permutation(lambda z, y, c, x: ((1, 3, 0, 2)[z], y, c, x))
Z_NEAR = permutation(lambda z, y, c, x: (z ^ 1, y, c, x))
Z_FAR = permutation(lambda z, y, c, x: (z ^ 2, y, c, x))
Z_MIDDLE = permutation(lambda z, y, c, x: ((0, 2, 1, 3)[z], y, c, x))
PLANE_A = permutation(lambda z, y, c, x: (z, 1 - y, c, x) if c == 0 else (z, y, c, 1 - x))
PLANE_B = permutation(lambda z, y, c, x: (z, y, c, 1 - x) if c == 0 else (z, 1 - y, c, x))
CORES = permutation(lambda z, y, c, x: (z, y, 1 - c, x))


def send(values, pairs):
    return lax.ppermute(values, AXES, pairs)


QUARTER_SLOT = np.array([[0, 1, 3, 2], [1, 0, 3, 2], [1, 3, 0, 2], [1, 3, 2, 0]])


FAR_COST = 40 * 10**9


class Ring:
    def __init__(self):
        dp = lax.axis_index("dp")
        self.z, self.y, self.c = dp // 4, (dp // 2) % 2, dp % 2
        self.x = lax.axis_index("opt")
        slots = [self.number([int(v) for v in QUARTER_SLOT[:, q]]) for q in range(4)]
        self.place = jnp.stack([self.y, self.c, self.x, self.z] + slots).astype(jnp.int32)

    def number(self, values):
        out = values[3]
        for z in (2, 1, 0):
            out = jnp.where(self.z == z, values[z], out)
        return out

    def gather_early(self, weights, vectors):
        place, rows = self.place, weights.shape[1] // 2
        own = prepare_own(place, weights.T, vectors[None, :])
        one = send(own, Z_CYCLE)
        side = send(own, PLANE_A)
        pass_on, slab, pair_a = after_one(place, own, one, side)
        two = send(pass_on, Z_NEAR)
        across_a = send(pair_a, PLANE_B)
        far = send(slab, Z_FAR)
        middle = send(own, Z_MIDDLE)
        swap_a = send(pair_a, CORES)
        block_b, slot_c = after_two(place, pass_on, one, two, far, after=[across_a, swap_a])
        side_b = send(block_b, PLANE_A)
        side_c = send(slot_c, PLANE_A)
        three = send(middle, Z_NEAR)
        swap_aa = send(across_a, CORES)
        pair_b, slot_d = after_three(place, block_b, side_b, middle, three, after=[side_c, swap_aa])
        across_b = send(pair_b, PLANE_B)
        swap_b = send(pair_b, CORES)
        side_d = send(slot_d, PLANE_A)
        self.late = after_four(slot_c, side_c, slot_d, side_d, after=[swap_b])
        swap_bb = send(across_b, CORES)
        slot_b = [pair_b, across_b, swap_b, swap_bb]
        table = read_vectors(place, slot_b, vectors.shape[0] // 2)
        return [pair_a, across_a, swap_a, swap_aa], slot_b, table.reshape(-1, D)

    def gather_late(self):
        self.across = send(self.late, PLANE_B)
        self.swapped = send(self.late, CORES)
        return [self.late]

    def gather_last(self, context):
        across = hold(self.across, context)
        return [self.late, across, self.swapped, send(across, CORES)]

    def reduction(self, pieces, after=()):
        return Reduction(pieces, after)

    def reduce_far(self, both, after=()):
        self.kept_far, give = far_sums(self.place, both.parts(), after)
        self.far = hold(send(give, Z_FAR), cost=FAR_COST)
        return [give]

    def reduce_near(self, zero, three, after=()):
        self.kept_near, give, self.kept_rows = near_sums(self.place, zero.parts(), three.parts(), after)
        self.near = send(give, Z_NEAR)

    def reduce_last(self):
        base, give, rows, packed = last_sums(
            self.place, self.kept_near, self.kept_far, self.kept_rows, self.near, self.far
        )
        last = send(give, Z_CYCLE_BACK)
        arrived = send(packed, Z_FAR).astype(f32)
        half = rows.shape[1]
        rows = rows + (arrived[:, :half] + arrived[:, half:])
        vector = lax.dynamic_index_in_dim(rows, self.z, 0, False)
        return base, last, vector[: NVEC // 32]


class Reduction:
    def __init__(self, pieces, after=()):
        self.keep_lo, self.keep_hi, give_lo, give_hi = pieces
        if after:
            give_hi = hold(give_hi, *after)
        self.got_hi = send(give_hi, CORES)
        self.got_lo = send(give_lo, CORES)
        self.more = []

    def across(self, after=(), cost=0):
        self.give = [add_pieces([self.keep_hi, self.got_hi], 0, 2, after)]
        got = send(*self.give, PLANE_B)
        self.more.append(hold(got, cost=cost) if cost else got)

    def side(self, after=()):
        self.give = [add_pieces(self.parts(), 1, 1, after)]
        self.more.append(send(*self.give, PLANE_A))

    def parts(self):
        return [self.keep_lo, self.got_lo, *self.more]

    def first(self):
        return [self.got_hi]

    def last(self):
        return self.more[-1:]


class Plain:
    def __init__(self):
        self.place = jnp.asarray(np.array([0, 0, 0, 0, 0, 1, 2, 3]), jnp.int32)

    def gather_early(self, weights, vectors):
        turned = lax.all_gather(weights, "dp", axis=1, tiled=True).T
        blocks = turned.reshape(4, 8, -1, D)
        self.mine, self.theirs = (blocks[:, np.array(k)] for k in ([0, 4, 1, 5], [2, 3, 6, 7]))
        entries = vectors.shape[0]
        tiles = -(-entries // 2048)
        padded = jnp.pad(vectors, (0, tiles * 2048 - entries)).reshape(tiles * 16, 128)
        gathered = lax.all_gather(padded, "dp", axis=0, tiled=True)
        gathered = gathered.reshape(-1, tiles * 2048)[:, :entries].reshape(-1, D).astype(f32)
        slots = [[jnp.pad(v, ((0, 0), (0, 16), (0, 0))) for v in self.halves(q)] for q in (0, 1)]
        return *slots, gathered

    def halves(self, q):
        return [self.mine[q, :2], self.mine[q, 2:], self.theirs[q, :2], self.theirs[q, 2:]]

    def gather_late(self):
        return []

    def gather_last(self, context):
        return [jnp.stack(both, axis=1) for both in zip(self.halves(2), self.halves(3))]

    def reduction(self, pieces, after=()):
        return PlainReduction(pieces)

    def reduce_far(self, both, after=()):
        self.both = both
        return []

    def reduce_near(self, zero, three, after=()):
        self.zero, self.three = zero, three

    def reduce_last(self):
        zero = self.zero.whole()
        block = Q // 8
        packed = zero[0, :, block:, :].astype(f32)
        rows = packed[..., : D // 2] + packed[..., D // 2 :]
        vectors = jnp.swapaxes(rows[:, :4, : NVEC // 32], 0, 1).reshape(-1)
        vectors = lax.psum_scatter(vectors, AXES, scatter_dimension=0, tiled=True)
        sums = jnp.concatenate([zero[:, :, :block].reshape(-1, D), *(v.whole().reshape(-1, D) for v in (self.both, self.three))])
        owned = lax.psum_scatter(sums, AXES, scatter_dimension=0, tiled=True)
        return owned.astype(f32), jnp.zeros_like(owned), vectors


class PlainReduction:
    def __init__(self, pieces):
        self.pieces = jnp.concatenate(pieces)
        self.give = []

    def across(self, after=(), cost=0):
        pass

    def side(self, after=()):
        pass

    def first(self):
        return []

    def last(self):
        return []

    def whole(self):
        order = np.argsort(np.array([0, 4, 1, 5, 2, 3, 6, 7]))
        return jnp.swapaxes(self.pieces[order], 0, 1)


VMEM_LIMIT = 60 * 1024 * 1024
whole = pl.BlockSpec(memory_space=pltpu.VMEM)
scalars = pl.BlockSpec(memory_space=pltpu.SMEM)
anywhere = pl.BlockSpec(memory_space=pl.ANY)
shape = jax.ShapeDtypeStruct
CHUNK = 256
CHUNKS = FF // CHUNK
Q = 3 * D
SPAN = 256
TALL = 512
flag_shape = jax.ShapeDtypeStruct((8, 128), jnp.float32)
PART = 256


def call(kernel, outs, out_specs, scratch, flops, moved, *args, specs, name, after=(), limit=VMEM_LIMIT):
    count, skip = len(specs), len(after)

    def body(*refs):
        kernel(*refs[:count], *refs[count + skip :])

    return pl.pallas_call(
        body,
        out_shape=outs,
        in_specs=[*specs, *[anywhere] * skip],
        out_specs=out_specs,
        scratch_shapes=scratch,
        compiler_params=pltpu.CompilerParams(vmem_limit_bytes=limit),
        cost_estimate=pl.CostEstimate(flops=flops, bytes_accessed=moved, transcendentals=0),
        name=name,
    )(*args, *after)


def block_place(place, who, k):
    y, c, x = place[0], place[1], place[2]
    core = c if who == 0 else 1 - c
    first, second = k & 1, k >> 1
    to_y = jnp.where(core == 0, y ^ first, y ^ second)
    to_x = jnp.where(core == 0, x ^ second, x ^ first)
    return to_y * 4 + core * 2 + to_x


def block_rows(place, who, k, rows):
    return pl.ds(pl.multiple_of(block_place(place, who, k) * rows, math.gcd(rows, 16)), rows)


def begin(source, target, sem):
    copy = pltpu.make_async_copy(source, target, sem)
    copy.start()
    return copy


def slot_pieces(slots):
    return [
        [(refs[k // 2], (k % 2,) + ((slot - 2,) if slot > 1 else ())) for k in range(8)]
        for slot, refs in enumerate(slots)
    ]


def ingest(place, quarter, slots, into, sems):
    rows = into.shape[0] // 8
    targets = [into.at[block_rows(place, k // 4, k % 4, rows)] for k in range(8)]
    all_pieces = slot_pieces(slots)
    for slot, pieces in enumerate(all_pieces):

        @pl.when(place[4 + quarter] == slot)
        def _():
            for k, (ref, index) in enumerate(pieces):
                pltpu.make_async_copy(ref.at[(*index, pl.ds(0, rows))], targets[k], sems.at[k]).start()

    return [
        pltpu.make_async_copy(ref.at[(*index, pl.ds(0, rows))], targets[k], sems.at[k])
        for k, (ref, index) in enumerate(all_pieces[0])
    ]


def piece_of(place, at):
    y, c, x = place[0], place[1], place[2]
    core = (at >> 1) & 1
    flip_y, flip_x = (at >> 2) ^ y, (at & 1) ^ x
    first = jnp.where(core == 0, flip_y, flip_x)
    second = jnp.where(core == 0, flip_x, flip_y)
    return jnp.where(core == c, 0, 2) + second, first


def hand_block(place, source, at, targets, part, sem):
    rows = source.shape[0] // 8
    which, first = piece_of(place, at)
    for k, target in enumerate(targets):

        @pl.when(which == k)
        def _():
            pltpu.make_async_copy(source.at[rows_of(at, rows)], target.at[first, part, pl.ds(0, rows)], sem).start()


def hand_rows(place, source, at, targets, sem):
    count = source.shape[1]
    which, first = piece_of(place, at)
    for k, target in enumerate(targets):

        @pl.when(which == k)
        def _():
            there = target.at[first, 0, pl.ds(target.shape[2] - count, count)]
            pltpu.make_async_copy(source.at[at], there, sem).start()


def pack_rows(values):
    return jnp.concatenate(twice(values), axis=1)


def unpack_rows(packed):
    half = packed.shape[1] // 2
    wide = packed.astype(f32)
    return wide[:, :half] + wide[:, half:]


def hand_wait(source, targets, part, sems):
    rows = source.shape[0] // 8
    for k in range(8):
        pltpu.make_async_copy(source.at[pl.ds(0, rows)], targets[0].at[0, part, pl.ds(0, rows)], sems.at[k]).wait()


def finish(*copies):
    for copy in copies:
        if isinstance(copy, (list, tuple)):
            finish(*copy)
        else:
            copy.wait()


def rows_of(i, step):
    return pl.ds(pl.multiple_of(i * step, math.gcd(step, 256)), step)


def loop(count, body):
    def step(i, carry):
        body(i)
        return carry

    lax.fori_loop(0, count, step, 0)


def column(row, width):
    return jnp.broadcast_to(row, (width, row.shape[1])).T


def is_region(types):
    return column((types == 1).astype(f32), 128)[:, 0:1] > 0.5


def allowed_keys(lengths, keys, s):
    slot = lax.broadcasted_iota(jnp.int32, (1, SPAN), 1)
    allowed = (slot < lengths[s]) & ((keys[:, rows_of(s, SPAN)] == 1) | (slot == 0))
    return jnp.where(allowed, 3e38, -1e30)


def embed(tokens, types, table):
    return tokens.astype(f32) + jnp.where(is_region(types), table[1:2, :], table[0:1, :])


def attend_kernel(
    place, lengths, a0, a1, a2, a3, b0, b1, b2, b3, tokens_in, types, keys, table,
    turned_out, context_out, spreads,
    weights, low, turned, context_turned, context, mask, tokens, sems, more,
):
    arrived = begin(tokens_in, tokens, sems.at[9])
    copies = ingest(place, 0, ((a0, a1, a2, a3), (b0, b1, b2, b3)), weights, sems)
    rows = tokens.shape[0]

    def prepare(i):
        here = rows_of(i, PART)
        low[here, :] = embed(tokens[here, :], types[:, here], table[...]).astype(bf16)
        mask[here, :] = column(allowed_keys(lengths, keys, i), SPAN)

    finish(arrived)
    loop(rows // PART, prepare)
    finish(copies)
    step = 384

    def project(i):
        here = rows_of(i, step)
        half = rows_of(i % 2, step)
        bias = jnp.where(i // 2 == 0, table[4:5, half], jnp.where(i // 2 == 2, table[5:6, half], 0.0))
        made = contract(weights[here, :], low[...], 1, 1) + column(bias, 128)[:, 0:1]
        made = made * jnp.where(i < D // step, HD ** (-0.5), 1.0)
        turned[here, :] = made.astype(bf16)

    loop(Q // step, project)
    sent = begin(turned, turned_out, sems.at[8])


    def sequence(s):
        cols = rows_of(s, SPAN)
        scores = [
            contract(turned[D + h * HD : D + (h + 1) * HD, cols], turned[h * HD : (h + 1) * HD, cols], 0, 0)
            for h in range(H)
        ]
        probs = []
        for h, score in enumerate(scores):
            score = jnp.minimum(score, mask[cols, :])
            peak = jnp.max(score, axis=0, keepdims=True)
            powers = jnp.exp(score - peak)
            total = jnp.sum(powers, axis=0, keepdims=True)
            probs.append((powers * (1.0 / total)).astype(bf16))
            spreads[h : h + 1, cols] = peak + jnp.log(total)
        for h, prob in enumerate(probs):
            value = turned[2 * D + h * HD : 2 * D + (h + 1) * HD, cols]
            context_turned[h * HD : (h + 1) * HD, :] = contract(value, prob, 1, 0).astype(bf16)
        context[cols, :] = context_turned[...].T
        pltpu.make_async_copy(context.at[cols], context_out.at[cols], more.at[s]).start()

    loop(rows // SPAN, sequence)
    for s in range(rows // SPAN):
        cols = pl.ds(s * SPAN, SPAN)
        pltpu.make_async_copy(context.at[cols], context_out.at[cols], more.at[s]).wait()
    finish(sent)


def attend(place, lengths, pieces, tokens, types, keys, table, after=()):
    rows = tokens.shape[0]
    return call(
        attend_kernel,
        [shape((Q, rows), bf16), shape((rows, D), bf16), shape((H, rows), f32)],
        [anywhere, anywhere, whole],
        [
            pltpu.VMEM((Q, D), bf16),
            pltpu.VMEM((rows, D), bf16),
            pltpu.VMEM((Q, rows), bf16),
            pltpu.VMEM((D, SPAN), bf16),
            pltpu.VMEM((rows, D), bf16),
            pltpu.VMEM((rows, SPAN), f32),
            pltpu.VMEM((rows, D), bf16),
            pltpu.SemaphoreType.DMA((10,)),
            pltpu.SemaphoreType.DMA((rows // SPAN,)),
        ],
        2 * rows * Q * D + 4 * rows * 256 * D,
        20 << 20,
        place, lengths, *pieces, tokens, types, keys, table,
        specs=[scalars] * 2 + [anywhere] * 9 + [whole] * 3,
        name="attend",
        after=after,
    )


def normalise(inputs):
    centre = jnp.mean(inputs, axis=-1, keepdims=True)
    offset = inputs - centre
    spread = lax.rsqrt(jnp.mean(offset * offset, axis=-1, keepdims=True) + norm_eps)
    return offset * spread, spread


def normalise_back(scaled, unit, spread):
    return spread * (
        scaled
        - jnp.mean(scaled, axis=-1, keepdims=True)
        - unit * jnp.mean(scaled * unit, axis=-1, keepdims=True)
    )


def gelu_both(v):
    cumulative = 0.5 * (1.0 + lax.erf(v * math.sqrt(0.5)))
    density = jnp.exp(-0.5 * v * v) * (1.0 / math.sqrt(2.0 * math.pi))
    return v * cumulative, cumulative + v * density


def weight_chunk(weights, offset, i):
    return weights[pl.ds(pl.multiple_of(offset + i * CHUNK, CHUNK), CHUNK), :]


def row_sums(count, body, sums, rows):
    zero = jnp.zeros((8, D), f32)

    def step(i, carry):
        made = body(i)
        return tuple(
            have + jnp.sum(more.reshape(-1, 8, D), axis=0) for have, more in zip(carry, made)
        )

    made = lax.fori_loop(0, count, step, (zero,) * len(rows))
    for have, row in zip(made, rows):
        sums[row : row + 1, 0:D] = jnp.sum(have, axis=0, keepdims=True)


STEP = 768


def middle_kernel(
    place, a0, a1, a2, a3, b0, b1, b2, b3, c0, c1, c2, c3, tokens_in, context_in, cotangent_in, types, table,
    layer_out_to, grad_first_to, grad_context_to, sums,
    keep_lo, keep_hi, give_lo, give_hi, keep_lo3, keep_hi3, give_lo3, give_hi3,
    weights, pre_a, pre_b, total, tokens, context, cotangent, layer_out, active, slope, unit_one, spread_one, normed_low,
    grad_context, down_made, sems, more,
):
    rows = tokens.shape[0]
    slots = ((a0, a1, a2, a3), (b0, b1, b2, b3), (c0, c1, c2, c3), (c0, c1, c2, c3))
    early = [begin(context_in, context, more.at[0]), begin(tokens_in, tokens, more.at[1])]
    batches = [ingest(place, 1, slots, weights.at[pl.ds(0, Q)], sems.at[0])]
    up, down = D, D + FF
    finish(early, batches[0])
    batches.append(ingest(place, 2, slots, weights.at[pl.ds(Q, Q)], sems.at[1]))
    batches.append(ingest(place, 3, slots, weights.at[pl.ds(2 * Q, Q)], sems.at[2]))
    late = begin(cotangent_in, cotangent, more.at[2])

    def branch(i):
        here = rows_of(i, TALL)
        total[here, :] = contract(context[here, :], weights[0:D, :], 1, 1)

    loop(rows // TALL, branch)

    def first(i):
        here = rows_of(i, PART)
        unit, spread = normalise(embed(tokens[here, :], types[:, here], table[...]) + (total[here, :] + table[6:7, :]))
        unit_one[here, :] = unit
        spread_one[here, :] = jnp.broadcast_to(spread, (PART, 128))
        normed_low[here, :] = (unit * table[2:3, :] + table[3:4, :]).astype(bf16)

    loop(rows // PART, first)
    sent = []
    targets = (keep_lo, keep_hi, give_lo, give_hi)
    targets3 = (keep_lo3, keep_hi3, give_lo3, give_hi3)
    finish(batches[1])

    def gelu(pre, i, here):
        bias = table[pl.ds(10 + i // (D // CHUNK), 1), rows_of(i % (D // CHUNK), CHUNK)]
        return gelu_both(pre[here, :] + bias)

    def keep_gelu(made, i, here):
        cols = rows_of(i, CHUNK)
        active[here, cols] = made[0].astype(bf16)
        slope[here, cols] = made[1]

    everything = slice(None)

    def forward(t):
        before = jnp.maximum(2 * t - 1, 0)
        both = gelu(pre_b, before, everything)
        pre_a[...] = contract(normed_low[...], weight_chunk(weights, up, 2 * t), 1, 1)
        keep_gelu(both, before, everything)
        both = gelu(pre_a, 2 * t, everything)
        pre_b[...] = contract(normed_low[...], weight_chunk(weights, up, 2 * t + 1), 1, 1)
        keep_gelu(both, 2 * t, everything)

    loop(CHUNKS // 2, forward)

    def forward_end(i):
        here = rows_of(i, PART)
        keep_gelu(gelu(pre_b, CHUNKS - 1, here), CHUNKS - 1, here)

    loop(rows // PART, forward_end)
    finish(batches[2])

    def add_down(i):
        here = rows_of(i, TALL)
        total[here, :] = contract(active[here, :], weights[down : down + FF, :], 1, 0)

    loop(rows // TALL, add_down)
    finish(late)

    def second(i):
        here = rows_of(i, PART)
        normed_one = unit_one[here, :] * table[2:3, :] + table[3:4, :]
        unit, spread = normalise(normed_one + (total[here, :] + table[9:10, :]))
        layer_out[here, :] = (unit * table[7:8, :] + table[8:9, :]).astype(bf16)
        upstream = cotangent[here, :].astype(f32)
        grad = normalise_back(upstream * table[7:8, :], unit, spread)
        total[here, :] = grad
        low = grad.astype(bf16)
        tokens[here, :] = low
        return upstream * unit, upstream, low.astype(f32)

    row_sums(rows // PART, second, sums, (7, 8, 9))
    sent.append(begin(layer_out, layer_out_to, more.at[5]))

    def weigh_down(i):
        here = rows_of(i, STEP)
        down_made[here, :] = contract(active[:, here], tokens[...], 0, 0).astype(bf16)

    loop(FF // STEP, weigh_down)
    third_quarter = down_made.at[pl.ds(D, Q)]
    loop(8, lambda p: hand_block(place, third_quarter, p, targets3, 0, sems.at[2, p]))

    def through(pre, i, here):
        return (pre[here, :] * slope[here, rows_of(i, CHUNK)]).astype(bf16)

    def backward(t):
        before = jnp.maximum(2 * t - 1, 0)
        low = through(pre_b, before, everything)
        pre_a[...] = contract(tokens[...], weight_chunk(weights, down, 2 * t), 1, 1)
        active[:, rows_of(before, CHUNK)] = low
        low = through(pre_a, 2 * t, everything)
        pre_b[...] = contract(tokens[...], weight_chunk(weights, down, 2 * t + 1), 1, 1)
        active[:, rows_of(2 * t, CHUNK)] = low

    loop(CHUNKS // 2, backward)

    def backward_end(i):
        here = rows_of(i, PART)
        active[here, rows_of(CHUNKS - 1, CHUNK)] = through(pre_b, CHUNKS - 1, here)

    loop(rows // PART, backward_end)

    def add_up(i):
        here = rows_of(i, TALL)
        total[here, :] += contract(active[here, :], weights[up : up + FF, :], 1, 0)

    loop(rows // TALL, add_up)

    def third(i):
        here = rows_of(i, PART)
        upstream = total[here, :]
        unit = unit_one[here, :]
        grad = normalise_back(upstream * table[2:3, :], unit, spread_one[here, 0:1])
        total[here, :] = grad
        low = grad.astype(bf16)
        cotangent[here, :] = low
        of_one = is_region(types[:, here])
        return upstream * unit, upstream, low.astype(f32), jnp.where(of_one, 0.0, grad), jnp.where(of_one, grad, 0.0)

    row_sums(rows // PART, third, sums, (2, 3, 6, 0, 1))
    sent.append(begin(total, grad_first_to, more.at[8]))

    def through_out(i):
        here = rows_of(i, TALL)
        grad_context[:, here] = contract(cotangent[here, :], weights[0:D, :], 1, 0).T.astype(bf16)

    loop(rows // TALL, through_out)
    sent.append(begin(grad_context, grad_context_to, more.at[10]))
    moved = begin(down_made.at[pl.ds(0, D)], weights.at[pl.ds(D + FF, D)], more.at[9])

    def weigh_up(i):
        here = rows_of(i, STEP)
        rows_there = pl.ds(pl.multiple_of(D + i * STEP, 256), STEP)
        weights[rows_there, :] = contract(active[:, here], normed_low[...], 0, 0).astype(bf16)
        added = jnp.sum(active[:, here].astype(f32), 0, keepdims=True)
        sums[pl.ds(10, 1), here] = added

    half = FF // STEP // 2
    loop(half, lambda i: weigh_up(half + i))
    finish(moved)
    hand_wait(third_quarter, targets3, 0, sems.at[2])
    quarters = weights.at[pl.ds(0, Q)], weights.at[pl.ds(Q, Q)]
    loop(8, lambda p: hand_block(place, quarters[1], p, targets, 1, sems.at[1, p]))

    def weigh_out(i):
        here = rows_of(i, 384)
        weights[here, :] = contract(cotangent[:, here], context[...], 0, 0).astype(bf16)

    def hand_one(p):
        hand_block(place, quarters[0], p, targets, 0, sems.at[0, p])

    def weigh_and_hand(i):
        weigh_up(i)
        loop(3, lambda p: hand_one(2 + 3 * i + p))

    loop(2, weigh_out)
    loop(2, hand_one)
    loop(half, weigh_and_hand)
    hand_wait(quarters[1], targets, 1, sems.at[1])
    hand_wait(quarters[0], targets, 0, sems.at[0])
    finish(sent)


def middle(place, pieces, tokens, types, context, cotangent, table, after=()):
    rows = tokens.shape[0]
    tall = pltpu.VMEM((rows, D), bf16)
    return call(
        middle_kernel,
        [shape((rows, D), bf16), shape((rows, D), f32), shape((D, rows), bf16), shape((11, FF), f32)]
        + [shape((2, 2, Q // 8, D), bf16)] * 4
        + [shape((2, 1, Q // 8, D), bf16)] * 4,
        [anywhere] * 3 + [whole] + [anywhere] * 8,
        [
            pltpu.VMEM((3 * Q, D), bf16),
            pltpu.VMEM((rows, CHUNK), f32),
            pltpu.VMEM((rows, CHUNK), f32),
            pltpu.VMEM((rows, D), f32),
            tall,
            tall,
            tall,
            tall,
            pltpu.VMEM((rows, FF), bf16),
            pltpu.VMEM((rows, FF), f32),
            pltpu.VMEM((rows, D), f32),
            pltpu.VMEM((rows, 128), f32),
            tall,
            pltpu.VMEM((D, rows), bf16),
            pltpu.VMEM((FF, D), bf16),
            pltpu.SemaphoreType.DMA((3, 8)),
            pltpu.SemaphoreType.DMA((11,)),
        ],
        6 * rows * 3 * Q * D,
        60 << 20,
        place, *pieces, tokens, context, cotangent, types, table,
        specs=[scalars] + [anywhere] * 15 + [whole] * 2,
        name="middle",
        after=after,
    )


def attend_back_kernel(
    place, lengths, turned, grad_context, spreads, keys,
    mixed_to,
    mixed, mask, sems,
):
    rows = turned.shape[1]

    def prepare(i):
        here = rows_of(i, PART)
        mask[here, :] = column(allowed_keys(lengths, keys, i), SPAN)

    loop(rows // PART, prepare)

    together = 6

    def units(i):
        places = []
        for j in range(together):
            u = i * together + j
            places.append((u % H, pl.multiple_of((u % H) * HD, HD), rows_of(u // H, SPAN)))
        query = [turned[pl.ds(at, HD), cols] for _, at, cols in places]
        key = [turned[pl.ds(D + at, HD), cols] for _, at, cols in places]
        grad = [grad_context[pl.ds(at, HD), cols] for _, at, cols in places]
        scores = [contract(k, q, 0, 0) for k, q in zip(key, query)]
        grad_probs = [
            contract(turned[pl.ds(2 * D + at, HD), cols], g, 0, 0) for (_, at, cols), g in zip(places, grad)
        ]
        made = []
        for (h, at, cols), score, grad_prob in zip(places, scores, grad_probs):
            probs = jnp.exp(jnp.minimum(score, mask[cols, :]) - spreads[pl.ds(h, 1), cols])
            inner = jnp.sum(probs * grad_prob, axis=0, keepdims=True)
            made.append(((probs * (grad_prob - inner)).astype(bf16), probs.astype(bf16)))
        for (h, at, cols), q, k, g, (grad_score, prob) in zip(places, query, key, grad, made):
            mixed[pl.ds(at, HD), cols] = (contract(k, grad_score, 1, 0) * HD ** (-0.5)).astype(bf16)
            mixed[pl.ds(D + at, HD), cols] = contract(q, grad_score, 1, 1).astype(bf16)
            mixed[pl.ds(2 * D + at, HD), cols] = contract(g, prob, 1, 1).astype(bf16)

    loop(H * (rows // SPAN) // together, units)
    finish(begin(mixed, mixed_to, sems.at[0]))


def attend_back(place, lengths, turned, grad_context, spreads, keys, after=()):
    rows = turned.shape[1]
    return call(
        attend_back_kernel,
        [shape((Q, rows), bf16)],
        [anywhere],
        [
            pltpu.VMEM((Q, rows), bf16),
            pltpu.VMEM((rows, SPAN), f32),
            pltpu.SemaphoreType.DMA((1,)),
        ],
        10 * rows * 256 * D,
        25 << 20,
        place, lengths, turned, grad_context, spreads, keys,
        specs=[scalars] * 2 + [whole] * 4,
        limit=36 * 1024 * 1024,
        name="attend_back",
        after=after,
    )[0]


def mixed_grad_kernel(
    place, a0, a1, a2, a3, b0, b1, b2, b3, mixed_in, tokens, types, table, middle_sums,
    keep_lo, keep_hi, give_lo, give_hi,
    low, mixed, made, weights, by_type, sums, wide, packed, sems, more, others,
):
    step = 384
    for i in range(Q // step):
        here = pl.ds(i * step, step)
        begin(mixed_in.at[here], mixed.at[here], more.at[i])
    copies = ingest(place, 0, ((a0, a1, a2, a3), (b0, b1, b2, b3)), weights, sems)
    rows = tokens.shape[0]
    targets = (keep_lo, keep_hi, give_lo, give_hi)

    def prepare(i):
        here = rows_of(i, PART)
        low[here, :] = embed(tokens[here, :], types[:, here], table[...]).astype(bf16)

    loop(rows // PART, prepare)
    type_row = lax.broadcasted_iota(jnp.int32, (8, rows), 0)
    one_hot = (type_row == types[...]).astype(f32).astype(bf16)

    def weigh(i):
        here = rows_of(i, step)
        pltpu.make_async_copy(mixed_in.at[here], mixed.at[here], more.at[i]).wait()
        made[here, :] = contract(mixed[here, :], low[...], 1, 0).astype(bf16)
        by_type[:, here] = contract(one_hot, mixed[here, :], 1, 1)

    loop(Q // step, weigh)
    finish(copies)
    loop(8, lambda p: hand_block(place, made, p, targets, 0, sems.at[p]))
    high, rest = twice(by_type[...])
    through = contract(high, weights[...], 1, 0) + contract(rest, weights[...], 1, 0)
    sums[0:10, :] = middle_sums[0:10, 0:D]
    sums[0:2, :] = middle_sums[0:2, 0:D] + through[0:2, :]
    for row, start in ((4, 0), (5, 2 * D)):
        sums[row : row + 1, :] = by_type[0:1, start : start + D] + by_type[1:2, start : start + D]
    for i in range(FF // D):
        sums[10 + i : 11 + i, :] = middle_sums[10:11, i * D : (i + 1) * D]
    wide[...] = jnp.zeros_like(wide)
    entries = NVEC // 32
    for block in range(8):
        for z in range(4):
            row, lane = divmod((z * 8 + block) * entries, D)
            taken = min(entries, D - lane)
            wide[block, z : z + 1, 0:taken] = sums[row : row + 1, lane : lane + taken]
            if taken < entries:
                wide[block, z : z + 1, taken:entries] = sums[row + 1 : row + 2, 0 : entries - taken]
        packed[block] = pack_rows(wide[block])

    loop(8, lambda p: hand_rows(place, packed, p, targets, others.at[p]))
    hand_wait(made, targets, 0, sems)
    for p in range(8):
        pltpu.make_async_copy(packed.at[p], keep_lo.at[0, 0, pl.ds(Q // 8, 16)], others.at[p]).wait()


def mixed_grad(place, pieces, mixed, tokens, types, table, middle_sums, after=()):
    rows = tokens.shape[0]
    return call(
        mixed_grad_kernel,
        [shape((2, 1, Q // 8 + 16, D), bf16)] * 4,
        [anywhere] * 4,
        [
            pltpu.VMEM((rows, D), bf16),
            pltpu.VMEM((Q, rows), bf16),
            pltpu.VMEM((Q, D), bf16),
            pltpu.VMEM((Q, D), bf16),
            pltpu.VMEM((8, Q), f32),
            pltpu.VMEM((16, D), f32),
            pltpu.VMEM((8, 16, D // 2), f32),
            pltpu.VMEM((8, 16, D), bf16),
            pltpu.SemaphoreType.DMA((8,)),
            pltpu.SemaphoreType.DMA((6,)),
            pltpu.SemaphoreType.DMA((8,)),
        ],
        2 * rows * Q * D,
        12 << 20,
        place, *pieces, mixed, tokens, types, table, middle_sums,
        specs=[scalars] + [anywhere] * 9 + [whole] * 4,
        name="mixed_grad",
        after=after,
    )


def input_kernel(place, a0, a1, a2, a3, b0, b1, b2, b3, mixed, grad_first, input_grad_to, flag, weights, made, sems):
    flag[...] = jnp.zeros_like(flag)
    finish(ingest(place, 0, ((a0, a1, a2, a3), (b0, b1, b2, b3)), weights, sems))
    rows = grad_first.shape[0]

    def through(i):
        here = rows_of(i, SPAN)
        made[here, :] = grad_first[here, :] + contract(mixed[:, here], weights[...], 0, 0)
        begin(made.at[here], input_grad_to.at[here], sems.at[i])

    loop(rows // SPAN, through)
    for i in range(rows // SPAN):
        here = pl.ds(i * SPAN, SPAN)
        pltpu.make_async_copy(made.at[here], input_grad_to.at[here], sems.at[i]).wait()


def input_back(place, pieces, mixed, grad_first, after=()):
    rows = grad_first.shape[0]
    return call(
        input_kernel,
        [shape((rows, D), f32), flag_shape],
        [anywhere, whole],
        [pltpu.VMEM((Q, D), bf16), pltpu.VMEM((rows, D), f32), pltpu.SemaphoreType.DMA((8,))],
        0,
        0,
        place, *pieces, mixed, grad_first,
        specs=[scalars] + [anywhere] * 8 + [whole] * 2,
        name="input_back",
        after=after,
    )


SMALL_LIMIT = 16 * 1024 * 1024


def small(kernel, outs, *args, name, after=(), scratch=(), specs=None, out_specs=None):
    specs = specs or [scalars if a.dtype == jnp.int32 else whole for a in args]
    many = isinstance(outs, (list, tuple))
    return call(
        kernel, outs, out_specs or ([whole] * len(outs) if many else whole), list(scratch), 0, 0, *args,
        specs=specs, name=name, after=after, limit=SMALL_LIMIT,
    )


def hold(values, *after, cost=0):
    skip = len(after)
    return pl.pallas_call(
        lambda *refs: None,
        out_shape=shape(values.shape, values.dtype),
        in_specs=[anywhere] * (1 + skip),
        out_specs=anywhere,
        input_output_aliases={0: 0},
        cost_estimate=pl.CostEstimate(flops=cost, bytes_accessed=0, transcendentals=0),
        name="hold",
    )(values, *after)


def prepare_kernel(place, turned, few, own, sem):
    rows = own.shape[0] - 16
    copy = begin(turned.at[pl.ds(pl.multiple_of(place[2] * rows, 16), rows)], own.at[pl.ds(0, rows)], sem)
    entries = few.shape[1] // 2
    row = few[...].astype(f32)
    row = jnp.where(place[2] == 0, row[:, :entries], row[:, entries:])
    here = lax.broadcasted_iota(jnp.int32, (16, entries), 0) == place[3]
    own[rows:, :] = jnp.zeros((16, D), bf16)
    own[rows:, 0:entries] = jnp.where(here, row, 0.0).astype(bf16)
    finish(copy)


def prepare_own(place, turned, few):
    return small(
        prepare_kernel, shape((turned.shape[0] // 2 + 16, D), bf16), place, turned, few,
        name="prepare_own", scratch=[pltpu.SemaphoreType.DMA], specs=[scalars, anywhere, whole],
    )


def by_plane(place, table, choices):
    out = choices[table[3]]
    for z in (2, 1, 0):
        out = jnp.where(place[3] == z, choices[table[z]], out)
    return out


def merge(old, new):
    old, new = old.astype(f32), new.astype(f32)
    return jnp.where(old == 0.0, new, old).astype(bf16)


def after_one_kernel(place, own, one, side, pass_on, slab, pair):
    rows = own.shape[0] - 16
    pass_on[:rows, :] = by_plane(place, (0, 1, 1, 0), (own[:rows, :], one[:rows, :]))
    merged = merge(own[rows:, :], one[rows:, :])
    pass_on[rows:, :] = merged
    slab[...] = merged
    pair[0] = own[...]
    pair[1] = side[...]


def after_one(place, own, one, side):
    outs = [shape(own.shape, bf16), shape((16, D), bf16), shape((2, *own.shape), bf16)]
    return small(after_one_kernel, outs, place, own, one, side, name="after_one")


def after_two_kernel(place, pass_on, one, two, far, block, slot):
    rows = one.shape[0] - 16
    block[:rows, :] = by_plane(place, (0, 1, 0, 1), (one[:rows, :], two[:rows, :]))
    block[rows:, :] = merge(merge(pass_on[rows:, :], two[rows:, :]), far[...])
    slot[...] = by_plane(place, (1, 0, 1, 0), (one[:rows, :], two[:rows, :]))


def after_two(place, pass_on, one, two, far, after):
    outs = [shape(one.shape, bf16), shape((one.shape[0] - 16, D), bf16)]
    return small(after_two_kernel, outs, place, pass_on, one, two, far, name="after_two", after=after)


def after_three_kernel(place, block, side, middle, three, pair, slot):
    rows = slot.shape[0]
    pair[0] = block[...]
    pair[1] = side[...]
    slot[...] = by_plane(place, (1, 0, 0, 1), (middle[:rows, :], three[:rows, :]))


def after_three(place, block, side, middle, three, after):
    outs = [shape((2, *block.shape), bf16), shape((block.shape[0] - 16, D), bf16)]
    return small(after_three_kernel, outs, place, block, side, middle, three, name="after_three", after=after)


def after_four_kernel(slot_c, side_c, slot_d, side_d, late):
    late[0, 0], late[0, 1] = slot_c[...], slot_d[...]
    late[1, 0], late[1, 1] = side_c[...], side_d[...]


def after_four(slot_c, side_c, slot_d, side_d, after):
    outs = shape((2, 2, *slot_c.shape), bf16)
    return small(after_four_kernel, outs, slot_c, side_c, slot_d, side_d, name="after_four", after=after)


def read_vectors_kernel(entries, place, a, b, c, d, out, got, sems):
    rows = a.shape[1] - 16
    refs = (a, b, c, d)
    finish([begin(refs[k // 2].at[k % 2, pl.ds(rows, 16)], got.at[k], sems.at[k]) for k in range(8)])
    for k in range(8):
        at = block_place(place, k // 4, k % 4)
        slab = got[k].astype(f32)
        for z in range(4):
            out[pl.ds(z * 8 + at, 1), :] = slab[z : z + 1, 0:entries]


def read_vectors(place, pieces, entries):
    return small(
        functools.partial(read_vectors_kernel, entries), shape((32, entries), f32), place, *pieces,
        name="read_vectors", specs=[scalars] + [anywhere] * 4,
        scratch=[pltpu.VMEM((8, 16, D), bf16), pltpu.SemaphoreType.DMA((8,))],
    )


def picked(kernel, outs, specs, args, name, after=()):
    count, skip = len(specs), len(after)

    def body(*refs):
        kernel(*refs[:count], *refs[count + skip :])

    return pl.pallas_call(
        body,
        grid=(1,),
        out_shape=outs,
        in_specs=[*specs, *[anywhere] * skip],
        out_specs=[pl.BlockSpec(o.shape, lambda i, n=len(o.shape): (0,) * n) for o in outs],
        compiler_params=pltpu.CompilerParams(vmem_limit_bytes=SMALL_LIMIT),
        cost_estimate=pl.CostEstimate(flops=0, bytes_accessed=0, transcendentals=0),
        name=name,
    )(*args, *after)


ADD_ROWS = 96


def add_pieces_kernel(*refs):
    count, n, rows, _ = refs[0].shape
    block = rows // ADD_ROWS * ADD_ROWS
    for a in range(count):
        for b in range(n):

            def step(i):
                here = rows_of(i, ADD_ROWS)
                total = refs[0][a, b, here, :].astype(f32)
                for ref in refs[1:-1]:
                    total = total + ref[a, b, here, :].astype(f32)
                refs[-1][a, b, here, :] = total.astype(bf16)

            loop(block // ADD_ROWS, step)
            if rows > block:
                refs[-1][a, b, block:, :] = pack_rows(sum(unpack_rows(ref[a, b, block:, :]) for ref in refs[:-1]))


def add_pieces(parts, first, count, after=()):
    _, n, rows, width = parts[0].shape
    block = (count, n, rows, width)
    return picked(
        add_pieces_kernel,
        [shape(block, bf16)],
        [pl.BlockSpec(block, lambda i: (first // count, 0, 0, 0))] * len(parts),
        parts,
        "add_pieces",
        after,
    )[0]


def piece_spec(part, j):
    return pl.BlockSpec((1, 1, *part.shape[2:]), lambda i: (0, j, 0, 0))


def sum_of(refs, here):
    total = refs[0][0, 0, here, :].astype(f32)
    for ref in refs[1:]:
        total = total + ref[0, 0, here, :].astype(f32)
    return total


def two_sums_kernel(table, keep_table, place, *refs):
    keep, give = refs[8], refs[9]
    block = keep.shape[0]

    def step(i):
        here = rows_of(i, ADD_ROWS)
        sums = sum_of(refs[:4], here), sum_of(refs[4:8], here)
        keep[here, :] = by_plane(place, keep_table, sums)
        give[here, :] = by_plane(place, table, sums).astype(bf16)

    loop(block // ADD_ROWS, step)
    if len(refs) > 10:
        total = sum(unpack_rows(ref[0, 0, block:, :]) for ref in refs[:4])
        refs[10][...] = total
        give[block:, :] = pack_rows(total)


def two_sums(place, table, first, second, name, after):
    rows, more = second[0][0].shape[2], first[0][0].shape[2] - second[0][0].shape[2]
    args = first + second
    return picked(
        functools.partial(two_sums_kernel, table, tuple(1 - k for k in table)),
        [shape((rows, D), f32), shape((rows + more, D), bf16)] + ([shape((more, D // 2), f32)] if more else []),
        [scalars] + [piece_spec(p, j) for p, j in args],
        [place] + [a for a, _ in args],
        name,
        after,
    )


def far_sums(place, rest, after=()):
    return two_sums(place, (1, 1, 0, 0), [(p, 0) for p in rest], [(p, 1) for p in rest], "far_sums", after)


def near_sums(place, zero, rest, after=()):
    return two_sums(place, (1, 0, 1, 0), [(p, 0) for p in zero], [(p, 0) for p in rest], "near_sums", after)


def last_sums_kernel(place, kept_near, kept_far, kept_rows, near, far, base, give, sums, packed):
    block = base.shape[0]

    def step(i):
        here = rows_of(i, ADD_ROWS)
        both = (kept_near[here, :] + near[here, :].astype(f32), kept_far[here, :] + far[here, :].astype(f32))
        give[here, :] = by_plane(place, (1, 0, 0, 1), both).astype(bf16)
        base[here, :] = by_plane(place, (0, 1, 1, 0), both)

    loop(block // ADD_ROWS, step)
    total = kept_rows[...] + unpack_rows(near[block:, :])
    sums[...] = total
    packed[...] = pack_rows(total)


def last_sums(place, *args):
    rows, more = args[0].shape[0], args[2].shape
    return picked(
        last_sums_kernel,
        [shape((rows, D), f32), shape((rows, D), bf16), shape(more, f32), shape((more[0], D), bf16)],
        [scalars] + [pl.BlockSpec(a.shape, lambda i: (0, 0)) for a in args],
        [place, *args],
        "last_sums",
    )


def twice(values):
    high = values.astype(bf16)
    return high, (values - high.astype(f32)).astype(bf16)


def owner_kernel(
    base, last, left, right, left_root, right_root, master, slow,
    grad_to, left_to, right_to, master_to, slow_to, low_to,
    grad_v, last_v, left_v, right_v, left_root_v, right_root_v, master_v, slow_v, low_v, sems,
):
    pairs = (
        (base, grad_v), (last, last_v), (left_root, left_root_v), (right_root, right_root_v),
        (left, left_v), (right, right_v), (master, master_v), (slow, slow_v),
    )
    loads = [begin(a, b, sems.at[i]) for i, (a, b) in enumerate(pairs)]
    finish(loads[:2])
    grad_v[...] = grad_v[...] + last_v[...].astype(f32)
    sent = [begin(grad_v, grad_to, sems.at[8])]
    high, low = twice(grad_v[...])
    wide = jnp.concatenate([high, high, low], axis=1)
    finish(loads[2:4])
    root_high, root_low = twice(left_root_v[...])
    turned = contract(wide, jnp.concatenate([root_high, root_low, root_high], axis=0), 1, 0)
    high_t, low_t = twice(turned)
    root_high, root_low = twice(right_root_v[...])
    steered = (
        contract(root_high, high_t, 1, 0) + contract(root_high, low_t, 1, 0) + contract(root_low, high_t, 1, 0)
    )
    finish(loads[6:])
    made = master_v[...] - learning_rate * steered
    master_v[...] = made
    slow_v[...] = slow_decay * slow_v[...] + (1.0 - slow_decay) * made
    low_v[...] = made.astype(bf16)
    sent += [
        begin(master_v, master_to, sems.at[9]), begin(slow_v, slow_to, sems.at[10]), begin(low_v, low_to, sems.at[11])
    ]
    finish(loads[4:6])
    left_v[...] = stat_decay * left_v[...] + (1.0 - stat_decay) * contract(high, high, 0, 0)
    sent.append(begin(left_v, left_to, sems.at[12]))
    right_v[...] = stat_decay * right_v[...] + (1.0 - stat_decay) * contract(high, high, 1, 1)
    finish(sent, begin(right_v, right_to, sems.at[13]))


def owner_step(base, last, left, right, left_root, right_root, master, slow):
    rows = base.shape[0]
    flat, stats, small_stats = (rows, D), (D, D), (rows, rows)
    return call(
        owner_kernel,
        [shape(flat, f32), shape(stats, f32), shape(small_stats, f32), shape(flat, f32), shape(flat, f32), shape(flat, bf16)],
        [anywhere] * 6,
        [
            pltpu.VMEM(flat, f32), pltpu.VMEM(flat, bf16), pltpu.VMEM(stats, f32), pltpu.VMEM(small_stats, f32),
            pltpu.VMEM(stats, f32), pltpu.VMEM(small_stats, f32), pltpu.VMEM(flat, f32), pltpu.VMEM(flat, f32),
            pltpu.VMEM(flat, bf16), pltpu.SemaphoreType.DMA((14,)),
        ],
        6 * D * rows * (2 * D + 2 * rows), 15 << 20,
        base, last, left, right, left_root, right_root, master, slow,
        specs=[anywhere] * 8, name="owner_step",
    )


def per_device(
    ring,
    tokens,
    cotangent,
    lengths,
    key_mask,
    type_ids,
    weights,
    vectors,
    master,
    slow_weights,
    left_stats,
    right_stats,
    left_root,
    right_root,
    vector_master,
    vector_moment,
    slow_vectors,
):
    ring = ring()
    place = ring.place
    slot_a, slot_b, table = ring.gather_early(weights, vectors)
    early = [*slot_a, *slot_b]
    types, keys = type_ids[None, :], key_mask[None, :]

    turned, context, spreads = attend(place, lengths, early, tokens, types, keys, table, after=ring.gather_late())
    pieces = early + ring.gather_last(context)
    layer_out, grad_first, grad_context, middle_sums, *parts = middle(
        place, pieces, tokens, types, context, cotangent, table
    )
    both, three = ring.reduction(parts[:4]), ring.reduction(parts[4:])
    three.across()
    both.across(after=three.give, cost=FAR_COST)
    mixed = attend_back(place, lengths, turned, grad_context, spreads, keys, after=both.give)
    three.side(after=[mixed])
    parts = mixed_grad(place, early, mixed, tokens, types, table, middle_sums, after=three.give)
    zero = ring.reduction(parts, after=three.last())
    zero.across()
    both.side(after=zero.give)
    input_grad, flag = input_back(place, early, mixed, grad_first, after=both.give)
    ring.reduce_far(both, after=[flag])
    zero.side(after=[flag])
    ring.reduce_near(zero, three)
    base, last, owned_vector = ring.reduce_last()
    grad_t, left_new, right_new, master_t, slow_t, low_t = owner_step(
        base, last, left_stats, right_stats, left_root, right_root, master.T, slow_weights.T
    )
    owned_grad, master_new, slow_new, weights_new = grad_t.T, master_t.T, slow_t.T, low_t.T
    moment_new = stat_decay * vector_moment + (1.0 - stat_decay) * owned_vector * owned_vector
    vector_master_new = vector_master - vector_rate * owned_vector / (jnp.sqrt(moment_new) + 1e-08)
    slow_vectors_new = slow_decay * slow_vectors + (1.0 - slow_decay) * vector_master_new
    vectors_new = vector_master_new.astype(bf16)
    return (
        layer_out,
        input_grad,
        owned_grad,
        left_new,
        right_new,
        master_new,
        slow_new,
        weights_new,
        owned_vector,
        moment_new,
        vector_master_new,
        slow_vectors_new,
        vectors_new,
    )


def solution(mesh):
    in_specs = (
        P(("dp", "opt"), None),
        P(("dp", "opt"), None),
        P(("dp", "opt")),
        P(("dp", "opt")),
        P(("dp", "opt")),
        P(None, "dp"),
        P("dp"),
        P(None, ("dp", "opt")),
        P(None, ("dp", "opt")),
        P(("dp", "opt"), None),
        P(("dp", "opt"), None),
        P(("dp", "opt"), None),
        P(("dp", "opt"), None),
        P(("dp", "opt")),
        P(("dp", "opt")),
        P(("dp", "opt")),
    )
    out_specs = (
        P(("dp", "opt"), None),
        P(("dp", "opt"), None),
        P(None, ("dp", "opt")),
        P(("dp", "opt"), None),
        P(("dp", "opt"), None),
        P(None, ("dp", "opt")),
        P(None, ("dp", "opt")),
        P(None, ("dp", "opt")),
        P(("dp", "opt")),
        P(("dp", "opt")),
        P(("dp", "opt")),
        P(("dp", "opt")),
        P(("dp", "opt")),
    )
    ring = Ring if dict(mesh.shape) == {"dp": 16, "opt": 2} else Plain
    return jax.shard_map(
        functools.partial(per_device, ring),
        mesh=mesh,
        in_specs=in_specs,
        out_specs=out_specs,
        check_vma=False,
    )
```
